32 devices in a mesh: sims: 8 (over y, x, core), rows: 4 (over z).
Axes of the slice: x: 2, y: 2, z: 4, core: 2. Of those that a mesh axis runs over, the one named last changes fastest.
Arguments:
- maps: float32 [8, 256, 2048], P('sims', 'rows'), may hold values from -6 to 6
- weight: float32 [256, 2048], P('rows'), may hold values from 0.1 to 1.5
- beam: float32 [65], replicated, may hold values from 0.05 to 1
- pair_one: int32 [8], replicated, may hold values from 0 to 7, each once
- pair_two: int32 [8], replicated, may hold values from 0 to 7, each once
- owner: int32 [8], replicated, may hold values from 0 to 7
Outputs:
- estimate: float32 [8, 256, 2048], P('sims', 'rows')
- mean_field: float32 [8, 256, 2048], P(None, 'rows', 'sims')
The draws below stay inside these ranges and needn't reach their ends.
Inputs may be any that keep to these rules, and one draw needn't show every extreme that they name: `pair_one`: each a permutation of the evolutions. `pair_two`: each a permutation of the evolutions.
All inputs are finite; a program needn't handle non-finite values.
Results may differ from the reference program's by a relative error of at most 0.00016.
Values sent between devices are 32-bit elements; how exact they have to be, the bound alone decides.
No kernel may reach another device: no remote copies, remote signals or barrier semaphores. Data moves between devices by JAX's collectives and lax.ppermute only.
A program may use at most 64 MiB of HBM per device.

```python
import math
import jax
import jax.numpy as jnp
from jax import lax

NCOL = 2048
TAPS = 65
ITERS = 3
OWNERS = 8
SIMS = 8
NROWS = 256


def plant(values, rng, least, high):
    spot = [jax.random.randint(jax.random.fold_in(rng, axis), (), 0, length) for axis, length in enumerate(values.shape)]
    widest = values.shape.index(max(values.shape))
    neighbour = spot[:widest] + [(spot[widest] + 1) % values.shape[widest]] + spot[widest + 1:]
    return values.at[tuple(spot)].set(least).at[tuple(neighbour)].set(high)


def level_of(key, shape, cuts, least, high):
    def one(axis_at, blocks):
        heights = jax.random.uniform(jax.random.fold_in(jax.random.fold_in(key, 6), axis_at), (blocks,), jnp.float32, least / len(cuts), high / len(cuts))
        return jnp.repeat(jnp.exp(heights), shape[axis_at] // blocks).reshape((-1,) + (1,) * (len(shape) - axis_at - 1))

    loudness = one(*cuts[0])
    for cut in cuts[1:]:
        loudness = loudness * one(*cut)
    return loudness


def scatter_about(rng, shape, deviation, most, pieces=(), kind=jnp.bfloat16):
    entries = deviation * jax.random.normal(rng, shape, jnp.float32)
    if pieces:
        entries = entries * level_of(rng, shape, pieces, -0.22, 0.18)
    return jnp.clip(entries, -most, most).astype(kind)


def setup_inputs(seed: int = 0) -> dict:
    keys = jax.random.split(jax.random.key(seed), 7)
    return {
        "maps": scatter_about(keys[0], (SIMS, NROWS, NCOL), 1.0, 6.0, ((0, 8), (1, 4)), jnp.float32),
        "weight": jnp.clip(jnp.exp(math.log(1.5) - 2.7080502 * jax.random.uniform(keys[1], (NROWS, NCOL), jnp.float32) ** level_of(keys[1], (NROWS, NCOL), ((0, 4),), -0.2, 0.2)), 0.1, 1.5),
        "beam": jnp.clip(jnp.exp(jax.random.uniform(keys[2], (TAPS,), jnp.float32, math.log(0.05), math.log(1.0))), 0.05, 1.0),
        "pair_one": jax.random.permutation(keys[3], SIMS).astype(jnp.int32),
        "pair_two": jax.random.permutation(keys[4], SIMS).astype(jnp.int32),
        "owner": plant(jax.random.randint(keys[5], (SIMS,), 0, OWNERS), jax.random.fold_in(keys[5], 1), 0, OWNERS - 1).astype(jnp.int32),
    }


ridge_term = 0.5
step_size = 0.6


def smear(field, coeffs, axis):
    length = field.shape[axis]
    extent = coeffs.shape[0]
    padded_len = length + extent - 1
    spectrum = jnp.fft.rfft(field, n=padded_len, axis=axis)
    response = jnp.fft.rfft(coeffs[::-1], n=padded_len)
    layout = [1, 1]
    layout[axis] = response.shape[0]
    complete = jnp.fft.irfft(spectrum * response.reshape(layout), n=padded_len, axis=axis)
    offset = (extent - 1) // 2
    return lax.slice_in_dim(complete, offset, offset + length, axis=axis)


def blur(field, coeffs):
    return smear(smear(field, coeffs, 1), coeffs, 0)


def diff_rows(field):
    padded = jnp.pad(field, ((1, 1), (0, 0)))
    return 0.5 * (padded[2:] - padded[:-2])


def diff_cols(field):
    padded = jnp.pad(field, ((0, 0), (1, 1)))
    return 0.5 * (padded[:, 2:] - padded[:, :-2])


def divergence(own_map, partner):
    return diff_rows(own_map * diff_rows(partner)) + diff_cols(own_map * diff_cols(partner))


def reference(maps, weight, beam, pair_one, pair_two, owner):
    kernel = beam / jnp.sum(beam)
    flipped = kernel[::-1]

    def filter_one(single):
        source = blur(weight * single, flipped)
        current = step_size * source
        for iteration in range(ITERS):
            applied = ridge_term * current + blur(weight * blur(current, kernel), flipped)
            current = current + step_size * (source - applied)
        return current

    filtered = lax.map(filter_one, maps)

    def estimate_one(index):
        own_map = filtered[index]
        first = filtered[pair_one[index]]
        second = filtered[pair_two[index]]
        return 2.0 * divergence(own_map, first) - divergence(own_map, second)

    estimate = lax.map(estimate_one, jnp.arange(SIMS, dtype=jnp.int32))
    sums = jax.ops.segment_sum(estimate, owner, num_segments=OWNERS)
    counts = jax.ops.segment_sum(jnp.ones((SIMS,), jnp.float32), owner, num_segments=OWNERS)
    mean_field = sums / jnp.maximum(counts, 1.0)[:, None, None]
    return estimate, mean_field
```

```python
import functools

import jax
import jax.numpy as jnp
from jax import lax
from jax.experimental import pallas as pl
from jax.experimental.pallas import tpu as pltpu
from jax.sharding import PartitionSpec as P

ITERS = 3
OWNERS = 8

ridge_term = 0.5
step_size = 0.6
exact = lax.Precision.HIGHEST
lane = 128
wide = 256
rim = 4
vmem_bytes = 48 * 1024 * 1024


def split(value):
    high = value.astype(jnp.bfloat16)
    low = (value - high.astype(jnp.float32)).astype(jnp.bfloat16)
    return high, low


def dot(a, b):
    return jnp.dot(a, b, preferred_element_type=jnp.float32)


def dot3(a_high, a_low, b_high, b_low):
    return dot(a_high, b_high) + (dot(a_low, b_high) + dot(a_high, b_low))


class Plan:
    def __init__(self, row_devices, sim_devices, row_local, columns, taps):
        self.row_devices, self.sim_devices = row_devices, sim_devices
        self.row_local, self.columns = row_local, columns
        self.rows = row_devices * row_local
        self.margin = (taps - 1) // 2
        self.share = columns // row_devices
        self.halo = -(-self.margin * (2 * ITERS + 1) // lane) * lane
        self.width = self.share + 2 * self.halo
        self.slab = row_local + 2 * rim
        self.sharers = min(sim_devices, row_local // 8)
        self.share_rows = row_local // self.sharers
        self.length = max(2 * wide, -(-self.rows // lane) * lane)
        inner = range(lane, self.width - lane, wide)
        blocks = [(0, lane)] + [(a, min(a + wide, self.width - lane)) for a in inner]
        self.blocks = blocks + [(self.width - lane, self.width)]
        centre = range(self.halo, self.halo + self.share, wide)
        self.out_blocks = [(a, min(a + wide, self.halo + self.share)) for a in centre]

    def window(self, block):
        return max(0, block[0] - lane), min(self.width, block[1] + lane)

    def stage_blocks(self, iteration):
        low = self.halo - self.margin * (2 * (ITERS - 1 - iteration) + 1)
        return [i for i, (a, b) in enumerate(self.blocks) if b > low and a < self.width - low]


def weighted_kernel(plan, place, maps, weight, *refs):
    count = plan.row_devices
    pieces, parts, padded = refs[:count], refs[count : 2 * count], refs[2 * count]
    zeros = jnp.zeros((plan.row_local, plan.halo), jnp.float32)
    inner = slice(plan.halo, plan.halo + plan.columns)
    padded[:, : plan.halo] = zeros
    padded[:, plan.halo + plan.columns :] = zeros
    padded[:, inner] = weight[...]
    row = pl.multiple_of(lax.rem(place[1], plan.sharers) * plan.share_rows, plan.share_rows)
    for step in range(count):
        column = pl.multiple_of((place[0] ^ step) * plan.share, lane)
        parts[step][...] = padded[pl.ds(row, plan.share_rows), pl.ds(column, plan.width)]
    padded[:, inner] = weight[...] * maps[...]
    for step in range(count):
        column = pl.multiple_of((place[0] ^ step) * plan.share, lane)
        pieces[step][...] = padded[:, pl.ds(column, plan.width)]


def band(plan, taps, rows, columns, offset):
    spread = jnp.broadcast_to(taps[...], (rows, plan.length))
    if offset % plan.length:
        spread = pltpu.roll(spread, offset % plan.length, 1)
    rolled = pltpu.roll(spread, 0, 1, stride=1, stride_axis=0)[:, :columns]
    row = lax.broadcasted_iota(jnp.int32, (rows, columns), 0)
    column = lax.broadcasted_iota(jnp.int32, (rows, columns), 1)
    return jnp.where(jnp.abs(column - row - offset) <= plan.margin, rolled, 0.0)


def table_kernel(plan, place, taps, reverse, *refs):
    tables = list(refs)

    def put(value):
        high, low = split(value)
        tables.pop(0)[...] = high
        tables.pop(0)[...] = low

    rows = plan.rows
    put(jnp.dot(band(plan, taps, rows, rows, 0), band(plan, reverse, rows, rows, 0), precision=exact))
    slabs = []
    for device in range(plan.row_devices):
        first = device * plan.row_local - rim
        part = band(plan, reverse, plan.slab, rows, first)
        row = lax.broadcasted_iota(jnp.int32, part.shape, 0) + first
        slabs.append(jnp.where((row >= 0) & (row < rows), part, 0.0))
    put(jnp.concatenate(slabs, axis=0))
    size = 2 * wide
    forward = band(plan, taps, size, size, 0)
    backward = band(plan, reverse, size, size, 0)
    for block in plan.blocks:
        low, high = plan.window(block)
        extent = high - low
        column = lax.broadcasted_iota(jnp.int32, (extent, extent), 1) + (place[0] * plan.share - plan.halo + low)
        inside = (column >= 0) & (column < plan.columns)
        left = jnp.where(inside, forward[:extent, :extent], 0.0)
        right = backward[:extent, block[0] - low : block[1] - low]
        put(step_size * jnp.dot(left, right, precision=exact))
    for block in plan.out_blocks[:1]:
        low, high = plan.window(block)
        put(step_size * forward[: high - low, block[0] - low : block[1] - low])


def filter_kernel(plan, sharers, place, *refs):
    refs = list(refs)

    def take(number):
        taken = refs[:number]
        del refs[:number]
        return taken

    pieces = take(plan.row_devices)
    parts = take(len(sharers))
    square, final = take(2), take(2)
    bands = [take(2) for _ in plan.blocks]
    last = take(2)
    outs = take(plan.row_devices)
    seen, weight, image, total, field, high, low, mid_high, mid_low = refs
    for step, piece in enumerate(pieces):
        row = pl.multiple_of((place[0] ^ step) * plan.row_local, plan.row_local)
        value = piece[...]
        seen[pl.ds(row, plan.row_local), :] = value
        a, b = split(value)
        high[pl.ds(row, plan.row_local), :] = a
        low[pl.ds(row, plan.row_local), :] = b
    for part, owners in zip(parts, sharers):
        for slot, offset in enumerate(owners):
            for step in range(plan.row_devices):
                row = (place[0] ^ step) * plan.row_local
                row = row + (lax.rem(place[1], plan.sharers) ^ offset) * plan.share_rows
                row = pl.multiple_of(row, plan.share_rows)
                weight[pl.ds(row, plan.share_rows), :] = part[slot, step]

    def rows_pass(table, start, stop):
        count = table[0].shape[0]
        for a in range(start, stop, wide):
            b = min(a + wide, stop)
            value = dot3(table[0][...], table[1][...], high[:, a:b], low[:, a:b])
            mid_high[:count, a:b], mid_low[:count, a:b] = split(value)

    def columns_pass(table, count, window):
        a, b = window
        return dot3(mid_high[:count, a:b], mid_low[:count, a:b], table[0][...], table[1][...])

    keep = 1.0 - step_size * ridge_term
    for iteration in range(ITERS):
        chosen = plan.stage_blocks(iteration)
        windows = [plan.window(plan.blocks[i]) for i in chosen]
        rows_pass(square, windows[0][0], windows[-1][1])
        for i, window in zip(chosen, windows):
            a, b = plan.blocks[i]
            value = columns_pass(bands[i], plan.rows, window)
            if iteration > 0:
                value = value + keep * image[:, a:b]
            image[:, a:b] = value
            given = seen[:, a:b]
            residual = given - weight[:, a:b] * value
            total[:, a:b] = residual + keep * (total[:, a:b] if iteration > 0 else given)
            high[:, a:b], low[:, a:b] = split(residual)
    first, stop = plan.window(plan.out_blocks[0])[0], plan.window(plan.out_blocks[-1])[1]
    high[:, first:stop], low[:, first:stop] = split(total[:, first:stop])
    rows_pass(final, first, stop)
    count = plan.row_devices * plan.slab
    for block in plan.out_blocks:
        size = block[1] - block[0]
        field[:, block[0] - plan.halo : block[1] - plan.halo] = columns_pass(last, count, plan.window(block))
    for step, out in enumerate(outs):
        row = pl.multiple_of((place[0] ^ step) * plan.slab, 8)
        out[...] = field[pl.ds(row, plan.slab), :]


def divergence(own, partner):
    rows, columns = own.shape
    stop = rows - rim
    inner = slice(lane, columns - lane)
    here = partner[rim:stop]
    down, up = partner[rim + 2 : stop + 2, inner], partner[rim - 2 : stop - 2, inner]
    middle = here[:, inner]
    flow = own[rim + 1 : stop + 1, inner] * (down - middle) - own[rim - 1 : stop - 1, inner] * (middle - up)
    level = own[rim:stop]

    def shifted(value, amount):
        return pltpu.roll(value, amount % columns, 1)[:, inner]

    right = shifted(level, -1) * (shifted(here, -2) - middle)
    left = shifted(level, 1) * (middle - shifted(here, 2))
    return 0.25 * (flow + (right - left))


def estimate_kernel(plan, holders, field_width, place, pair_one, pair_two, owner, *refs):
    refs = list(refs)
    pieces = []
    for orders in holders:
        flat = []
        for order in orders:
            ref = refs.pop(0)
            flat += [(offset, ref.at[slot]) for slot, offset in enumerate(order)]
        pieces.append(sorted(flat, key=lambda entry: entry[0]))
    estimate = refs.pop(0)
    mean_field = refs.pop(0) if field_width else None
    own, first, second = refs[:3]
    sems = refs[3]
    rows_at, sim_at = place[0], place[1]
    edge = jnp.zeros((plan.slab, lane), jnp.float32)
    offset_one, offset_two = sim_at ^ pair_one[sim_at], sim_at ^ pair_two[sim_at]
    for step in range(plan.row_devices):
        column = pl.multiple_of(lane + (rows_at ^ step) * plan.share, lane)
        for offset, source in pieces[step]:
            def fetch(target, sem, source=source, column=column):
                pltpu.make_async_copy(source, target.at[:, pl.ds(column, plan.share)], sems.at[sem]).start()

            if offset == 0:
                fetch(own, 0)
            pl.when(offset == offset_one)(functools.partial(fetch, first, 1))
            pl.when(offset == offset_two)(functools.partial(fetch, second, 2))
    if field_width:
        every = refs[4]
        units = field_width // lane
        per = plan.share // lane
        for unit in range(units + 2):
            at = sim_at * units - 1 + unit
            inside = (at >= 0) & (at < plan.columns // lane)
            span = slice(unit * lane, (unit + 1) * lane)
            for step in range(plan.row_devices):
                def fetch_all(step=step, at=at, span=span, unit=unit):
                    column = pl.multiple_of(lax.rem(at, per) * lane, lane)
                    for offset, source in pieces[step]:
                        pltpu.make_async_copy(
                            source.at[:, pl.ds(column, lane)], every.at[sim_at ^ offset, :, span], sems.at[3 + unit]
                        ).start()

                pl.when(inside & (lax.div(at, per) == (rows_at ^ step)))(fetch_all)

            @pl.when(jnp.logical_not(inside))
            def _(span=span):
                every[:, :, span] = jnp.zeros((plan.sim_devices, plan.slab, lane), jnp.float32)

    for number, target in enumerate((own, first, second)):
        target[:, :lane] = edge
        target[:, lane + plan.columns :] = edge
        span = target.at[:, pl.ds(lane, plan.columns)]
        pltpu.make_async_copy(span, span, sems.at[number]).wait()
    for a in range(0, plan.columns, wide):
        span = slice(a, a + wide + 2 * lane)
        estimate[:, a : a + wide] = divergence(own[:, span], 2.0 * first[:, span] - second[:, span])
    if not field_width:
        return
    for unit in range(units + 2):
        at = sim_at * units - 1 + unit

        @pl.when((at >= 0) & (at < plan.columns // lane))
        def _(unit=unit):
            span = every.at[:, :, unit * lane : (unit + 1) * lane]
            pltpu.make_async_copy(span, span, sems.at[3 + unit]).wait()

    mean_field[...] = jnp.zeros(mean_field.shape, jnp.float32)
    for sim in range(plan.sim_devices):
        partner = 2.0 * every[pair_one[sim]] - every[pair_two[sim]]
        mean_field[owner[sim]] += divergence(every[sim], partner)
    for group in range(OWNERS):
        count = jnp.int32(0)
        for sim in range(plan.sim_devices):
            count = count + (owner[sim] == group).astype(jnp.int32)
        mean_field[group] = mean_field[group] / jnp.maximum(count, 1).astype(jnp.float32)


def exchange(value, axis, offset):
    count = lax.axis_size(axis)
    return lax.ppermute(value, axis, [(i, i ^ offset) for i in range(count)])


def gather(first, axis, bits):
    arrays, offsets = [first[None]], [[0]]
    for bit in bits:
        whole = jnp.concatenate(arrays, axis=0) if len(arrays) > 1 else arrays[0]
        arrays.append(exchange(whole, axis, bit))
        offsets.append([offset ^ bit for order in offsets for offset in order])
    return arrays, offsets


def call(kernel, out_shapes, in_specs, scratch, flops, moved, out_specs=None):
    vmem = pl.BlockSpec(memory_space=pltpu.VMEM)
    return pl.pallas_call(
        kernel,
        out_shape=out_shapes,
        in_specs=in_specs,
        out_specs=[vmem] * len(out_shapes) if out_specs is None else out_specs,
        scratch_shapes=scratch,
        compiler_params=pltpu.CompilerParams(vmem_limit_bytes=vmem_bytes),
        cost_estimate=pl.CostEstimate(flops=flops, bytes_accessed=moved, transcendentals=0),
    )


def body(maps, weight, beam, pair_one, pair_two, owner):
    sim_local, row_local, columns = maps.shape
    taps = beam.shape[0]
    row_devices, sim_devices = lax.axis_size("rows"), lax.axis_size("sims")
    plan = Plan(row_devices, sim_devices, row_local, columns, taps)
    place = jnp.stack([lax.axis_index("rows"), lax.axis_index("sims")]).astype(jnp.int32)
    vmem = pl.BlockSpec(memory_space=pltpu.VMEM)
    smem = pl.BlockSpec(memory_space=pltpu.SMEM)
    hbm = pl.BlockSpec(memory_space=pl.ANY)

    def f32(*shape):
        return jax.ShapeDtypeStruct(shape, jnp.float32)

    def b16(*shape):
        return jax.ShapeDtypeStruct(shape, jnp.bfloat16)

    cells = row_local * columns
    made = call(
        functools.partial(weighted_kernel, plan),
        [f32(row_local, plan.width)] * row_devices + [f32(plan.share_rows, plan.width)] * row_devices,
        [smem, vmem, vmem],
        [pltpu.VMEM((row_local, columns + 2 * plan.halo), jnp.float32)],
        cells,
        16 * cells,
    )(place, maps.reshape(row_local, columns), weight)
    pieces, parts = made[:row_devices], made[row_devices:]
    parts = [parts[0]] + [exchange(parts[d], "rows", d) for d in range(1, row_devices)]
    pieces = [pieces[0]] + [exchange(pieces[d], "rows", d) for d in range(1, row_devices)]
    bits = [1 << i for i in range(1, plan.sharers.bit_length() - 1)] + [1]
    parts, sharers = gather(jnp.stack(parts), "sims", bits)

    kernel = beam / jnp.sum(beam)
    blank = jnp.zeros((plan.length - taps,), jnp.float32)
    forward = jnp.roll(jnp.concatenate([kernel, blank]), -plan.margin)[None]
    backward = jnp.roll(jnp.concatenate([kernel[::-1], blank]), -plan.margin)[None]
    shapes = [(plan.rows, plan.rows), (row_devices * plan.slab, plan.rows)]
    for block in plan.blocks + plan.out_blocks[:1]:
        low, high = plan.window(block)
        shapes.append((high - low, block[1] - block[0]))
    tables = call(
        functools.partial(table_kernel, plan),
        [b16(*shape) for shape in shapes for _ in range(2)],
        [smem, vmem, vmem],
        [],
        1 << 32,
        1 << 23,
    )(place, forward, backward)

    full = (plan.rows, plan.width)
    tall = (max(plan.rows, row_devices * plan.slab), plan.width)
    filtered = call(
        functools.partial(filter_kernel, plan, sharers),
        [f32(plan.slab, plan.share)] * row_devices,
        [smem] + [vmem] * (len(pieces) + len(parts) + len(tables)),
        [pltpu.VMEM(full, jnp.float32)] * 4
        + [pltpu.VMEM((row_devices * plan.slab, plan.share), jnp.float32)]
        + [pltpu.VMEM(full, jnp.bfloat16)] * 2
        + [pltpu.VMEM(tall, jnp.bfloat16)] * 2,
        1 << 33,
        1 << 23,
    )(place, *pieces, *parts, *tables)

    held, holders = [], []
    for step in range(row_devices):
        piece = filtered[step] if step == 0 else exchange(filtered[step], "rows", step)
        bits = [1 << i for i in range(1, sim_devices.bit_length() - 1)]
        turn = step % max(len(bits), 1)
        arrays, offsets = gather(piece, "sims", bits[turn:] + bits[:turn] + [1])
        held += arrays
        holders.append(offsets)

    field_width = columns // sim_devices
    fused = field_width if field_width % lane == 0 else 0
    outs = [f32(row_local, columns)]
    extended = (plan.slab, columns + 2 * lane)
    scratch = [pltpu.VMEM(extended, jnp.float32)] * 3
    if fused:
        outs.append(f32(OWNERS, row_local, fused))
        scratch.append(pltpu.SemaphoreType.DMA((3 + fused // lane + 2,)))
        scratch.append(pltpu.VMEM((sim_devices, plan.slab, fused + 2 * lane), jnp.float32))
    else:
        scratch.append(pltpu.SemaphoreType.DMA((3,)))
    results = call(
        functools.partial(estimate_kernel, plan, holders, fused),
        outs,
        [smem] * 4 + [hbm] * len(held),
        scratch,
        1 << 24,
        1 << 23,
    )(place, pair_one, pair_two, owner, *held)
    estimate = results[0]
    if fused:
        mean_field = results[1]
    else:
        groups = jnp.arange(OWNERS, dtype=jnp.int32)
        local_owner = owner[place[1]]
        term = jnp.where((groups == local_owner)[:, None, None], estimate[None], 0.0)
        total = lax.psum_scatter(term, "sims", scatter_dimension=2, tiled=True)
        tally = jnp.sum((groups[:, None] == owner[None, :]).astype(jnp.float32), axis=1)
        mean_field = total / jnp.maximum(tally, 1.0)[:, None, None]
    return estimate.reshape(maps.shape), mean_field


def solution(mesh):
    in_specs = (P("sims", "rows", None), P("rows", None), P(), P(), P(), P())
    out_specs = (P("sims", "rows", None), P(None, "rows", "sims"))
    return jax.shard_map(body, mesh=mesh, in_specs=in_specs, out_specs=out_specs, check_vma=False)
```

```python
import functools

import jax
import jax.numpy as jnp
from jax import lax
from jax.experimental import pallas as pl
from jax.experimental.pallas import tpu as pltpu
from jax.sharding import PartitionSpec as P

ITERS = 3
OWNERS = 8

ridge_term = 0.5
step_size = 0.6
exact = lax.Precision.HIGHEST
lane = 128
wide = 256
stretch = 1024
rim = 4
loads = 4


def split(value):
    high = value.astype(jnp.bfloat16)
    low = (value - high.astype(jnp.float32)).astype(jnp.bfloat16)
    return high, low


def dot(a, b):
    return jnp.dot(a, b, preferred_element_type=jnp.float32)


def dot3(a_high, a_low, b_high, b_low):
    return dot(a_high, b_high) + (dot(a_low, b_high) + dot(a_high, b_low))


class Plan:
    def __init__(self, row_devices, sim_devices, row_local, columns, taps):
        self.row_devices, self.sim_devices = row_devices, sim_devices
        self.row_local, self.columns = row_local, columns
        self.rows = row_devices * row_local
        self.margin = (taps - 1) // 2
        self.share = columns // row_devices
        self.halo = -(-self.margin * (2 * ITERS + 1) // lane) * lane
        self.width = self.share + 2 * self.halo
        self.slab = row_local + 2 * rim
        self.sharers = min(sim_devices, row_local // 8)
        self.share_rows = row_local // self.sharers
        self.length = max(2 * wide, -(-self.rows // lane) * lane)
        inner = range(lane, self.width - lane, wide)
        blocks = [(0, lane)] + [(a, min(a + wide, self.width - lane)) for a in inner]
        self.blocks = blocks + [(self.width - lane, self.width)]
        centre = range(self.halo, self.halo + self.share, wide)
        self.out_blocks = [(a, min(a + wide, self.halo + self.share)) for a in centre]

    def window(self, block):
        return max(0, block[0] - lane), min(self.width, block[1] + lane)

    def stage_blocks(self, iteration):
        low = self.halo - self.margin * (2 * (ITERS - 1 - iteration) + 1)
        return [i for i, (a, b) in enumerate(self.blocks) if b > low and a < self.width - low]


def weighted_kernel(plan, place, maps, weight, *refs):
    count = plan.row_devices
    pieces, parts = refs[:count], refs[count : 2 * count]
    padded, weights, given, sems = refs[2 * count :]
    chunk = plan.row_local // loads
    copies = []
    for number in range(loads):
        rows = pl.ds(number * chunk, chunk)
        inner = pl.ds(plan.halo, plan.columns)
        copies.append((
            pltpu.make_async_copy(weight.at[rows], weights.at[rows, inner], sems.at[0, number]),
            pltpu.make_async_copy(maps.at[rows], given.at[rows], sems.at[1, number]),
        ))
        for copy in copies[-1]:
            copy.start()
    zeros = jnp.zeros((plan.row_local, plan.halo), jnp.float32)
    for target in (padded, weights):
        target[:, : plan.halo] = zeros
        target[:, plan.halo + plan.columns :] = zeros
    inner = slice(plan.halo, plan.halo + plan.columns)
    starts = [pl.multiple_of((place[0] ^ step) * plan.share, lane) for step in range(count)]
    for number in range(loads):
        for copy in copies[number]:
            copy.wait()
        rows = slice(number * chunk, (number + 1) * chunk)
        padded[rows, inner] = weights[rows, inner] * given[rows]
        for step, column in enumerate(starts):
            pieces[step][rows] = padded[rows, pl.ds(column, plan.width)]
    row = pl.multiple_of(lax.rem(place[1], plan.sharers) * plan.share_rows, plan.share_rows)
    for step, column in enumerate(starts):
        parts[step][...] = weights[pl.ds(row, plan.share_rows), pl.ds(column, plan.width)]


def band(plan, taps, rows, columns, offset):
    spread = jnp.broadcast_to(taps[...], (rows, plan.length))
    if offset % plan.length:
        spread = pltpu.roll(spread, offset % plan.length, 1)
    rolled = pltpu.roll(spread, 0, 1, stride=1, stride_axis=0)[:, :columns]
    row = lax.broadcasted_iota(jnp.int32, (rows, columns), 0)
    column = lax.broadcasted_iota(jnp.int32, (rows, columns), 1)
    return jnp.where(jnp.abs(column - row - offset) <= plan.margin, rolled, 0.0)


def table_kernel(plan, place, taps, reverse, *refs):
    tables = list(refs)

    def put(value):
        high, low = split(value)
        tables.pop(0)[...] = high
        tables.pop(0)[...] = low

    rows = plan.rows
    put(jnp.dot(band(plan, taps, rows, rows, 0), band(plan, reverse, rows, rows, 0), precision=exact))
    slabs = []
    for device in range(plan.row_devices):
        first = device * plan.row_local - rim
        part = band(plan, reverse, plan.slab, rows, first)
        row = lax.broadcasted_iota(jnp.int32, part.shape, 0) + first
        slabs.append(jnp.where((row >= 0) & (row < rows), part, 0.0))
    put(jnp.concatenate(slabs, axis=0))
    size = 2 * wide
    forward = band(plan, taps, size, size, 0)
    backward = band(plan, reverse, size, size, 0)
    for block in plan.blocks:
        low, high = plan.window(block)
        extent = high - low
        column = lax.broadcasted_iota(jnp.int32, (extent, extent), 1) + (place[0] * plan.share - plan.halo + low)
        inside = (column >= 0) & (column < plan.columns)
        left = jnp.where(inside, forward[:extent, :extent], 0.0)
        right = backward[:extent, block[0] - low : block[1] - low]
        put(step_size * jnp.dot(left, right, precision=exact))
    for block in plan.out_blocks[:1]:
        low, high = plan.window(block)
        put(step_size * forward[: high - low, block[0] - low : block[1] - low])


def filter_kernel(plan, sharers, place, *refs):
    refs = list(refs)

    def take(number):
        taken = refs[:number]
        del refs[:number]
        return taken

    pieces = take(plan.row_devices)
    parts = take(len(sharers))
    sources = take(2 * (len(plan.blocks) + 3))
    outs = take(plan.row_devices)
    seen, weight, image, total, field, high, low, mid_high, mid_low, sem, sems = refs[:11]
    tables = refs[11:]
    copies = [pltpu.make_async_copy(a, b, sems.at[i]) for i, (a, b) in enumerate(zip(sources, tables))]
    for copy in copies:
        copy.start()
    groups = [(tables[i], tables[i + 1]) for i in range(0, len(tables), 2)]
    square, final, bands, last = groups[0], groups[1], groups[2:-1], groups[-1]
    for part, owners in zip(parts, sharers):
        for slot, offset in enumerate(owners):
            for step in range(plan.row_devices):
                row = (place[0] ^ step) * plan.row_local
                row = row + (lax.rem(place[1], plan.sharers) ^ offset) * plan.share_rows
                rows = pl.ds(pl.multiple_of(row, plan.share_rows), plan.share_rows)
                pltpu.make_async_copy(part.at[slot, step], weight.at[rows], sem).start()
    for step, piece in enumerate(pieces):
        row = pl.multiple_of((place[0] ^ step) * plan.row_local, plan.row_local)
        value = piece[...]
        seen[pl.ds(row, plan.row_local), :] = value
        a, b = split(value)
        high[pl.ds(row, plan.row_local), :] = a
        low[pl.ds(row, plan.row_local), :] = b

    def rows_pass(table, start, stop):
        count = table[0].shape[0]
        for a in range(start, stop, wide):
            b = min(a + wide, stop)
            value = dot3(table[0][...], table[1][...], high[:, a:b], low[:, a:b])
            mid_high[:count, a:b], mid_low[:count, a:b] = split(value)

    def columns_pass(table, count, window):
        a, b = window
        return dot3(mid_high[:count, a:b], mid_low[:count, a:b], table[0][...], table[1][...])

    keep = 1.0 - step_size * ridge_term
    for iteration in range(ITERS):
        chosen = plan.stage_blocks(iteration)
        windows = [plan.window(plan.blocks[i]) for i in chosen]
        if iteration == 0:
            copies[0].wait()
            copies[1].wait()
        rows_pass(square, windows[0][0], windows[-1][1])
        if iteration == 0:
            for copy in copies[2:]:
                copy.wait()
            pltpu.make_async_copy(weight, weight, sem).wait()
        for i, window in zip(chosen, windows):
            a, b = plan.blocks[i]
            value = columns_pass(bands[i], plan.rows, window)
            if iteration > 0:
                value = value + keep * image[:, a:b]
            image[:, a:b] = value
            given = seen[:, a:b]
            residual = given - weight[:, a:b] * value
            total[:, a:b] = residual + keep * (total[:, a:b] if iteration > 0 else given)
            high[:, a:b], low[:, a:b] = split(residual)
    first, stop = plan.window(plan.out_blocks[0])[0], plan.window(plan.out_blocks[-1])[1]
    high[:, first:stop], low[:, first:stop] = split(total[:, first:stop])
    rows_pass(final, first, stop)
    count = plan.row_devices * plan.slab
    for block in plan.out_blocks:
        size = block[1] - block[0]
        field[:, block[0] - plan.halo : block[1] - plan.halo] = columns_pass(last, count, plan.window(block))
    for step, out in enumerate(outs):
        row = pl.multiple_of((place[0] ^ step) * plan.slab, 8)
        out[...] = field[pl.ds(row, plan.slab), :]


def divergence(own, partner):
    rows, columns = own.shape
    stop = rows - rim
    inner = slice(lane, columns - lane)
    here = partner[rim:stop]
    down, up = partner[rim + 2 : stop + 2, inner], partner[rim - 2 : stop - 2, inner]
    middle = here[:, inner]
    flow = own[rim + 1 : stop + 1, inner] * (down - middle) - own[rim - 1 : stop - 1, inner] * (middle - up)
    level = own[rim:stop]

    def shifted(value, amount):
        return pltpu.roll(value, amount % columns, 1)[:, inner]

    right = shifted(level, -1) * (shifted(here, -2) - middle)
    left = shifted(level, 1) * (middle - shifted(here, 2))
    return 0.25 * (flow + (right - left))


def estimate_kernel(plan, holders, field_width, place, pair_one, pair_two, owner, *refs):
    refs = list(refs)
    pieces = []
    for orders in holders:
        flat = []
        for order in orders:
            ref = refs.pop(0)
            flat += [(offset, ref.at[slot]) for slot, offset in enumerate(order)]
        pieces.append(sorted(flat, key=lambda entry: entry[0]))
    estimate = refs.pop(0)
    mean_field = refs.pop(0) if field_width else None
    own, partner, sems = refs[:3]
    rows_at, sim_at = place[0], place[1]
    if field_width:
        every = refs[3]
        units = field_width // lane
        per = plan.share // lane
        for unit in range(units + 2):
            at = sim_at * units - 1 + unit
            inside = (at >= 0) & (at < plan.columns // lane)
            span = slice(unit * lane, (unit + 1) * lane)
            for step in range(plan.row_devices):
                def fetch_all(step=step, at=at, span=span, unit=unit):
                    column = pl.multiple_of(lax.rem(at, per) * lane, lane)
                    for offset, source in pieces[step]:
                        pltpu.make_async_copy(
                            source.at[:, pl.ds(column, lane)], every.at[sim_at ^ offset, :, span], sems.at[unit]
                        ).start()

                pl.when(inside & (lax.div(at, per) == (rows_at ^ step)))(fetch_all)

            @pl.when(jnp.logical_not(inside))
            def _(span=span):
                every[:, :, span] = jnp.zeros((plan.sim_devices, plan.slab, lane), jnp.float32)

    edge = jnp.zeros((plan.slab, lane), jnp.float32)
    for target in (own, partner):
        target[:, :lane] = edge
        target[:, lane + plan.columns :] = edge
    one, two = sim_at ^ pair_one[sim_at], sim_at ^ pair_two[sim_at]

    def factor(offset):
        return jnp.where(one == offset, 2.0, 0.0) - jnp.where(two == offset, 1.0, 0.0)

    for step in range(plan.row_devices):
        column = pl.multiple_of(lane + (rows_at ^ step) * plan.share, lane)
        own[:, pl.ds(column, plan.share)] = pieces[step][0][1][...]
        mixed = factor(0) * pieces[step][0][1][...]
        for offset, source in pieces[step][1:]:
            mixed = mixed + factor(offset) * source[...]
        partner[:, pl.ds(column, plan.share)] = mixed
    for a in range(0, plan.columns, stretch):
        b = min(a + stretch, plan.columns)
        span = slice(a, b + 2 * lane)
        estimate[:, a:b] = divergence(own[:, span], partner[:, span])
    if not field_width:
        return
    for unit in range(units + 2):
        at = sim_at * units - 1 + unit

        @pl.when((at >= 0) & (at < plan.columns // lane))
        def _(unit=unit):
            span = every.at[:, :, unit * lane : (unit + 1) * lane]
            pltpu.make_async_copy(span, span, sems.at[unit]).wait()

    mean_field[...] = jnp.zeros(mean_field.shape, jnp.float32)
    for sim in range(plan.sim_devices):
        partner = 2.0 * every[pair_one[sim]] - every[pair_two[sim]]
        mean_field[owner[sim]] += divergence(every[sim], partner)
    for group in range(OWNERS):
        count = jnp.int32(0)
        for sim in range(plan.sim_devices):
            count = count + (owner[sim] == group).astype(jnp.int32)
        mean_field[group] = mean_field[group] / jnp.maximum(count, 1).astype(jnp.float32)


def exchange(value, axis, offset):
    count = lax.axis_size(axis)
    return lax.ppermute(value, axis, [(i, i ^ offset) for i in range(count)])


def gather(first, axis, bits):
    arrays, offsets = [first[None]], [[0]]
    for bit in bits:
        whole = jnp.concatenate(arrays, axis=0) if len(arrays) > 1 else arrays[0]
        arrays.append(exchange(whole, axis, bit))
        offsets.append([offset ^ bit for order in offsets for offset in order])
    return arrays, offsets


def call(kernel, out_shapes, in_specs, scratch, flops, moved, limit=48):
    vmem = pl.BlockSpec(memory_space=pltpu.VMEM)
    return pl.pallas_call(
        kernel,
        out_shape=out_shapes,
        in_specs=in_specs,
        out_specs=[vmem] * len(out_shapes),
        scratch_shapes=scratch,
        compiler_params=pltpu.CompilerParams(vmem_limit_bytes=limit * 1024 * 1024),
        cost_estimate=pl.CostEstimate(flops=flops, bytes_accessed=moved, transcendentals=0),
    )


def body(maps, weight, beam, pair_one, pair_two, owner):
    sim_local, row_local, columns = maps.shape
    taps = beam.shape[0]
    row_devices, sim_devices = lax.axis_size("rows"), lax.axis_size("sims")
    plan = Plan(row_devices, sim_devices, row_local, columns, taps)
    place = jnp.stack([lax.axis_index("rows"), lax.axis_index("sims")]).astype(jnp.int32)
    vmem = pl.BlockSpec(memory_space=pltpu.VMEM)
    smem = pl.BlockSpec(memory_space=pltpu.SMEM)
    far = pl.BlockSpec(memory_space=pltpu.HBM)

    def f32(*shape):
        return jax.ShapeDtypeStruct(shape, jnp.float32)

    def b16(*shape):
        return jax.ShapeDtypeStruct(shape, jnp.bfloat16)

    cells = row_local * columns
    made = call(
        functools.partial(weighted_kernel, plan),
        [f32(row_local, plan.width)] * row_devices + [f32(plan.share_rows, plan.width)] * row_devices,
        [smem, far, far],
        [pltpu.VMEM((row_local, columns + 2 * plan.halo), jnp.float32)] * 2
        + [pltpu.VMEM((row_local, columns), jnp.float32), pltpu.SemaphoreType.DMA((2, loads))],
        cells,
        16 * cells,
        limit=60,
    )(place, maps.reshape(row_local, columns), weight)
    pieces, parts = made[:row_devices], made[row_devices:]
    pieces = [pieces[0]] + [exchange(pieces[d], "rows", d) for d in range(1, row_devices)]
    sharers = []
    shapes = [(plan.rows, plan.rows), (row_devices * plan.slab, plan.rows)]
    for block in plan.blocks + plan.out_blocks[:1]:
        low, high = plan.window(block)
        shapes.append((high - low, block[1] - block[0]))

    def prepare(parts, beam):
        parts = list(parts)
        for bit in [1 << i for i in reversed(range(row_devices.bit_length() - 1))]:
            moved = [step for step in range(row_devices) if step & bit]
            received = exchange(jnp.stack([parts[step] for step in moved]), "rows", bit)
            for slot, step in enumerate(moved):
                parts[step] = received[slot]
        bits = [1 << i for i in range(1, plan.sharers.bit_length() - 1)] + [1]
        arrays, offsets = gather(jnp.stack(parts), "sims", bits)
        sharers[:] = offsets
        kernel = beam / jnp.sum(beam)
        blank = jnp.zeros((plan.length - taps,), jnp.float32)
        forward = jnp.roll(jnp.concatenate([kernel, blank]), -plan.margin)[None]
        backward = jnp.roll(jnp.concatenate([kernel[::-1], blank]), -plan.margin)[None]
        tables = call(
            functools.partial(table_kernel, plan),
            [b16(*shape) for shape in shapes for _ in range(2)],
            [smem, vmem, vmem],
            [],
            1 << 32,
            1 << 23,
        )(place, forward, backward)
        return arrays, tables

    made = jax.eval_shape(prepare, parts, beam)
    parts, tables = lax.cond(
        owner[0] >= 0,
        prepare,
        lambda parts, beam: jax.tree.map(lambda x: jnp.zeros(x.shape, x.dtype), made),
        parts,
        beam,
    )

    full = (plan.rows, plan.width)
    tall = (max(plan.rows, row_devices * plan.slab), plan.width)
    filtered = call(
        functools.partial(filter_kernel, plan, sharers),
        [f32(plan.slab, plan.share)] * row_devices,
        [smem] + [vmem] * len(pieces) + [far] * (len(parts) + len(tables)),
        [pltpu.VMEM(full, jnp.float32)] * 4
        + [pltpu.VMEM((row_devices * plan.slab, plan.share), jnp.float32)]
        + [pltpu.VMEM(full, jnp.bfloat16)] * 2
        + [pltpu.VMEM(tall, jnp.bfloat16)] * 2
        + [pltpu.SemaphoreType.DMA, pltpu.SemaphoreType.DMA((2 * len(shapes),))]
        + [pltpu.VMEM(shape, jnp.bfloat16) for shape in shapes for _ in range(2)],
        1 << 33,
        1 << 23,
    )(place, *pieces, *parts, *tables)

    held, holders = [], []
    for step in range(row_devices):
        piece = filtered[step] if step == 0 else exchange(filtered[step], "rows", step)
        bits = [1 << i for i in range(1, sim_devices.bit_length() - 1)]
        turn = step % max(len(bits), 1)
        arrays, offsets = gather(piece, "sims", bits[turn:] + bits[:turn] + [1])
        held += arrays
        holders.append(offsets)

    field_width = columns // sim_devices
    fused = field_width if field_width % lane == 0 else 0
    outs = [f32(row_local, columns)]
    extended = (plan.slab, columns + 2 * lane)
    scratch = [pltpu.VMEM(extended, jnp.float32)] * 2
    if fused:
        outs.append(f32(OWNERS, row_local, fused))
        scratch.append(pltpu.SemaphoreType.DMA((fused // lane + 2,)))
        scratch.append(pltpu.VMEM((sim_devices, plan.slab, fused + 2 * lane), jnp.float32))
    else:
        scratch.append(pltpu.SemaphoreType.DMA((1,)))
    results = call(
        functools.partial(estimate_kernel, plan, holders, fused),
        outs,
        [smem] * 4 + [vmem] * len(held),
        scratch,
        1 << 24,
        1 << 23,
    )(place, pair_one, pair_two, owner, *held)
    estimate = results[0]
    if fused:
        mean_field = results[1]
    else:
        groups = jnp.arange(OWNERS, dtype=jnp.int32)
        local_owner = owner[place[1]]
        term = jnp.where((groups == local_owner)[:, None, None], estimate[None], 0.0)
        total = lax.psum_scatter(term, "sims", scatter_dimension=2, tiled=True)
        tally = jnp.sum((groups[:, None] == owner[None, :]).astype(jnp.float32), axis=1)
        mean_field = total / jnp.maximum(tally, 1.0)[:, None, None]
    return estimate.reshape(maps.shape), mean_field


def solution(mesh):
    in_specs = (P("sims", "rows", None), P("rows", None), P(), P(), P(), P())
    out_specs = (P("sims", "rows", None), P(None, "rows", "sims"))
    return jax.shard_map(body, mesh=mesh, in_specs=in_specs, out_specs=out_specs, check_vma=False)
```

```python
import functools

import jax
import jax.numpy as jnp
from jax import lax
from jax.experimental import pallas as pl
from jax.experimental.pallas import tpu as pltpu
from jax.sharding import PartitionSpec as P

ITERS = 3
OWNERS = 8

ridge_term = 0.5
step_size = 0.6
exact = lax.Precision.HIGHEST
lane = 128
wide = 256
stretch = 1024
rim = 4
loads = 4


def split(value):
    high = value.astype(jnp.bfloat16)
    low = (value - high.astype(jnp.float32)).astype(jnp.bfloat16)
    return high, low


def dot(a, b):
    return jnp.dot(a, b, preferred_element_type=jnp.float32)


def dot3(a_high, a_low, b_high, b_low):
    return dot(a_high, b_high) + (dot(a_low, b_high) + dot(a_high, b_low))


class Plan:
    def __init__(self, row_devices, sim_devices, row_local, columns, taps):
        self.row_devices, self.sim_devices = row_devices, sim_devices
        self.row_local, self.columns = row_local, columns
        self.rows = row_devices * row_local
        self.margin = (taps - 1) // 2
        self.share = columns // row_devices
        self.halo = -(-self.margin * (2 * ITERS + 1) // lane) * lane
        self.width = self.share + 2 * self.halo
        self.slab = row_local + 2 * rim
        self.sharers = min(sim_devices, row_local // 8)
        self.share_rows = row_local // self.sharers
        self.length = max(2 * wide, -(-self.rows // lane) * lane)
        inner = range(lane, self.width - lane, wide)
        blocks = [(0, lane)] + [(a, min(a + wide, self.width - lane)) for a in inner]
        self.blocks = blocks + [(self.width - lane, self.width)]
        centre = range(self.halo, self.halo + self.share, wide)
        self.out_blocks = [(a, min(a + wide, self.halo + self.share)) for a in centre]

    def window(self, block):
        return max(0, block[0] - lane), min(self.width, block[1] + lane)

    def stage_blocks(self, iteration):
        low = self.halo - self.margin * (2 * (ITERS - 1 - iteration) + 1)
        return [i for i, (a, b) in enumerate(self.blocks) if b > low and a < self.width - low]


def share_kernel(plan, place, weight, *refs):
    parts, padded, sem = refs[: plan.row_devices], refs[-2], refs[-1]
    row = pl.multiple_of(lax.rem(place[1], plan.sharers) * plan.share_rows, plan.share_rows)
    source = weight.at[pl.ds(row, plan.share_rows)]
    copy = pltpu.make_async_copy(source, padded.at[:, pl.ds(plan.halo, plan.columns)], sem)
    copy.start()
    zeros = jnp.zeros((plan.share_rows, plan.halo), jnp.float32)
    padded[:, : plan.halo] = zeros
    padded[:, plan.halo + plan.columns :] = zeros
    copy.wait()
    for step, part in enumerate(parts):
        column = pl.multiple_of((place[0] ^ step) * plan.share, lane)
        part[...] = padded[:, pl.ds(column, plan.width)]


def weighted_kernel(plan, place, maps, weight, *refs):
    pieces = refs[: plan.row_devices]
    padded, weights, given, sems = refs[plan.row_devices :]
    chunk = plan.row_local // loads
    copies = []
    for number in range(loads):
        rows = pl.ds(number * chunk, chunk)
        copies.append((
            pltpu.make_async_copy(weight.at[rows], weights.at[rows], sems.at[0, number]),
            pltpu.make_async_copy(maps.at[rows], given.at[rows], sems.at[1, number]),
        ))
        for copy in copies[-1]:
            copy.start()
    zeros = jnp.zeros((plan.row_local, plan.halo), jnp.float32)
    padded[:, : plan.halo] = zeros
    padded[:, plan.halo + plan.columns :] = zeros
    for number in range(loads):
        for copy in copies[number]:
            copy.wait()
        rows = slice(number * chunk, (number + 1) * chunk)
        padded[rows, plan.halo : plan.halo + plan.columns] = weights[rows] * given[rows]
        for step, piece in enumerate(pieces):
            column = pl.multiple_of((place[0] ^ step) * plan.share, lane)
            piece[rows] = padded[rows, pl.ds(column, plan.width)]


def band(plan, taps, rows, columns, offset):
    spread = jnp.broadcast_to(taps[...], (rows, plan.length))
    if offset % plan.length:
        spread = pltpu.roll(spread, offset % plan.length, 1)
    rolled = pltpu.roll(spread, 0, 1, stride=1, stride_axis=0)[:, :columns]
    row = lax.broadcasted_iota(jnp.int32, (rows, columns), 0)
    column = lax.broadcasted_iota(jnp.int32, (rows, columns), 1)
    return jnp.where(jnp.abs(column - row - offset) <= plan.margin, rolled, 0.0)


def table_kernel(plan, place, taps, reverse, *refs):
    tables = list(refs)

    def put(value):
        high, low = split(value)
        tables.pop(0)[...] = high
        tables.pop(0)[...] = low

    rows = plan.rows
    put(jnp.dot(band(plan, taps, rows, rows, 0), band(plan, reverse, rows, rows, 0), precision=exact))
    slabs = []
    for device in range(plan.row_devices):
        first = device * plan.row_local - rim
        part = band(plan, reverse, plan.slab, rows, first)
        row = lax.broadcasted_iota(jnp.int32, part.shape, 0) + first
        slabs.append(jnp.where((row >= 0) & (row < rows), part, 0.0))
    put(jnp.concatenate(slabs, axis=0))
    size = 2 * wide
    forward = band(plan, taps, size, size, 0)
    backward = band(plan, reverse, size, size, 0)
    for block in plan.blocks:
        low, high = plan.window(block)
        extent = high - low
        column = lax.broadcasted_iota(jnp.int32, (extent, extent), 1) + (place[0] * plan.share - plan.halo + low)
        inside = (column >= 0) & (column < plan.columns)
        left = jnp.where(inside, forward[:extent, :extent], 0.0)
        right = backward[:extent, block[0] - low : block[1] - low]
        put(step_size * jnp.dot(left, right, precision=exact))
    for block in plan.out_blocks[:1]:
        low, high = plan.window(block)
        put(step_size * forward[: high - low, block[0] - low : block[1] - low])


def filter_kernel(plan, sharers, place, *refs):
    refs = list(refs)

    def take(number):
        taken = refs[:number]
        del refs[:number]
        return taken

    pieces = take(plan.row_devices)
    parts = take(len(sharers))
    square, final = take(2), take(2)
    bands = [take(2) for _ in plan.blocks]
    last = take(2)
    outs = take(plan.row_devices)
    seen, weight, image, total, field, high, low, mid_high, mid_low = refs
    for step, piece in enumerate(pieces):
        row = pl.multiple_of((place[0] ^ step) * plan.row_local, plan.row_local)
        value = piece[...]
        seen[pl.ds(row, plan.row_local), :] = value
        a, b = split(value)
        high[pl.ds(row, plan.row_local), :] = a
        low[pl.ds(row, plan.row_local), :] = b
    for part, owners in zip(parts, sharers):
        for slot, offset in enumerate(owners):
            for step in range(plan.row_devices):
                row = (place[0] ^ step) * plan.row_local
                row = row + (lax.rem(place[1], plan.sharers) ^ offset) * plan.share_rows
                row = pl.multiple_of(row, plan.share_rows)
                weight[pl.ds(row, plan.share_rows), :] = part[slot, step]

    def rows_pass(table, start, stop):
        count = table[0].shape[0]
        for a in range(start, stop, wide):
            b = min(a + wide, stop)
            value = dot3(table[0][...], table[1][...], high[:, a:b], low[:, a:b])
            mid_high[:count, a:b], mid_low[:count, a:b] = split(value)

    def columns_pass(table, count, window):
        a, b = window
        return dot3(mid_high[:count, a:b], mid_low[:count, a:b], table[0][...], table[1][...])

    keep = 1.0 - step_size * ridge_term
    for iteration in range(ITERS):
        chosen = plan.stage_blocks(iteration)
        windows = [plan.window(plan.blocks[i]) for i in chosen]
        rows_pass(square, windows[0][0], windows[-1][1])
        for i, window in zip(chosen, windows):
            a, b = plan.blocks[i]
            value = columns_pass(bands[i], plan.rows, window)
            if iteration > 0:
                value = value + keep * image[:, a:b]
            image[:, a:b] = value
            given = seen[:, a:b]
            residual = given - weight[:, a:b] * value
            total[:, a:b] = residual + keep * (total[:, a:b] if iteration > 0 else given)
            high[:, a:b], low[:, a:b] = split(residual)
    first, stop = plan.window(plan.out_blocks[0])[0], plan.window(plan.out_blocks[-1])[1]
    high[:, first:stop], low[:, first:stop] = split(total[:, first:stop])
    rows_pass(final, first, stop)
    count = plan.row_devices * plan.slab
    for block in plan.out_blocks:
        size = block[1] - block[0]
        field[:, block[0] - plan.halo : block[1] - plan.halo] = columns_pass(last, count, plan.window(block))
    for step, out in enumerate(outs):
        row = pl.multiple_of((place[0] ^ step) * plan.slab, 8)
        out[...] = field[pl.ds(row, plan.slab), :]


def divergence(own, partner):
    rows, columns = own.shape
    stop = rows - rim
    inner = slice(lane, columns - lane)
    here = partner[rim:stop]
    down, up = partner[rim + 2 : stop + 2, inner], partner[rim - 2 : stop - 2, inner]
    middle = here[:, inner]
    flow = own[rim + 1 : stop + 1, inner] * (down - middle) - own[rim - 1 : stop - 1, inner] * (middle - up)
    level = own[rim:stop]

    def shifted(value, amount):
        return pltpu.roll(value, amount % columns, 1)[:, inner]

    right = shifted(level, -1) * (shifted(here, -2) - middle)
    left = shifted(level, 1) * (middle - shifted(here, 2))
    return 0.25 * (flow + (right - left))


def estimate_kernel(plan, holders, field_width, place, pair_one, pair_two, owner, *refs):
    refs = list(refs)
    pieces = []
    for orders in holders:
        flat = []
        for order in orders:
            ref = refs.pop(0)
            flat += [(offset, ref.at[slot]) for slot, offset in enumerate(order)]
        pieces.append(sorted(flat, key=lambda entry: entry[0]))
    estimate = refs.pop(0)
    mean_field = refs.pop(0) if field_width else None
    own, partner, sems = refs[:3]
    rows_at, sim_at = place[0], place[1]
    if field_width:
        every = refs[3]
        units = field_width // lane
        per = plan.share // lane
        for unit in range(units + 2):
            at = sim_at * units - 1 + unit
            inside = (at >= 0) & (at < plan.columns // lane)
            span = slice(unit * lane, (unit + 1) * lane)
            for step in range(plan.row_devices):
                def fetch_all(step=step, at=at, span=span, unit=unit):
                    column = pl.multiple_of(lax.rem(at, per) * lane, lane)
                    for offset, source in pieces[step]:
                        pltpu.make_async_copy(
                            source.at[:, pl.ds(column, lane)], every.at[sim_at ^ offset, :, span], sems.at[unit]
                        ).start()

                pl.when(inside & (lax.div(at, per) == (rows_at ^ step)))(fetch_all)

            @pl.when(jnp.logical_not(inside))
            def _(span=span):
                every[:, :, span] = jnp.zeros((plan.sim_devices, plan.slab, lane), jnp.float32)

    edge = jnp.zeros((plan.slab, lane), jnp.float32)
    for target in (own, partner):
        target[:, :lane] = edge
        target[:, lane + plan.columns :] = edge
    one, two = sim_at ^ pair_one[sim_at], sim_at ^ pair_two[sim_at]

    def factor(offset):
        return jnp.where(one == offset, 2.0, 0.0) - jnp.where(two == offset, 1.0, 0.0)

    for step in range(plan.row_devices):
        column = pl.multiple_of(lane + (rows_at ^ step) * plan.share, lane)
        own[:, pl.ds(column, plan.share)] = pieces[step][0][1][...]
        mixed = factor(0) * pieces[step][0][1][...]
        for offset, source in pieces[step][1:]:
            mixed = mixed + factor(offset) * source[...]
        partner[:, pl.ds(column, plan.share)] = mixed
    for a in range(0, plan.columns, stretch):
        b = min(a + stretch, plan.columns)
        span = slice(a, b + 2 * lane)
        estimate[:, a:b] = divergence(own[:, span], partner[:, span])
    if not field_width:
        return
    for unit in range(units + 2):
        at = sim_at * units - 1 + unit

        @pl.when((at >= 0) & (at < plan.columns // lane))
        def _(unit=unit):
            span = every.at[:, :, unit * lane : (unit + 1) * lane]
            pltpu.make_async_copy(span, span, sems.at[unit]).wait()

    mean_field[...] = jnp.zeros(mean_field.shape, jnp.float32)
    for sim in range(plan.sim_devices):
        partner = 2.0 * every[pair_one[sim]] - every[pair_two[sim]]
        mean_field[owner[sim]] += divergence(every[sim], partner)
    for group in range(OWNERS):
        count = jnp.int32(0)
        for sim in range(plan.sim_devices):
            count = count + (owner[sim] == group).astype(jnp.int32)
        mean_field[group] = mean_field[group] / jnp.maximum(count, 1).astype(jnp.float32)


def exchange(value, axis, offset):
    count = lax.axis_size(axis)
    return lax.ppermute(value, axis, [(i, i ^ offset) for i in range(count)])


def gather(first, axis, bits):
    arrays, offsets = [first[None]], [[0]]
    for bit in bits:
        whole = jnp.concatenate(arrays, axis=0) if len(arrays) > 1 else arrays[0]
        arrays.append(exchange(whole, axis, bit))
        offsets.append([offset ^ bit for order in offsets for offset in order])
    return arrays, offsets


def call(kernel, out_shapes, in_specs, scratch, flops, moved, limit=48):
    vmem = pl.BlockSpec(memory_space=pltpu.VMEM)
    return pl.pallas_call(
        kernel,
        out_shape=out_shapes,
        in_specs=in_specs,
        out_specs=[vmem] * len(out_shapes),
        scratch_shapes=scratch,
        compiler_params=pltpu.CompilerParams(vmem_limit_bytes=limit * 1024 * 1024),
        cost_estimate=pl.CostEstimate(flops=flops, bytes_accessed=moved, transcendentals=0),
    )


def body(maps, weight, beam, pair_one, pair_two, owner):
    sim_local, row_local, columns = maps.shape
    taps = beam.shape[0]
    row_devices, sim_devices = lax.axis_size("rows"), lax.axis_size("sims")
    plan = Plan(row_devices, sim_devices, row_local, columns, taps)
    place = jnp.stack([lax.axis_index("rows"), lax.axis_index("sims")]).astype(jnp.int32)
    vmem = pl.BlockSpec(memory_space=pltpu.VMEM)
    smem = pl.BlockSpec(memory_space=pltpu.SMEM)
    far = pl.BlockSpec(memory_space=pltpu.HBM)

    def f32(*shape):
        return jax.ShapeDtypeStruct(shape, jnp.float32)

    def b16(*shape):
        return jax.ShapeDtypeStruct(shape, jnp.bfloat16)

    cells = row_local * columns
    parts = call(
        functools.partial(share_kernel, plan),
        [f32(plan.share_rows, plan.width)] * row_devices,
        [smem, far],
        [pltpu.VMEM((plan.share_rows, columns + 2 * plan.halo), jnp.float32), pltpu.SemaphoreType.DMA],
        0,
        1 << 18,
        limit=60,
    )(place, weight)
    pieces = call(
        functools.partial(weighted_kernel, plan),
        [f32(row_local, plan.width)] * row_devices,
        [smem, far, far],
        [pltpu.VMEM((row_local, columns + 2 * plan.halo), jnp.float32)]
        + [pltpu.VMEM((row_local, columns), jnp.float32)] * 2
        + [pltpu.SemaphoreType.DMA((2, loads))],
        cells,
        16 * cells,
        limit=60,
    )(place, maps.reshape(row_local, columns), weight)
    parts = [parts[0]] + [exchange(parts[d], "rows", d) for d in range(1, row_devices)]
    pieces, parts = lax.optimization_barrier((pieces, parts))
    pieces = [pieces[0]] + [exchange(pieces[d], "rows", d) for d in range(1, row_devices)]
    sharers = []
    shapes = [(plan.rows, plan.rows), (row_devices * plan.slab, plan.rows)]
    for block in plan.blocks + plan.out_blocks[:1]:
        low, high = plan.window(block)
        shapes.append((high - low, block[1] - block[0]))

    def prepare(parts, beam):
        bits = [1 << i for i in range(1, plan.sharers.bit_length() - 1)] + [1]
        arrays, offsets = gather(jnp.stack(parts), "sims", bits)
        sharers[:] = offsets
        kernel = beam / jnp.sum(beam)
        blank = jnp.zeros((plan.length - taps,), jnp.float32)
        forward = jnp.roll(jnp.concatenate([kernel, blank]), -plan.margin)[None]
        backward = jnp.roll(jnp.concatenate([kernel[::-1], blank]), -plan.margin)[None]
        tables = call(
            functools.partial(table_kernel, plan),
            [b16(*shape) for shape in shapes for _ in range(2)],
            [smem, vmem, vmem],
            [],
            1 << 32,
            1 << 23,
        )(place, forward, backward)
        return arrays, tables

    made = jax.eval_shape(prepare, parts, beam)
    parts, tables = lax.cond(
        lax.axis_index("rows") < row_devices,
        prepare,
        lambda parts, beam: jax.tree.map(lambda x: jnp.zeros(x.shape, x.dtype), made),
        parts,
        beam,
    )

    full = (plan.rows, plan.width)
    tall = (max(plan.rows, row_devices * plan.slab), plan.width)
    filtered = call(
        functools.partial(filter_kernel, plan, sharers),
        [f32(plan.slab, plan.share)] * row_devices,
        [smem] + [vmem] * len(pieces) + [vmem] * (len(parts) + len(tables)),
        [pltpu.VMEM(full, jnp.float32)] * 4
        + [pltpu.VMEM((row_devices * plan.slab, plan.share), jnp.float32)]
        + [pltpu.VMEM(full, jnp.bfloat16)] * 2
        + [pltpu.VMEM(tall, jnp.bfloat16)] * 2,
        1 << 33,
        1 << 23,
    )(place, *pieces, *parts, *tables)

    moved = [filtered[0]] + [exchange(filtered[step], "rows", step) for step in range(1, row_devices)]
    bits = [1 << i for i in range(1, sim_devices.bit_length() - 1)]
    arrays, holders = [], []
    for step in range(row_devices):
        turn = step % max(len(bits), 1)
        found, offsets = gather(moved[step], "sims", bits[turn:] + bits[:turn])
        arrays.append(found)
        holders.append(offsets)
    held = []
    for found, offsets in zip(arrays, holders):
        held += found + [exchange(jnp.concatenate(found), "sims", 1)]
        offsets.append([offset ^ 1 for order in offsets for offset in order])

    field_width = columns // sim_devices
    fused = field_width if field_width % lane == 0 else 0
    outs = [f32(row_local, columns)]
    extended = (plan.slab, columns + 2 * lane)
    scratch = [pltpu.VMEM(extended, jnp.float32)] * 2
    if fused:
        outs.append(f32(OWNERS, row_local, fused))
        scratch.append(pltpu.SemaphoreType.DMA((fused // lane + 2,)))
        scratch.append(pltpu.VMEM((sim_devices, plan.slab, fused + 2 * lane), jnp.float32))
    else:
        scratch.append(pltpu.SemaphoreType.DMA((1,)))
    results = call(
        functools.partial(estimate_kernel, plan, holders, fused),
        outs,
        [smem] * 4 + [vmem] * len(held),
        scratch,
        1 << 24,
        1 << 23,
    )(place, pair_one, pair_two, owner, *held)
    estimate = results[0]
    if fused:
        mean_field = results[1]
    else:
        groups = jnp.arange(OWNERS, dtype=jnp.int32)
        local_owner = owner[place[1]]
        term = jnp.where((groups == local_owner)[:, None, None], estimate[None], 0.0)
        total = lax.psum_scatter(term, "sims", scatter_dimension=2, tiled=True)
        tally = jnp.sum((groups[:, None] == owner[None, :]).astype(jnp.float32), axis=1)
        mean_field = total / jnp.maximum(tally, 1.0)[:, None, None]
    return estimate.reshape(maps.shape), mean_field


def solution(mesh):
    in_specs = (P("sims", "rows", None), P("rows", None), P(), P(), P(), P())
    out_specs = (P("sims", "rows", None), P(None, "rows", "sims"))
    return jax.shard_map(body, mesh=mesh, in_specs=in_specs, out_specs=out_specs, check_vma=False)
```

```python
import functools

import jax
import jax.numpy as jnp
from jax import lax
from jax.experimental import pallas as pl
from jax.experimental.pallas import tpu as pltpu
from jax.sharding import PartitionSpec as P

ITERS = 3
OWNERS = 8

ridge_term = 0.5
step_size = 0.6
exact = lax.Precision.HIGHEST
lane = 128
wide = 256
stretch = 1024
rim = 4
loads = 4


def split(value):
    high = value.astype(jnp.bfloat16)
    low = (value - high.astype(jnp.float32)).astype(jnp.bfloat16)
    return high, low


def dot(a, b):
    return jnp.dot(a, b, preferred_element_type=jnp.float32)


def dot3(a_high, a_low, b_high, b_low):
    return dot(a_high, b_high) + (dot(a_low, b_high) + dot(a_high, b_low))


class Plan:
    def __init__(self, row_devices, sim_devices, row_local, columns, taps):
        self.row_devices, self.sim_devices = row_devices, sim_devices
        self.row_local, self.columns = row_local, columns
        self.rows = row_devices * row_local
        self.margin = (taps - 1) // 2
        self.share = columns // row_devices
        self.halo = -(-self.margin * (2 * ITERS + 1) // lane) * lane
        self.width = self.share + 2 * self.halo
        self.slab = row_local + 2 * rim
        self.sharers = min(sim_devices, row_local // 8)
        self.share_rows = row_local // self.sharers
        self.head = row_local // 2
        self.length = max(2 * wide, -(-self.rows // lane) * lane)
        inner = range(lane, self.width - lane, wide)
        blocks = [(0, lane)] + [(a, min(a + wide, self.width - lane)) for a in inner]
        self.blocks = blocks + [(self.width - lane, self.width)]
        centre = range(self.halo, self.halo + self.share, wide)
        self.out_blocks = [(a, min(a + wide, self.halo + self.share)) for a in centre]

    def window(self, block):
        return max(0, block[0] - lane), min(self.width, block[1] + lane)

    def stage_blocks(self, iteration):
        low = self.halo - self.margin * (2 * (ITERS - 1 - iteration) + 1)
        return [i for i, (a, b) in enumerate(self.blocks) if b > low and a < self.width - low]


def piece_kernel(plan, place, maps, weight, *refs):
    count = plan.row_devices
    heads, tails = refs[:count], refs[count : 2 * count]
    product, weights, given, sems = refs[2 * count :]
    chunk = plan.row_local // loads
    inner = slice(plan.halo, plan.halo + plan.columns)
    copies = []
    for number in range(loads):
        rows = pl.ds(number * chunk, chunk)
        copies.append((
            pltpu.make_async_copy(weight.at[rows], weights.at[rows, inner], sems.at[0, number]),
            pltpu.make_async_copy(maps.at[rows], given.at[rows], sems.at[1, number]),
        ))
        for copy in copies[-1]:
            copy.start()
    zeros = jnp.zeros((plan.row_local, plan.halo), jnp.float32)
    for target in (product, weights):
        target[:, : plan.halo] = zeros
        target[:, plan.halo + plan.columns :] = zeros
    for number in range(loads):
        for copy in copies[number]:
            copy.wait()
        rows = slice(number * chunk, (number + 1) * chunk)
        product[rows, inner] = weights[rows, inner] * given[rows]
    row = pl.multiple_of(lax.rem(place[1], plan.sharers) * plan.share_rows, plan.share_rows)
    for step in range(count):
        span = pl.ds(pl.multiple_of((place[0] ^ step) * plan.share, lane), plan.width)
        heads[step][: plan.share_rows] = weights[pl.ds(row, plan.share_rows), span]
        heads[step][plan.share_rows :] = product[: plan.head, span]
        tails[step][...] = product[plan.head :, span]


def band(plan, taps, rows, columns, offset):
    if offset % plan.length:
        taps = pltpu.roll(taps, offset % plan.length, 1)
    spread = jnp.broadcast_to(taps[:1], (rows, plan.length))
    rolled = pltpu.roll(spread, 0, 1, stride=1, stride_axis=0)[:, :columns]
    row = lax.broadcasted_iota(jnp.int32, (rows, columns), 0)
    column = lax.broadcasted_iota(jnp.int32, (rows, columns), 1)
    return jnp.where(jnp.abs(column - row - offset) <= plan.margin, rolled, 0.0)


def table_kernel(plan, place, beam, *refs):
    refs, line = refs[:-1], refs[-1]
    count = beam.shape[1]
    line[...] = jnp.zeros(line.shape, jnp.float32)
    line[:1, :count] = beam[...]
    kernel = line[...]
    kernel = kernel / jnp.sum(kernel[:1], axis=1, keepdims=True)
    size = kernel.shape[1]
    row = lax.broadcasted_iota(jnp.int32, (size, size), 0)
    column = lax.broadcasted_iota(jnp.int32, (size, size), 1)
    mirror = (row + column == count - 1).astype(jnp.float32)
    blank = jnp.zeros((kernel.shape[0], plan.length - size), jnp.float32)

    def centred(values):
        return pltpu.roll(jnp.concatenate([values, blank], axis=1), plan.length - plan.margin, 1)

    taps, reverse = centred(kernel), centred(jnp.dot(kernel, mirror, precision=exact))
    tables = list(refs)

    def put(value):
        high, low = split(value)
        tables.pop(0)[...] = high
        tables.pop(0)[...] = low

    rows = plan.rows
    put(jnp.dot(band(plan, taps, rows, rows, 0), band(plan, reverse, rows, rows, 0), precision=exact))
    slabs = []
    for device in range(plan.row_devices):
        first = device * plan.row_local - rim
        part = band(plan, reverse, plan.slab, rows, first)
        row = lax.broadcasted_iota(jnp.int32, part.shape, 0) + first
        slabs.append(jnp.where((row >= 0) & (row < rows), part, 0.0))
    put(jnp.concatenate(slabs, axis=0))
    size = 2 * wide
    forward = band(plan, taps, size, size, 0)
    backward = band(plan, reverse, size, size, 0)
    for block in plan.blocks:
        low, high = plan.window(block)
        extent = high - low
        column = lax.broadcasted_iota(jnp.int32, (extent, extent), 1) + (place[0] * plan.share - plan.halo + low)
        inside = (column >= 0) & (column < plan.columns)
        left = jnp.where(inside, forward[:extent, :extent], 0.0)
        right = backward[:extent, block[0] - low : block[1] - low]
        put(step_size * jnp.dot(left, right, precision=exact))
    for block in plan.out_blocks[:1]:
        low, high = plan.window(block)
        put(step_size * forward[: high - low, block[0] - low : block[1] - low])


def filter_kernel(plan, sharers, place, *refs):
    refs = list(refs)

    def take(number):
        taken = refs[:number]
        del refs[:number]
        return taken

    heads, tails = take(plan.row_devices), take(plan.row_devices)
    parts = take(len(sharers))
    square, final = take(2), take(2)
    bands = [take(2) for _ in plan.blocks]
    last = take(2)
    outs = take(plan.row_devices)
    seen, weight, image, total, field, high, low, mid_high, mid_low = refs
    for step in range(plan.row_devices):
        row = pl.multiple_of((place[0] ^ step) * plan.row_local, plan.row_local)
        for first, value in ((0, heads[step][plan.share_rows :]), (plan.head, tails[step][...])):
            rows = pl.ds(row + first, value.shape[0])
            seen[rows, :] = value
            high[rows, :], low[rows, :] = split(value)
    for part, owners in zip(parts, sharers):
        for slot, offset in enumerate(owners):
            for step in range(plan.row_devices):
                row = (place[0] ^ step) * plan.row_local
                row = row + (lax.rem(place[1], plan.sharers) ^ offset) * plan.share_rows
                row = pl.multiple_of(row, plan.share_rows)
                weight[pl.ds(row, plan.share_rows), :] = part[slot, step]

    def rows_pass(table, start, stop):
        count = table[0].shape[0]
        for a in range(start, stop, wide):
            b = min(a + wide, stop)
            value = dot3(table[0][...], table[1][...], high[:, a:b], low[:, a:b])
            mid_high[:count, a:b], mid_low[:count, a:b] = split(value)

    def columns_pass(table, count, window):
        a, b = window
        return dot3(mid_high[:count, a:b], mid_low[:count, a:b], table[0][...], table[1][...])

    keep = 1.0 - step_size * ridge_term
    for iteration in range(ITERS):
        chosen = plan.stage_blocks(iteration)
        windows = [plan.window(plan.blocks[i]) for i in chosen]
        rows_pass(square, windows[0][0], windows[-1][1])
        for i, window in zip(chosen, windows):
            a, b = plan.blocks[i]
            value = columns_pass(bands[i], plan.rows, window)
            if iteration > 0:
                value = value + keep * image[:, a:b]
            image[:, a:b] = value
            given = seen[:, a:b]
            residual = given - weight[:, a:b] * value
            total[:, a:b] = residual + keep * (total[:, a:b] if iteration > 0 else given)
            high[:, a:b], low[:, a:b] = split(residual)
    first, stop = plan.window(plan.out_blocks[0])[0], plan.window(plan.out_blocks[-1])[1]
    high[:, first:stop], low[:, first:stop] = split(total[:, first:stop])
    rows_pass(final, first, stop)
    count = plan.row_devices * plan.slab
    for block in plan.out_blocks:
        size = block[1] - block[0]
        field[:, block[0] - plan.halo : block[1] - plan.halo] = columns_pass(last, count, plan.window(block))
    for step, out in enumerate(outs):
        row = pl.multiple_of((place[0] ^ step) * plan.slab, 8)
        out[...] = field[pl.ds(row, plan.slab), :]


def divergence(own, partner):
    rows, columns = own.shape
    stop = rows - rim
    inner = slice(lane, columns - lane)
    here = partner[rim:stop]
    down, up = partner[rim + 2 : stop + 2, inner], partner[rim - 2 : stop - 2, inner]
    middle = here[:, inner]
    flow = own[rim + 1 : stop + 1, inner] * (down - middle) - own[rim - 1 : stop - 1, inner] * (middle - up)
    level = own[rim:stop]

    def shifted(value, amount):
        return pltpu.roll(value, amount % columns, 1)[:, inner]

    right = shifted(level, -1) * (shifted(here, -2) - middle)
    left = shifted(level, 1) * (middle - shifted(here, 2))
    return 0.25 * (flow + (right - left))


def estimate_kernel(plan, holders, field_width, place, pair_one, pair_two, owner, *refs):
    refs = list(refs)
    pieces = []
    for orders in holders:
        flat = []
        for order in orders:
            ref = refs.pop(0)
            flat += [(offset, ref.at[slot]) for slot, offset in enumerate(order)]
        pieces.append(sorted(flat, key=lambda entry: entry[0]))
    estimate = refs.pop(0)
    mean_field = refs.pop(0) if field_width else None
    own, partner, sems = refs[:3]
    rows_at, sim_at = place[0], place[1]
    if field_width:
        every = refs[3]
        units = field_width // lane
        per = plan.share // lane
        for unit in range(units + 2):
            at = sim_at * units - 1 + unit
            inside = (at >= 0) & (at < plan.columns // lane)
            span = slice(unit * lane, (unit + 1) * lane)
            for step in range(plan.row_devices):
                def fetch_all(step=step, at=at, span=span, unit=unit):
                    column = pl.multiple_of(lax.rem(at, per) * lane, lane)
                    for offset, source in pieces[step]:
                        pltpu.make_async_copy(
                            source.at[:, pl.ds(column, lane)], every.at[sim_at ^ offset, :, span], sems.at[unit]
                        ).start()

                pl.when(inside & (lax.div(at, per) == (rows_at ^ step)))(fetch_all)

            @pl.when(jnp.logical_not(inside))
            def _(span=span):
                every[:, :, span] = jnp.zeros((plan.sim_devices, plan.slab, lane), jnp.float32)

    edge = jnp.zeros((plan.slab, lane), jnp.float32)
    for target in (own, partner):
        target[:, :lane] = edge
        target[:, lane + plan.columns :] = edge
    one, two = sim_at ^ pair_one[sim_at], sim_at ^ pair_two[sim_at]

    def factor(offset):
        return jnp.where(one == offset, 2.0, 0.0) - jnp.where(two == offset, 1.0, 0.0)

    for step in range(plan.row_devices):
        column = pl.multiple_of(lane + (rows_at ^ step) * plan.share, lane)
        own[:, pl.ds(column, plan.share)] = pieces[step][0][1][...]
        mixed = factor(0) * pieces[step][0][1][...]
        for offset, source in pieces[step][1:]:
            mixed = mixed + factor(offset) * source[...]
        partner[:, pl.ds(column, plan.share)] = mixed
    for a in range(0, plan.columns, stretch):
        b = min(a + stretch, plan.columns)
        span = slice(a, b + 2 * lane)
        estimate[:, a:b] = divergence(own[:, span], partner[:, span])
    if not field_width:
        return
    for unit in range(units + 2):
        at = sim_at * units - 1 + unit

        @pl.when((at >= 0) & (at < plan.columns // lane))
        def _(unit=unit):
            span = every.at[:, :, unit * lane : (unit + 1) * lane]
            pltpu.make_async_copy(span, span, sems.at[unit]).wait()

    mean_field[...] = jnp.zeros(mean_field.shape, jnp.float32)
    for sim in range(plan.sim_devices):
        partner = 2.0 * every[pair_one[sim]] - every[pair_two[sim]]
        mean_field[owner[sim]] += divergence(every[sim], partner)
    for group in range(OWNERS):
        count = jnp.int32(0)
        for sim in range(plan.sim_devices):
            count = count + (owner[sim] == group).astype(jnp.int32)
        mean_field[group] = mean_field[group] / jnp.maximum(count, 1).astype(jnp.float32)


def exchange(value, axis, offset):
    count = lax.axis_size(axis)
    return lax.ppermute(value, axis, [(i, i ^ offset) for i in range(count)])


def gather(first, axis, bits):
    arrays, offsets = [first[None]], [[0]]
    for bit in bits:
        whole = jnp.concatenate(arrays, axis=0) if len(arrays) > 1 else arrays[0]
        arrays.append(exchange(whole, axis, bit))
        offsets.append([offset ^ bit for order in offsets for offset in order])
    return arrays, offsets


def call(kernel, out_shapes, in_specs, scratch, flops, moved, limit=48):
    vmem = pl.BlockSpec(memory_space=pltpu.VMEM)
    return pl.pallas_call(
        kernel,
        out_shape=out_shapes,
        in_specs=in_specs,
        out_specs=[vmem] * len(out_shapes),
        scratch_shapes=scratch,
        compiler_params=pltpu.CompilerParams(vmem_limit_bytes=limit * 1024 * 1024),
        cost_estimate=pl.CostEstimate(flops=flops, bytes_accessed=moved, transcendentals=0),
    )


def body(maps, weight, beam, pair_one, pair_two, owner):
    sim_local, row_local, columns = maps.shape
    taps = beam.shape[0]
    row_devices, sim_devices = lax.axis_size("rows"), lax.axis_size("sims")
    plan = Plan(row_devices, sim_devices, row_local, columns, taps)
    place = jnp.stack([lax.axis_index("rows"), lax.axis_index("sims")]).astype(jnp.int32)
    vmem = pl.BlockSpec(memory_space=pltpu.VMEM)
    smem = pl.BlockSpec(memory_space=pltpu.SMEM)
    far = pl.BlockSpec(memory_space=pltpu.HBM)

    def pinned(value):
        return pltpu.with_memory_space_constraint(value, pltpu.HBM)

    def f32(*shape):
        return jax.ShapeDtypeStruct(shape, jnp.float32)

    def b16(*shape):
        return jax.ShapeDtypeStruct(shape, jnp.bfloat16)

    cells = row_local * columns
    near = plan.share_rows + plan.head
    made = call(
        functools.partial(piece_kernel, plan),
        [f32(near, plan.width)] * row_devices + [f32(row_local - plan.head, plan.width)] * row_devices,
        [smem, far, far],
        [pltpu.VMEM((row_local, columns + 2 * plan.halo), jnp.float32)] * 2
        + [pltpu.VMEM((row_local, columns), jnp.float32), pltpu.SemaphoreType.DMA((2, loads))],
        cells,
        16 * cells,
    )(place, pinned(maps.reshape(row_local, columns)), pinned(weight))
    heads, tails = made[:row_devices], made[row_devices:]
    heads = [heads[0]] + [exchange(heads[d], "rows", d) for d in range(1, row_devices)]
    tails = [tails[0]] + [exchange(tails[d], "rows", d) for d in range(1, row_devices)]
    sharers = []
    shapes = [(plan.rows, plan.rows), (row_devices * plan.slab, plan.rows)]
    for block in plan.blocks + plan.out_blocks[:1]:
        low, high = plan.window(block)
        shapes.append((high - low, block[1] - block[0]))

    def prepare(heads, beam):
        first = jnp.stack([head[: plan.share_rows] for head in heads])[None]
        found = {0: first}
        for bit in [1 << i for i in range(1, plan.sharers.bit_length() - 1)]:
            found |= {offset | bit: exchange(value, "sims", bit) for offset, value in found.items()}
        across = list(found)
        tables = call(
            functools.partial(table_kernel, plan),
            [b16(*shape) for shape in shapes for _ in range(2)],
            [smem, vmem],
            [pltpu.VMEM((8, lane), jnp.float32)],
            1 << 32,
            1 << 23,
        )(place, beam[None])
        sharers[:] = [[offset] for offset in across] + [[offset ^ 1 for offset in across]]
        whole, tables = lax.optimization_barrier((jnp.concatenate(list(found.values())), tables))
        return [*found.values(), exchange(whole, "sims", 1)], tables

    made = jax.eval_shape(prepare, heads, beam)
    parts, tables = lax.cond(
        lax.axis_index("rows") < row_devices,
        prepare,
        lambda heads, beam: jax.tree.map(lambda x: jnp.zeros(x.shape, x.dtype), made),
        heads,
        beam,
    )

    full = (plan.rows, plan.width)
    tall = (max(plan.rows, row_devices * plan.slab), plan.width)
    filtered = call(
        functools.partial(filter_kernel, plan, sharers),
        [f32(plan.slab, plan.share)] * row_devices,
        [smem] + [vmem] * (2 * row_devices + len(parts) + len(tables)),
        [pltpu.VMEM(full, jnp.float32)] * 4
        + [pltpu.VMEM((row_devices * plan.slab, plan.share), jnp.float32)]
        + [pltpu.VMEM(full, jnp.bfloat16)] * 2
        + [pltpu.VMEM(tall, jnp.bfloat16)] * 2,
        1 << 33,
        1 << 23,
    )(place, *heads, *tails, *parts, *tables)

    moved = [filtered[0]] + [exchange(filtered[step], "rows", step) for step in range(1, row_devices)]
    bits = [1 << i for i in range(1, sim_devices.bit_length() - 1)]
    arrays, holders = [], []
    for step in range(row_devices):
        turn = step % max(len(bits), 1)
        found, offsets = gather(moved[step], "sims", bits[turn:] + bits[:turn])
        arrays.append(found)
        holders.append(offsets)
    held = []
    for found, offsets in zip(arrays, holders):
        held += found + [exchange(jnp.concatenate(found), "sims", 1)]
        offsets.append([offset ^ 1 for order in offsets for offset in order])

    field_width = columns // sim_devices
    fused = field_width if field_width % lane == 0 else 0
    outs = [f32(row_local, columns)]
    extended = (plan.slab, columns + 2 * lane)
    scratch = [pltpu.VMEM(extended, jnp.float32)] * 2
    if fused:
        outs.append(f32(OWNERS, row_local, fused))
        scratch.append(pltpu.SemaphoreType.DMA((fused // lane + 2,)))
        scratch.append(pltpu.VMEM((sim_devices, plan.slab, fused + 2 * lane), jnp.float32))
    else:
        scratch.append(pltpu.SemaphoreType.DMA((1,)))
    results = call(
        functools.partial(estimate_kernel, plan, holders, fused),
        outs,
        [smem] * 4 + [vmem] * len(held),
        scratch,
        1 << 24,
        1 << 23,
    )(place, pair_one, pair_two, owner, *held)
    estimate = results[0]
    if fused:
        mean_field = results[1]
    else:
        groups = jnp.arange(OWNERS, dtype=jnp.int32)
        local_owner = owner[place[1]]
        term = jnp.where((groups == local_owner)[:, None, None], estimate[None], 0.0)
        total = lax.psum_scatter(term, "sims", scatter_dimension=2, tiled=True)
        tally = jnp.sum((groups[:, None] == owner[None, :]).astype(jnp.float32), axis=1)
        mean_field = total / jnp.maximum(tally, 1.0)[:, None, None]
    return estimate.reshape(maps.shape), mean_field


def solution(mesh):
    in_specs = (P("sims", "rows", None), P("rows", None), P(), P(), P(), P())
    out_specs = (P("sims", "rows", None), P(None, "rows", "sims"))
    return jax.shard_map(body, mesh=mesh, in_specs=in_specs, out_specs=out_specs, check_vma=False)
```

```python
import functools

import jax
import jax.numpy as jnp
from jax import lax
from jax.experimental import pallas as pl
from jax.experimental.pallas import tpu as pltpu
from jax.sharding import PartitionSpec as P

ITERS = 3
OWNERS = 8

ridge_term = 0.5
step_size = 0.6
exact = lax.Precision.HIGHEST
lane = 128
wide = 256
stretch = 1024
rim = 4
loads = 4
vmem_bytes = 48 * 1024 * 1024


def split(value):
    high = value.astype(jnp.bfloat16)
    low = (value - high.astype(jnp.float32)).astype(jnp.bfloat16)
    return high, low


def dot(a, b):
    return jnp.dot(a, b, preferred_element_type=jnp.float32)


class Plan:
    def __init__(self, row_devices, sim_devices, row_local, columns, taps):
        self.row_devices, self.sim_devices = row_devices, sim_devices
        self.row_local, self.columns = row_local, columns
        self.rows = row_devices * row_local
        self.margin = (taps - 1) // 2
        self.share = columns // row_devices
        self.halo = -(-self.margin * (2 * ITERS + 1) // lane) * lane
        self.width = self.share + 2 * self.halo
        self.slab = row_local + 2 * rim
        self.sharers = min(sim_devices, row_local // 8)
        self.share_rows = row_local // self.sharers
        self.length = max(2 * wide, -(-self.rows // lane) * lane)
        inner = range(lane, self.width - lane, wide)
        blocks = [(0, lane)] + [(a, min(a + wide, self.width - lane)) for a in inner]
        self.blocks = blocks + [(self.width - lane, self.width)]
        centre = range(self.halo, self.halo + self.share, wide)
        self.out_blocks = [(a, min(a + wide, self.halo + self.share)) for a in centre]

    def window(self, block):
        return max(0, block[0] - lane), min(self.width, block[1] + lane)

    def stage_blocks(self, iteration):
        low = self.halo - self.margin * (2 * (ITERS - 1 - iteration) + 1)
        return [i for i, (a, b) in enumerate(self.blocks) if b > low and a < self.width - low]


def share_kernel(plan, place, weight, *refs):
    parts, padded, sem = refs[: plan.row_devices], refs[-2], refs[-1]
    row = pl.multiple_of(lax.rem(place[1], plan.sharers) * plan.share_rows, plan.share_rows)
    source = weight.at[pl.ds(row, plan.share_rows)]
    copy = pltpu.make_async_copy(source, padded.at[:, pl.ds(plan.halo, plan.columns)], sem)
    copy.start()
    zeros = jnp.zeros((plan.share_rows, plan.halo), jnp.float32)
    padded[:, : plan.halo] = zeros
    padded[:, plan.halo + plan.columns :] = zeros
    copy.wait()
    for step, part in enumerate(parts):
        column = pl.multiple_of((place[0] ^ step) * plan.share, lane)
        part[...] = padded[:, pl.ds(column, plan.width)]


def weighted_kernel(plan, place, maps, weight, *refs):
    pieces = refs[: plan.row_devices]
    padded, weights, given, sems = refs[plan.row_devices :]
    chunk = plan.row_local // loads
    copies = []
    for number in range(loads):
        rows = pl.ds(number * chunk, chunk)
        copies.append((
            pltpu.make_async_copy(weight.at[rows], weights.at[rows], sems.at[0, number]),
            pltpu.make_async_copy(maps.at[rows], given.at[rows], sems.at[1, number]),
        ))
        for copy in copies[-1]:
            copy.start()
    zeros = jnp.zeros((plan.row_local, plan.halo), jnp.float32)
    padded[:, : plan.halo] = zeros
    padded[:, plan.halo + plan.columns :] = zeros
    for number in range(loads):
        for copy in copies[number]:
            copy.wait()
        rows = slice(number * chunk, (number + 1) * chunk)
        padded[rows, plan.halo : plan.halo + plan.columns] = weights[rows] * given[rows]
        for step, piece in enumerate(pieces):
            column = pl.multiple_of((place[0] ^ step) * plan.share, lane)
            piece[rows] = padded[rows, pl.ds(column, plan.width)]


def band(plan, taps, rows, columns, offset):
    if offset % plan.length:
        taps = pltpu.roll(taps, offset % plan.length, 1)
    spread = jnp.broadcast_to(taps[:1], (rows, plan.length))
    rolled = pltpu.roll(spread, 0, 1, stride=1, stride_axis=0)[:, :columns]
    row = lax.broadcasted_iota(jnp.int32, (rows, columns), 0)
    column = lax.broadcasted_iota(jnp.int32, (rows, columns), 1)
    return jnp.where(jnp.abs(column - row - offset) <= plan.margin, rolled, 0.0)


def table_kernel(plan, place, beam, *refs):
    refs, line = refs[:-1], refs[-1]
    count = beam.shape[1]
    line[...] = jnp.zeros(line.shape, jnp.float32)
    line[:1, :count] = beam[...]
    kernel = line[...]
    kernel = kernel / jnp.sum(kernel[:1], axis=1, keepdims=True)
    size = kernel.shape[1]
    row = lax.broadcasted_iota(jnp.int32, (size, size), 0)
    column = lax.broadcasted_iota(jnp.int32, (size, size), 1)
    mirror = (row + column == count - 1).astype(jnp.float32)
    blank = jnp.zeros((kernel.shape[0], plan.length - size), jnp.float32)

    def centred(values):
        return pltpu.roll(jnp.concatenate([values, blank], axis=1), plan.length - plan.margin, 1)

    taps, reverse = centred(kernel), centred(jnp.dot(kernel, mirror, precision=exact))
    tables = list(refs)

    def put(value):
        high, low = split(value)
        tables.pop(0)[...] = high
        tables.pop(0)[...] = low

    rows = plan.rows
    put(jnp.dot(band(plan, taps, rows, rows, 0), band(plan, reverse, rows, rows, 0), precision=exact))
    slabs = []
    for device in range(plan.row_devices):
        first = device * plan.row_local - rim
        part = band(plan, reverse, plan.slab, rows, first)
        row = lax.broadcasted_iota(jnp.int32, part.shape, 0) + first
        slabs.append(jnp.where((row >= 0) & (row < rows), part, 0.0))
    put(jnp.concatenate(slabs, axis=0))
    size = 2 * wide
    forward = band(plan, taps, size, size, 0)
    backward = band(plan, reverse, size, size, 0)
    for block in plan.blocks:
        low, high = plan.window(block)
        extent = high - low
        column = lax.broadcasted_iota(jnp.int32, (extent, extent), 1) + (place[0] * plan.share - plan.halo + low)
        inside = (column >= 0) & (column < plan.columns)
        left = jnp.where(inside, forward[:extent, :extent], 0.0)
        right = backward[:extent, block[0] - low : block[1] - low]
        put(step_size * jnp.dot(left, right, precision=exact))
    for block in plan.out_blocks[:1]:
        low, high = plan.window(block)
        put(step_size * forward[: high - low, block[0] - low : block[1] - low])


def filter_kernel(plan, sharers, place, *refs):
    refs = list(refs)

    def take(number):
        taken = refs[:number]
        del refs[:number]
        return taken

    pieces = take(plan.row_devices)
    parts = take(len(sharers))
    square, final = take(2), take(2)
    bands = [take(2) for _ in plan.blocks]
    last = take(2)
    outs = take(plan.row_devices)
    seen, weight, image, base, total, field, high, low, mid_high, mid_low, sem = refs
    for part, owners in zip(parts, sharers):
        for slot, offset in enumerate(owners):
            for step in range(plan.row_devices):
                row = (place[0] ^ step) * plan.row_local
                row = row + (lax.rem(place[1], plan.sharers) ^ offset) * plan.share_rows
                rows = pl.ds(pl.multiple_of(row, plan.share_rows), plan.share_rows)
                pltpu.make_async_copy(part.at[slot, step], weight.at[rows], sem).start()
    for step, piece in enumerate(pieces):
        rows = pl.ds(pl.multiple_of((place[0] ^ step) * plan.row_local, plan.row_local), plan.row_local)
        value = piece[...]
        seen[rows, :] = value
        high[rows, :], low[rows, :] = split(value)
    def rows_pass(table, start, stop, full=True):
        count = table[0].shape[0]
        for a in range(start, stop, wide):
            b = min(a + wide, stop)
            value = dot(table[0][...], high[:, a:b]) + dot(table[1][...], high[:, a:b])
            if full:
                value = value + dot(table[0][...], low[:, a:b])
                mid_high[:count, a:b], mid_low[:count, a:b] = split(value)
            else:
                mid_high[:count, a:b] = value.astype(jnp.bfloat16)

    def columns_pass(table, count, window, full=True):
        a, b = window
        value = dot(mid_high[:count, a:b], table[0][...]) + dot(mid_high[:count, a:b], table[1][...])
        return value + dot(mid_low[:count, a:b], table[0][...]) if full else value

    keep = 1.0 - step_size * ridge_term
    for iteration in range(ITERS):
        chosen = plan.stage_blocks(iteration)
        windows = [plan.window(plan.blocks[i]) for i in chosen]
        rows_pass(square, windows[0][0], windows[-1][1], iteration == 0)
        if iteration == 0:
            pltpu.make_async_copy(weight, weight, sem).wait()
        for i, window in zip(chosen, windows):
            a, b = plan.blocks[i]
            value = columns_pass(bands[i], plan.rows, window, iteration == 0)
            if iteration == 0:
                base[:, a:b] = value
            else:
                value = keep * image[:, a:b] + base[:, a:b] - value
            image[:, a:b] = value
            product = weight[:, a:b] * value
            given = seen[:, a:b]
            total[:, a:b] = given - product + keep * (total[:, a:b] if iteration > 0 else given)
            high[:, a:b] = product.astype(jnp.bfloat16)
    first, stop = plan.window(plan.out_blocks[0])[0], plan.window(plan.out_blocks[-1])[1]
    high[:, first:stop], low[:, first:stop] = split(total[:, first:stop])
    rows_pass(final, first, stop)
    count = plan.row_devices * plan.slab
    for block in plan.out_blocks:
        size = block[1] - block[0]
        field[:, block[0] - plan.halo : block[1] - plan.halo] = columns_pass(last, count, plan.window(block))
    for step, out in enumerate(outs):
        row = pl.multiple_of((place[0] ^ step) * plan.slab, 8)
        out[...] = field[pl.ds(row, plan.slab), :]


def divergence(own, partner):
    rows, columns = own.shape
    stop = rows - rim
    inner = slice(lane, columns - lane)
    here = partner[rim:stop]
    down, up = partner[rim + 2 : stop + 2, inner], partner[rim - 2 : stop - 2, inner]
    middle = here[:, inner]
    flow = own[rim + 1 : stop + 1, inner] * (down - middle) - own[rim - 1 : stop - 1, inner] * (middle - up)
    level = own[rim:stop]

    def shifted(value, amount):
        return pltpu.roll(value, amount % columns, 1)[:, inner]

    right = shifted(level, -1) * (shifted(here, -2) - middle)
    left = shifted(level, 1) * (middle - shifted(here, 2))
    return 0.25 * (flow + (right - left))


def estimate_kernel(plan, holders, field_width, place, pair_one, pair_two, owner, *refs):
    refs = list(refs)
    pieces = []
    for orders in holders:
        flat = []
        for order in orders:
            ref = refs.pop(0)
            flat += [(offset, ref.at[slot]) for slot, offset in enumerate(order)]
        pieces.append(sorted(flat, key=lambda entry: entry[0]))
    estimate = refs.pop(0)
    mean_field = refs.pop(0) if field_width else None
    own, partner, result, done, sems = refs[:5]
    rows_at, sim_at = place[0], place[1]
    if field_width:
        every, means, sent = refs[5:]
        units = field_width // lane
        per = plan.share // lane
        for unit in range(units + 2):
            at = sim_at * units - 1 + unit
            inside = (at >= 0) & (at < plan.columns // lane)
            span = slice(unit * lane, (unit + 1) * lane)
            for step in range(plan.row_devices):
                def fetch_all(step=step, at=at, span=span, unit=unit):
                    column = pl.multiple_of(lax.rem(at, per) * lane, lane)
                    for offset, source in pieces[step]:
                        pltpu.make_async_copy(
                            source.at[:, pl.ds(column, lane)], every.at[sim_at ^ offset, :, span], sems.at[unit]
                        ).start()

                pl.when(inside & (lax.div(at, per) == (rows_at ^ step)))(fetch_all)

            @pl.when(jnp.logical_not(inside))
            def _(span=span):
                every[:, :, span] = jnp.zeros((plan.sim_devices, plan.slab, lane), jnp.float32)

    edge = jnp.zeros((plan.slab, lane), jnp.float32)
    for target in (own, partner):
        target[:, :lane] = edge
        target[:, lane + plan.columns :] = edge
    one, two = sim_at ^ pair_one[sim_at], sim_at ^ pair_two[sim_at]

    def factor(offset):
        return jnp.where(one == offset, 2.0, 0.0) - jnp.where(two == offset, 1.0, 0.0)

    for step in range(plan.row_devices):
        column = pl.multiple_of(lane + (rows_at ^ step) * plan.share, lane)
        own[:, pl.ds(column, plan.share)] = pieces[step][0][1][...]
        mixed = factor(0) * pieces[step][0][1][...]
        for offset, source in pieces[step][1:]:
            mixed = mixed + factor(offset) * source[...]
        partner[:, pl.ds(column, plan.share)] = mixed
    for a in range(0, plan.columns, stretch):
        b = min(a + stretch, plan.columns)
        span = slice(a, b + 2 * lane)
        result[:, a:b] = divergence(own[:, span], partner[:, span])
    copies = [pltpu.make_async_copy(result, estimate, done)]
    copies[0].start()
    if not field_width:
        copies[0].wait()
        return
    for unit in range(units + 2):
        at = sim_at * units - 1 + unit

        @pl.when((at >= 0) & (at < plan.columns // lane))
        def _(unit=unit):
            span = every.at[:, :, unit * lane : (unit + 1) * lane]
            pltpu.make_async_copy(span, span, sems.at[unit]).wait()

    means[...] = jnp.zeros(means.shape, jnp.float32)
    for sim in range(plan.sim_devices):
        means[owner[sim]] += divergence(every[sim], 2.0 * every[pair_one[sim]] - every[pair_two[sim]])
    for group in range(OWNERS):
        count = jnp.int32(0)
        for sim in range(plan.sim_devices):
            count = count + (owner[sim] == group).astype(jnp.int32)
        means[group] = means[group] / jnp.maximum(count, 1).astype(jnp.float32)
        copies.append(pltpu.make_async_copy(means.at[group], mean_field.at[group], sent.at[group]))
        copies[-1].start()
    for copy in copies:
        copy.wait()


def exchange(value, axis, offset):
    count = lax.axis_size(axis)
    return lax.ppermute(value, axis, [(i, i ^ offset) for i in range(count)])


def gather(first, axis, bits):
    arrays, offsets = [first[None]], [[0]]
    for bit in bits:
        whole = jnp.concatenate(arrays, axis=0) if len(arrays) > 1 else arrays[0]
        arrays.append(exchange(whole, axis, bit))
        offsets.append([offset ^ bit for order in offsets for offset in order])
    return arrays, offsets


def call(kernel, out_shapes, in_specs, scratch, flops, moved, outs_in=pltpu.VMEM):
    return pl.pallas_call(
        kernel,
        out_shape=out_shapes,
        in_specs=in_specs,
        out_specs=[pl.BlockSpec(memory_space=outs_in)] * len(out_shapes),
        scratch_shapes=scratch,
        compiler_params=pltpu.CompilerParams(vmem_limit_bytes=vmem_bytes),
        cost_estimate=pl.CostEstimate(flops=flops, bytes_accessed=moved, transcendentals=0),
    )


def body(maps, weight, beam, pair_one, pair_two, owner):
    sim_local, row_local, columns = maps.shape
    taps = beam.shape[0]
    row_devices, sim_devices = lax.axis_size("rows"), lax.axis_size("sims")
    plan = Plan(row_devices, sim_devices, row_local, columns, taps)
    place = jnp.stack([lax.axis_index("rows"), lax.axis_index("sims")]).astype(jnp.int32)
    vmem = pl.BlockSpec(memory_space=pltpu.VMEM)
    smem = pl.BlockSpec(memory_space=pltpu.SMEM)
    far = pl.BlockSpec(memory_space=pltpu.HBM)

    def pinned(value):
        return pltpu.with_memory_space_constraint(value, pltpu.HBM)

    def f32(*shape):
        return jax.ShapeDtypeStruct(shape, jnp.float32)

    def b16(*shape):
        return jax.ShapeDtypeStruct(shape, jnp.bfloat16)

    cells = row_local * columns
    parts = call(
        functools.partial(share_kernel, plan),
        [f32(plan.share_rows, plan.width)] * row_devices,
        [smem, far],
        [pltpu.VMEM((plan.share_rows, columns + 2 * plan.halo), jnp.float32), pltpu.SemaphoreType.DMA],
        0,
        1 << 18,
    )(place, pinned(weight))
    pieces = call(
        functools.partial(weighted_kernel, plan),
        [f32(row_local, plan.width)] * row_devices,
        [smem, far, far],
        [pltpu.VMEM((row_local, columns + 2 * plan.halo), jnp.float32)]
        + [pltpu.VMEM((row_local, columns), jnp.float32)] * 2
        + [pltpu.SemaphoreType.DMA((2, loads))],
        cells,
        16 * cells,
    )(place, pinned(maps.reshape(row_local, columns)), pinned(weight))
    parts = [parts[0]] + [exchange(parts[d], "rows", d) for d in range(1, row_devices)]
    pieces, parts = lax.optimization_barrier((pieces, parts))
    pieces = [pieces[0]] + [exchange(pieces[d], "rows", d) for d in range(1, row_devices)]
    sharers = []
    shapes = [(plan.rows, plan.rows), (row_devices * plan.slab, plan.rows)]
    for block in plan.blocks + plan.out_blocks[:1]:
        low, high = plan.window(block)
        shapes.append((high - low, block[1] - block[0]))

    tables = call(
        functools.partial(table_kernel, plan),
        [b16(*shape) for shape in shapes for _ in range(2)],
        [smem, vmem],
        [pltpu.VMEM((8, lane), jnp.float32)],
        1 << 32,
        1 << 23,
    )(place, beam[None])
    parts, tables = lax.optimization_barrier((parts, tables))

    def spread(parts):
        found = {0: jnp.stack(parts)[None]}
        for bit in [1 << i for i in range(1, plan.sharers.bit_length() - 1)]:
            found |= {offset | bit: exchange(value, "sims", bit) for offset, value in found.items()}
        sharers[:] = [[offset] for offset in found] + [[offset ^ 1 for offset in found]]
        return [*found.values(), exchange(jnp.concatenate(list(found.values())), "sims", 1)]

    made = jax.eval_shape(spread, parts)
    parts = lax.cond(
        lax.axis_index("rows") < row_devices,
        spread,
        lambda parts: jax.tree.map(lambda x: jnp.zeros(x.shape, x.dtype), made),
        parts,
    )

    full = (plan.rows, plan.width)
    tall = (max(plan.rows, row_devices * plan.slab), plan.width)
    filtered = call(
        functools.partial(filter_kernel, plan, sharers),
        [f32(plan.slab, plan.share)] * row_devices,
        [smem] + [vmem] * row_devices + [far] * len(parts) + [vmem] * len(tables),
        [pltpu.VMEM(full, jnp.float32)] * 5
        + [pltpu.VMEM((row_devices * plan.slab, plan.share), jnp.float32)]
        + [pltpu.VMEM(full, jnp.bfloat16)] * 2
        + [pltpu.VMEM(tall, jnp.bfloat16)] * 2
        + [pltpu.SemaphoreType.DMA],
        1 << 33,
        1 << 23,
    )(place, *pieces, *parts, *tables)

    moved = [filtered[0]] + [exchange(filtered[step], "rows", step) for step in range(1, row_devices)]
    bits = [1 << i for i in range(1, sim_devices.bit_length() - 1)]
    arrays, holders = [], []
    for step in range(row_devices):
        turn = step % max(len(bits), 1)
        found, offsets = gather(moved[step], "sims", bits[turn:] + bits[:turn])
        arrays.append(found)
        holders.append(offsets)
    held = []
    for found, offsets in zip(arrays, holders):
        held += found + [exchange(jnp.concatenate(found), "sims", 1)]
        offsets.append([offset ^ 1 for order in offsets for offset in order])

    field_width = columns // sim_devices
    fused = field_width if field_width % lane == 0 else 0
    outs = [f32(row_local, columns)]
    extended = (plan.slab, columns + 2 * lane)
    scratch = [pltpu.VMEM(extended, jnp.float32)] * 2
    scratch += [pltpu.VMEM((row_local, columns), jnp.float32), pltpu.SemaphoreType.DMA]
    if fused:
        outs.append(f32(OWNERS, row_local, fused))
        scratch.append(pltpu.SemaphoreType.DMA((fused // lane + 2,)))
        scratch.append(pltpu.VMEM((sim_devices, plan.slab, fused + 2 * lane), jnp.float32))
        scratch.append(pltpu.VMEM((OWNERS, row_local, fused), jnp.float32))
        scratch.append(pltpu.SemaphoreType.DMA((OWNERS,)))
    else:
        scratch.append(pltpu.SemaphoreType.DMA((1,)))
    results = call(
        functools.partial(estimate_kernel, plan, holders, fused),
        outs,
        [smem] * 4 + [vmem] * len(held),
        scratch,
        1 << 24,
        1 << 23,
        outs_in=pltpu.HBM,
    )(place, pair_one, pair_two, owner, *held)
    estimate = results[0]
    if fused:
        mean_field = results[1]
    else:
        groups = jnp.arange(OWNERS, dtype=jnp.int32)
        local_owner = owner[place[1]]
        term = jnp.where((groups == local_owner)[:, None, None], estimate[None], 0.0)
        total = lax.psum_scatter(term, "sims", scatter_dimension=2, tiled=True)
        tally = jnp.sum((groups[:, None] == owner[None, :]).astype(jnp.float32), axis=1)
        mean_field = total / jnp.maximum(tally, 1.0)[:, None, None]
    return estimate.reshape(maps.shape), mean_field


def solution(mesh):
    in_specs = (P("sims", "rows", None), P("rows", None), P(), P(), P(), P())
    out_specs = (P("sims", "rows", None), P(None, "rows", "sims"))
    return jax.shard_map(body, mesh=mesh, in_specs=in_specs, out_specs=out_specs, check_vma=False)
```

```python
import functools

import jax
import jax.numpy as jnp
from jax import lax
from jax.experimental import pallas as pl
from jax.experimental.pallas import tpu as pltpu
from jax.sharding import PartitionSpec as P

ITERS = 3
OWNERS = 8

ridge_term = 0.5
step_size = 0.6
exact = lax.Precision.HIGHEST
lane = 128
wide = 256
stretch = 1024
rim = 4
loads = 4
vmem_bytes = 48 * 1024 * 1024


def split(value):
    high = value.astype(jnp.bfloat16)
    low = (value - high.astype(jnp.float32)).astype(jnp.bfloat16)
    return high, low


def dot(a, b):
    return jnp.dot(a, b, preferred_element_type=jnp.float32)


class Plan:
    def __init__(self, row_devices, sim_devices, row_local, columns, taps):
        self.row_devices, self.sim_devices = row_devices, sim_devices
        self.row_local, self.columns = row_local, columns
        self.rows = row_devices * row_local
        self.steps = [0, *range(row_devices - 1, 0, -1)]
        self.margin = (taps - 1) // 2
        self.share = columns // row_devices
        self.halo = -(-self.margin * (2 * ITERS + 1) // lane) * lane
        self.width = self.share + 2 * self.halo
        self.slab = row_local + 2 * rim
        self.sharers = min(sim_devices, row_local // 8)
        self.share_rows = row_local // self.sharers
        self.length = max(2 * wide, -(-self.rows // lane) * lane)
        inner = range(lane, self.width - lane, wide)
        blocks = [(0, lane)] + [(a, min(a + wide, self.width - lane)) for a in inner]
        self.blocks = blocks + [(self.width - lane, self.width)]
        centre = range(self.halo, self.halo + self.share, wide)
        self.out_blocks = [(a, min(a + wide, self.halo + self.share)) for a in centre]

    def window(self, block):
        return max(0, block[0] - lane), min(self.width, block[1] + lane)

    def stage_blocks(self, iteration):
        low = self.halo - self.margin * (2 * (ITERS - 1 - iteration) + 1)
        return [i for i, (a, b) in enumerate(self.blocks) if b > low and a < self.width - low]


def piece_kernel(plan, maps, weight, *refs):
    count = plan.row_devices
    pieces, parts = refs[:count], refs[count : 2 * count]
    padded, weights, given, sems = refs[2 * count :]
    rows_at, sims_at = lax.axis_index("rows"), lax.axis_index("sims")
    chunk = plan.row_local // loads
    inner = slice(plan.halo, plan.halo + plan.columns)
    copies = []
    for number in range(loads):
        rows = pl.ds(number * chunk, chunk)
        copies.append((
            pltpu.make_async_copy(weight.at[rows], weights.at[rows, inner], sems.at[0, number]),
            pltpu.make_async_copy(maps.at[rows], given.at[rows], sems.at[1, number]),
        ))
        for copy in copies[-1]:
            copy.start()
    zeros = jnp.zeros((plan.row_local, plan.halo), jnp.float32)
    for target in (padded, weights):
        target[:, : plan.halo] = zeros
        target[:, plan.halo + plan.columns :] = zeros
    starts = [pl.multiple_of((rows_at ^ step) * plan.share, lane) for step in plan.steps]
    for number in range(loads):
        for copy in copies[number]:
            copy.wait()
        rows = slice(number * chunk, (number + 1) * chunk)
        padded[rows, inner] = weights[rows, inner] * given[rows]
        for piece, column in zip(pieces, starts):
            piece[rows] = padded[rows, pl.ds(column, plan.width)]
    row = pl.multiple_of(lax.rem(sims_at, plan.sharers) * plan.share_rows, plan.share_rows)
    for part, column in zip(parts, starts):
        part[...] = weights[pl.ds(row, plan.share_rows), pl.ds(column, plan.width)]


def band(plan, taps, rows, columns, offset):
    if offset % plan.length:
        taps = pltpu.roll(taps, offset % plan.length, 1)
    spread = jnp.broadcast_to(taps[:1], (rows, plan.length))
    rolled = pltpu.roll(spread, 0, 1, stride=1, stride_axis=0)[:, :columns]
    row = lax.broadcasted_iota(jnp.int32, (rows, columns), 0)
    column = lax.broadcasted_iota(jnp.int32, (rows, columns), 1)
    return jnp.where(jnp.abs(column - row - offset) <= plan.margin, rolled, 0.0)


def table_kernel(plan, beam, *refs):
    refs, line = refs[:-1], refs[-1]
    count = beam.shape[1]
    line[...] = jnp.zeros(line.shape, jnp.float32)
    line[:1, :count] = beam[...]
    kernel = line[...]
    kernel = kernel / jnp.sum(kernel[:1], axis=1, keepdims=True)
    size = kernel.shape[1]
    row = lax.broadcasted_iota(jnp.int32, (size, size), 0)
    column = lax.broadcasted_iota(jnp.int32, (size, size), 1)
    mirror = (row + column == count - 1).astype(jnp.float32)
    blank = jnp.zeros((kernel.shape[0], plan.length - size), jnp.float32)

    def centred(values):
        return pltpu.roll(jnp.concatenate([values, blank], axis=1), plan.length - plan.margin, 1)

    taps, reverse = centred(kernel), centred(jnp.dot(kernel, mirror, precision=exact))
    tables = list(refs)

    def put(value):
        high, low = split(value)
        tables.pop(0)[...] = high
        tables.pop(0)[...] = low

    rows = plan.rows
    put(jnp.dot(band(plan, taps, rows, rows, 0), band(plan, reverse, rows, rows, 0), precision=exact))
    slabs = []
    for device in range(plan.row_devices):
        first = device * plan.row_local - rim
        part = band(plan, reverse, plan.slab, rows, first)
        row = lax.broadcasted_iota(jnp.int32, part.shape, 0) + first
        slabs.append(jnp.where((row >= 0) & (row < rows), part, 0.0))
    put(jnp.concatenate(slabs, axis=0))
    size = 2 * wide
    forward = band(plan, taps, size, size, 0)
    backward = band(plan, reverse, size, size, 0)[:, lane : lane + wide]
    square = step_size * jnp.dot(forward, backward, precision=exact)
    for block in plan.blocks:
        low, high = plan.window(block)
        first = low - block[0] + lane
        wanted = square[first : first + high - low, : block[1] - block[0]]
        high_term, low_term = tables[0], tables[1]
        put(wanted)
        origin = lax.axis_index("rows") * plan.share - plan.halo + low
        reach = origin + high - low
        cut = ((origin < 0) & (reach > 0)) | ((origin < plan.columns) & (reach > plan.columns))

        @pl.when(cut)
        def _(origin=origin, extent=high - low, first=first, span=block[1] - block[0], terms=(high_term, low_term)):
            column = lax.broadcasted_iota(jnp.int32, (size, size), 1) + (origin - first)
            inside = (column >= 0) & (column < plan.columns)
            value = step_size * jnp.dot(jnp.where(inside, forward, 0.0), backward, precision=exact)
            high_part, low_part = split(value[first : first + extent, :span])
            terms[0][...] = high_part
            terms[1][...] = low_part

    for block in plan.out_blocks[:1]:
        low, high = plan.window(block)
        put(step_size * forward[: high - low, block[0] - low : block[1] - low])


def filter_kernel(plan, sharers, *refs):
    refs = list(refs)

    def take(number):
        taken = refs[:number]
        del refs[:number]
        return taken

    pieces = take(plan.row_devices)
    parts = take(len(sharers))
    square, final = take(2), take(2)
    bands = [take(2) for _ in plan.blocks]
    last = take(2)
    outs = take(plan.row_devices)
    seen, weight, image, base, total, field, high, low, mid_high, mid_low, sem = refs
    for part, owners in zip(parts, sharers):
        for slot, offset in enumerate(owners):
            for index, step in enumerate(plan.steps):
                row = (lax.axis_index("rows") ^ step) * plan.row_local
                row = row + (lax.rem(lax.axis_index("sims"), plan.sharers) ^ offset) * plan.share_rows
                rows = pl.ds(pl.multiple_of(row, plan.share_rows), plan.share_rows)
                pltpu.make_async_copy(part.at[slot, index], weight.at[rows], sem).start()
    for step, piece in zip(plan.steps, pieces):
        rows = pl.ds(pl.multiple_of((lax.axis_index("rows") ^ step) * plan.row_local, plan.row_local), plan.row_local)
        value = piece[...]
        seen[rows, :] = value
        high[rows, :], low[rows, :] = split(value)
    def rows_pass(table, start, stop, full=True):
        count = table[0].shape[0]
        for a in range(start, stop, wide):
            b = min(a + wide, stop)
            value = dot(table[0][...], high[:, a:b]) + dot(table[1][...], high[:, a:b])
            if full:
                value = value + dot(table[0][...], low[:, a:b])
                mid_high[:count, a:b], mid_low[:count, a:b] = split(value)
            else:
                mid_high[:count, a:b] = value.astype(jnp.bfloat16)

    def columns_pass(table, count, window, full=True):
        a, b = window
        value = dot(mid_high[:count, a:b], table[0][...]) + dot(mid_high[:count, a:b], table[1][...])
        return value + dot(mid_low[:count, a:b], table[0][...]) if full else value

    keep = 1.0 - step_size * ridge_term
    for iteration in range(ITERS):
        chosen = plan.stage_blocks(iteration)
        windows = [plan.window(plan.blocks[i]) for i in chosen]
        rows_pass(square, windows[0][0], windows[-1][1], iteration == 0)
        if iteration == 0:
            for i, window in zip(chosen, windows):
                base[:, slice(*plan.blocks[i])] = columns_pass(bands[i], plan.rows, window)
            pltpu.make_async_copy(weight, weight, sem).wait()
        for i, window in zip(chosen, windows):
            a, b = plan.blocks[i]
            value = base[:, a:b]
            if iteration > 0:
                value = keep * image[:, a:b] + value - columns_pass(bands[i], plan.rows, window, False)
            image[:, a:b] = value
            product = weight[:, a:b] * value
            given = seen[:, a:b]
            total[:, a:b] = given - product + keep * (total[:, a:b] if iteration > 0 else given)
            high[:, a:b] = product.astype(jnp.bfloat16)
    first, stop = plan.window(plan.out_blocks[0])[0], plan.window(plan.out_blocks[-1])[1]
    high[:, first:stop], low[:, first:stop] = split(total[:, first:stop])
    rows_pass(final, first, stop)
    count = plan.row_devices * plan.slab
    for block in plan.out_blocks:
        size = block[1] - block[0]
        field[:, block[0] - plan.halo : block[1] - plan.halo] = columns_pass(last, count, plan.window(block))
    for step, out in zip(plan.steps, outs):
        row = pl.multiple_of((lax.axis_index("rows") ^ step) * plan.slab, 8)
        out[...] = field[pl.ds(row, plan.slab), :]


def divergence(own, partner):
    rows, columns = own.shape
    stop = rows - rim
    inner = slice(lane, columns - lane)
    here = partner[rim:stop]
    down, up = partner[rim + 2 : stop + 2, inner], partner[rim - 2 : stop - 2, inner]
    middle = here[:, inner]
    flow = own[rim + 1 : stop + 1, inner] * (down - middle) - own[rim - 1 : stop - 1, inner] * (middle - up)
    level = own[rim:stop]

    def shifted(value, amount):
        return pltpu.roll(value, amount % columns, 1)[:, inner]

    right = shifted(level, -1) * (shifted(here, -2) - middle)
    left = shifted(level, 1) * (middle - shifted(here, 2))
    return 0.25 * (flow + (right - left))


def estimate_kernel(plan, holders, field_width, pair_one, pair_two, owner, *refs):
    refs = list(refs)
    pieces = []
    for orders in holders:
        flat = []
        for order in orders:
            ref = refs.pop(0)
            flat += [(offset, ref.at[slot]) for slot, offset in enumerate(order)]
        pieces.append(sorted(flat, key=lambda entry: entry[0]))
    estimate = refs.pop(0)
    mean_field = refs.pop(0) if field_width else None
    own, partner, result, done, sems = refs[:5]
    rows_at, sim_at = lax.axis_index("rows"), lax.axis_index("sims")
    if field_width:
        every, means, sent = refs[5:]
        units = field_width // lane
        per = plan.share // lane
        for unit in range(units + 2):
            at = sim_at * units - 1 + unit
            inside = (at >= 0) & (at < plan.columns // lane)
            span = slice(unit * lane, (unit + 1) * lane)
            for step, sources in zip(plan.steps, pieces):
                def fetch_all(sources=sources, at=at, span=span, unit=unit):
                    column = pl.multiple_of(lax.rem(at, per) * lane, lane)
                    for offset, source in sources:
                        pltpu.make_async_copy(
                            source.at[:, pl.ds(column, lane)], every.at[sim_at ^ offset, :, span], sems.at[unit]
                        ).start()

                pl.when(inside & (lax.div(at, per) == (rows_at ^ step)))(fetch_all)

            @pl.when(jnp.logical_not(inside))
            def _(span=span):
                every[:, :, span] = jnp.zeros((plan.sim_devices, plan.slab, lane), jnp.float32)

    edge = jnp.zeros((plan.slab, lane), jnp.float32)
    for target in (own, partner):
        target[:, :lane] = edge
        target[:, lane + plan.columns :] = edge
    one, two = sim_at ^ pair_one[sim_at], sim_at ^ pair_two[sim_at]

    def factor(offset):
        return jnp.where(one == offset, 2.0, 0.0) - jnp.where(two == offset, 1.0, 0.0)

    for step, sources in zip(plan.steps, pieces):
        column = pl.multiple_of(lane + (rows_at ^ step) * plan.share, lane)
        own[:, pl.ds(column, plan.share)] = sources[0][1][...]
        mixed = factor(0) * sources[0][1][...]
        for offset, source in sources[1:]:
            mixed = mixed + factor(offset) * source[...]
        partner[:, pl.ds(column, plan.share)] = mixed
    for a in range(0, plan.columns, stretch):
        b = min(a + stretch, plan.columns)
        span = slice(a, b + 2 * lane)
        result[:, a:b] = divergence(own[:, span], partner[:, span])
    copies = [pltpu.make_async_copy(result, estimate, done)]
    copies[0].start()
    if not field_width:
        copies[0].wait()
        return
    for unit in range(units + 2):
        at = sim_at * units - 1 + unit

        @pl.when((at >= 0) & (at < plan.columns // lane))
        def _(unit=unit):
            span = every.at[:, :, unit * lane : (unit + 1) * lane]
            pltpu.make_async_copy(span, span, sems.at[unit]).wait()

    means[...] = jnp.zeros(means.shape, jnp.float32)
    for sim in range(plan.sim_devices):
        means[owner[sim]] += divergence(every[sim], 2.0 * every[pair_one[sim]] - every[pair_two[sim]])
    for group in range(OWNERS):
        count = jnp.int32(0)
        for sim in range(plan.sim_devices):
            count = count + (owner[sim] == group).astype(jnp.int32)
        means[group] = means[group] / jnp.maximum(count, 1).astype(jnp.float32)
        copies.append(pltpu.make_async_copy(means.at[group], mean_field.at[group], sent.at[group]))
        copies[-1].start()
    for copy in copies:
        copy.wait()


def exchange(value, axis, offset):
    count = lax.axis_size(axis)
    return lax.ppermute(value, axis, [(i, i ^ offset) for i in range(count)])


def exchange_all(plan, values):
    return [exchange(value, "rows", step) if step else value for step, value in zip(plan.steps, values)]


def gather(first, axis, bits):
    arrays, offsets = [first[None]], [[0]]
    for bit in bits:
        whole = jnp.concatenate(arrays, axis=0) if len(arrays) > 1 else arrays[0]
        arrays.append(exchange(whole, axis, bit))
        offsets.append([offset ^ bit for order in offsets for offset in order])
    return arrays, offsets


def call(kernel, out_shapes, in_specs, scratch, flops, moved, outs_in=pltpu.VMEM):
    return pl.pallas_call(
        kernel,
        out_shape=out_shapes,
        in_specs=in_specs,
        out_specs=[pl.BlockSpec(memory_space=outs_in)] * len(out_shapes),
        scratch_shapes=scratch,
        compiler_params=pltpu.CompilerParams(vmem_limit_bytes=vmem_bytes),
        cost_estimate=pl.CostEstimate(flops=flops, bytes_accessed=moved, transcendentals=0),
    )


def run_filter(plan, sharers, pieces, parts, tables):
    vmem = pl.BlockSpec(memory_space=pltpu.VMEM)
    far = pl.BlockSpec(memory_space=pltpu.HBM)
    full = (plan.rows, plan.width)
    tall = (max(plan.rows, plan.row_devices * plan.slab), plan.width)
    return call(
        functools.partial(filter_kernel, plan, sharers),
        [jax.ShapeDtypeStruct((plan.slab, plan.share), jnp.float32)] * plan.row_devices,
        [vmem] * plan.row_devices + [far] * len(parts) + [vmem] * len(tables),
        [pltpu.VMEM(full, jnp.float32)] * 5
        + [pltpu.VMEM((plan.row_devices * plan.slab, plan.share), jnp.float32)]
        + [pltpu.VMEM(full, jnp.bfloat16)] * 2
        + [pltpu.VMEM(tall, jnp.bfloat16)] * 2
        + [pltpu.SemaphoreType.DMA],
        1 << 33,
        1 << 23,
    )(*pieces, *parts, *tables)


def run_estimate(plan, holders, pair_one, pair_two, owner, held):
    vmem = pl.BlockSpec(memory_space=pltpu.VMEM)
    smem = pl.BlockSpec(memory_space=pltpu.SMEM)

    def f32(*shape):
        return jax.ShapeDtypeStruct(shape, jnp.float32)

    field_width = plan.columns // plan.sim_devices
    fused = field_width if field_width % lane == 0 else 0
    outs = [f32(plan.row_local, plan.columns)]
    extended = (plan.slab, plan.columns + 2 * lane)
    scratch = [pltpu.VMEM(extended, jnp.float32)] * 2
    scratch += [pltpu.VMEM((plan.row_local, plan.columns), jnp.float32), pltpu.SemaphoreType.DMA]
    if fused:
        outs.append(f32(OWNERS, plan.row_local, fused))
        scratch.append(pltpu.SemaphoreType.DMA((fused // lane + 2,)))
        scratch.append(pltpu.VMEM((plan.sim_devices, plan.slab, fused + 2 * lane), jnp.float32))
        scratch.append(pltpu.VMEM((OWNERS, plan.row_local, fused), jnp.float32))
        scratch.append(pltpu.SemaphoreType.DMA((OWNERS,)))
    else:
        scratch.append(pltpu.SemaphoreType.DMA((1,)))
    results = call(
        functools.partial(estimate_kernel, plan, holders, fused),
        outs,
        [smem] * 3 + [vmem] * len(held),
        scratch,
        1 << 24,
        1 << 23,
        outs_in=pltpu.HBM,
    )(pair_one, pair_two, owner, *held)
    return results, fused


def body(maps, weight, beam, pair_one, pair_two, owner):
    sim_local, row_local, columns = maps.shape
    taps = beam.shape[0]
    row_devices, sim_devices = lax.axis_size("rows"), lax.axis_size("sims")
    plan = Plan(row_devices, sim_devices, row_local, columns, taps)
    vmem = pl.BlockSpec(memory_space=pltpu.VMEM)
    smem = pl.BlockSpec(memory_space=pltpu.SMEM)
    far = pl.BlockSpec(memory_space=pltpu.HBM)

    def pinned(value):
        return pltpu.with_memory_space_constraint(value, pltpu.HBM)

    def f32(*shape):
        return jax.ShapeDtypeStruct(shape, jnp.float32)

    def b16(*shape):
        return jax.ShapeDtypeStruct(shape, jnp.bfloat16)

    cells = row_local * columns
    made = call(
        functools.partial(piece_kernel, plan),
        [f32(row_local, plan.width)] * row_devices + [f32(plan.share_rows, plan.width)] * row_devices,
        [far, far],
        [pltpu.VMEM((row_local, columns + 2 * plan.halo), jnp.float32)] * 2
        + [pltpu.VMEM((row_local, columns), jnp.float32), pltpu.SemaphoreType.DMA((2, loads))],
        cells,
        16 * cells,
    )(pinned(maps.reshape(row_local, columns)), pinned(weight))
    pieces, parts = made[:row_devices], made[row_devices:]
    parts = exchange_all(plan, parts)
    pieces, parts = lax.optimization_barrier((pieces, parts))
    pieces = exchange_all(plan, pieces)
    shapes = [(plan.rows, plan.rows), (row_devices * plan.slab, plan.rows)]
    for block in plan.blocks + plan.out_blocks[:1]:
        low, high = plan.window(block)
        shapes.append((high - low, block[1] - block[0]))


    def spread(parts):
        found = {0: jnp.stack(parts)[None]}
        for bit in [1 << i for i in range(1, plan.sharers.bit_length() - 1)]:
            found |= {offset | bit: exchange(value, "sims", bit) for offset, value in found.items()}
        sharers[:] = [[offset] for offset in found] + [[offset ^ 1 for offset in found]]
        return [*found.values(), exchange(jnp.concatenate(list(found.values())), "sims", 1)]

    sharers = []
    made = jax.eval_shape(spread, parts)
    parts = lax.cond(
        lax.axis_index("rows") < row_devices,
        spread,
        lambda parts: jax.tree.map(lambda x: jnp.zeros(x.shape, x.dtype), made),
        parts,
    )
    beam, parts = lax.optimization_barrier((beam, parts))
    tables = call(
        functools.partial(table_kernel, plan),
        [b16(*shape) for shape in shapes for _ in range(2)],
        [vmem],
        [pltpu.VMEM((8, lane), jnp.float32)],
        0,
        0,
    )(beam[None])
    filtered = run_filter(plan, sharers, pieces, parts, tables)
    moved = exchange_all(plan, filtered)
    bits = [1 << i for i in range(1, sim_devices.bit_length() - 1)]
    arrays, holders = [], []
    for step, piece in enumerate(moved):
        turn = step % max(len(bits), 1)
        found, offsets = gather(piece, "sims", bits[turn:] + bits[:turn])
        arrays.append(found)
        holders.append(offsets)
    held = []
    for found, offsets in zip(arrays, holders):
        held += found + [exchange(jnp.concatenate(found), "sims", 1)]
        offsets.append([offset ^ 1 for order in offsets for offset in order])

    results, fused = run_estimate(plan, holders, pair_one, pair_two, owner, held)
    estimate = results[0]
    if fused:
        mean_field = results[1]
    else:
        groups = jnp.arange(OWNERS, dtype=jnp.int32)
        local_owner = owner[lax.axis_index("sims")]
        term = jnp.where((groups == local_owner)[:, None, None], estimate[None], 0.0)
        total = lax.psum_scatter(term, "sims", scatter_dimension=2, tiled=True)
        tally = jnp.sum((groups[:, None] == owner[None, :]).astype(jnp.float32), axis=1)
        mean_field = total / jnp.maximum(tally, 1.0)[:, None, None]
    return estimate.reshape(maps.shape), mean_field


def solution(mesh):
    in_specs = (P("sims", "rows", None), P("rows", None), P(), P(), P(), P())
    out_specs = (P("sims", "rows", None), P(None, "rows", "sims"))
    return jax.shard_map(body, mesh=mesh, in_specs=in_specs, out_specs=out_specs, check_vma=False)
```

```python
import functools

import jax
import jax.numpy as jnp
from jax import lax
from jax.experimental import pallas as pl
from jax.experimental.pallas import tpu as pltpu
from jax.sharding import PartitionSpec as P

ITERS = 3
OWNERS = 8

ridge_term = 0.5
step_size = 0.6
exact = lax.Precision.HIGHEST
lane = 128
wide = 256
stretch = 1024
rim = 2
loads = 4
vmem_bytes = 48 * 1024 * 1024


def split(value):
    high = value.astype(jnp.bfloat16)
    low = (value - high.astype(jnp.float32)).astype(jnp.bfloat16)
    return high, low


def dot(a, b):
    return jnp.dot(a, b, preferred_element_type=jnp.float32)


class Plan:
    def __init__(self, row_devices, sim_devices, row_local, columns, taps):
        self.row_devices, self.sim_devices = row_devices, sim_devices
        self.row_local, self.columns = row_local, columns
        self.rows = row_devices * row_local
        self.steps = [0, *range(row_devices - 1, 0, -1)]
        self.margin = (taps - 1) // 2
        self.share = columns // row_devices
        self.halo = -(-self.margin * (2 * ITERS + 1) // lane) * lane
        self.width = self.share + 2 * self.halo
        self.slab = row_local + 4 * rim
        self.chips = sim_devices // 2
        self.sharers = min(sim_devices, row_local // 8)
        self.share_rows = row_local // self.sharers
        self.length = max(2 * wide, -(-self.rows // lane) * lane)
        inner = range(lane, self.width - lane, wide)
        blocks = [(0, lane)] + [(a, min(a + wide, self.width - lane)) for a in inner]
        self.blocks = blocks + [(self.width - lane, self.width)]
        centre = range(self.halo, self.halo + self.share, wide)
        self.out_blocks = [(a, min(a + wide, self.halo + self.share)) for a in centre]

    def sides(self):
        left = (self.halo - rim - self.margin) // lane * lane
        return left, (self.halo + self.share - self.margin) // lane * lane

    def window(self, block):
        return max(0, block[0] - lane), min(self.width, block[1] + lane)

    def stage_blocks(self, iteration):
        low = self.halo - self.margin * (2 * (ITERS - 1 - iteration) + 1)
        return [i for i, (a, b) in enumerate(self.blocks) if b > low and a < self.width - low]


def piece_kernel(plan, maps, weight, *refs):
    count = plan.row_devices
    pieces, parts = refs[:count], refs[count : 2 * count]
    padded, weights, given, sems = refs[2 * count :]
    rows_at, sims_at = lax.axis_index("rows"), lax.axis_index("sims")
    chunk = plan.row_local // loads
    inner = slice(plan.halo, plan.halo + plan.columns)
    copies = []
    for number in range(loads):
        rows = pl.ds(number * chunk, chunk)
        copies.append((
            pltpu.make_async_copy(weight.at[rows], weights.at[rows, inner], sems.at[0, number]),
            pltpu.make_async_copy(maps.at[rows], given.at[rows], sems.at[1, number]),
        ))
        for copy in copies[-1]:
            copy.start()
    zeros = jnp.zeros((plan.row_local, plan.halo), jnp.float32)
    for target in (padded, weights):
        target[:, : plan.halo] = zeros
        target[:, plan.halo + plan.columns :] = zeros
    starts = [pl.multiple_of((rows_at ^ step) * plan.share, lane) for step in plan.steps]
    for number in range(loads):
        for copy in copies[number]:
            copy.wait()
        rows = slice(number * chunk, (number + 1) * chunk)
        padded[rows, inner] = weights[rows, inner] * given[rows]
        for piece, column in zip(pieces, starts):
            piece[rows] = padded[rows, pl.ds(column, plan.width)]
    row = pl.multiple_of(lax.rem(sims_at, plan.sharers) * plan.share_rows, plan.share_rows)
    for part, column in zip(parts, starts):
        part[...] = weights[pl.ds(row, plan.share_rows), pl.ds(column, plan.width)]


def band(plan, taps, rows, columns, offset):
    if offset % plan.length:
        taps = pltpu.roll(taps, offset % plan.length, 1)
    spread = jnp.broadcast_to(taps[:1], (rows, plan.length))
    rolled = pltpu.roll(spread, 0, 1, stride=1, stride_axis=0)[:, :columns]
    row = lax.broadcasted_iota(jnp.int32, (rows, columns), 0)
    column = lax.broadcasted_iota(jnp.int32, (rows, columns), 1)
    return jnp.where(jnp.abs(column - row - offset) <= plan.margin, rolled, 0.0)


def table_kernel(plan, beam, *refs):
    refs, line = refs[:-1], refs[-1]
    count = beam.shape[1]
    line[...] = jnp.zeros(line.shape, jnp.float32)
    line[:1, :count] = beam[...]
    kernel = line[...]
    kernel = kernel / jnp.sum(kernel[:1], axis=1, keepdims=True)
    size = kernel.shape[1]
    row = lax.broadcasted_iota(jnp.int32, (size, size), 0)
    column = lax.broadcasted_iota(jnp.int32, (size, size), 1)
    mirror = (row + column == count - 1).astype(jnp.float32)
    blank = jnp.zeros((kernel.shape[0], plan.length - size), jnp.float32)

    def centred(values):
        return pltpu.roll(jnp.concatenate([values, blank], axis=1), plan.length - plan.margin, 1)

    taps, reverse = centred(kernel), centred(jnp.dot(kernel, mirror, precision=exact))
    tables = list(refs)

    def put(value):
        high, low = split(value)
        tables.pop(0)[...] = high
        tables.pop(0)[...] = low

    rows = plan.rows
    put(jnp.dot(band(plan, taps, rows, rows, 0), band(plan, reverse, rows, rows, 0), precision=exact))
    slabs = []
    for device in range(plan.row_devices):
        first = device * plan.row_local - rim
        part = band(plan, reverse, plan.slab, rows, first)
        row = lax.broadcasted_iota(jnp.int32, part.shape, 0)
        inside = (row + first >= 0) & (row + first < rows) & (row < plan.row_local + 2 * rim)
        slabs.append(jnp.where(inside, part, 0.0))
    put(jnp.concatenate(slabs, axis=0))
    size = 2 * wide
    forward = band(plan, taps, size, size, 0)
    backward = band(plan, reverse, size, size, 0)[:, lane : lane + wide]
    square = step_size * jnp.dot(forward, backward, precision=exact)
    for block in plan.blocks:
        low, high = plan.window(block)
        first = low - block[0] + lane
        wanted = square[first : first + high - low, : block[1] - block[0]]
        high_term, low_term = tables[0], tables[1]
        put(wanted)
        origin = lax.axis_index("rows") * plan.share - plan.halo + low
        reach = origin + high - low
        cut = ((origin < 0) & (reach > 0)) | ((origin < plan.columns) & (reach > plan.columns))

        @pl.when(cut)
        def _(origin=origin, extent=high - low, first=first, span=block[1] - block[0], terms=(high_term, low_term)):
            column = lax.broadcasted_iota(jnp.int32, (size, size), 1) + (origin - first)
            inside = (column >= 0) & (column < plan.columns)
            value = step_size * jnp.dot(jnp.where(inside, forward, 0.0), backward, precision=exact)
            high_part, low_part = split(value[first : first + extent, :span])
            terms[0][...] = high_part
            terms[1][...] = low_part

    for block in plan.out_blocks[:1]:
        low, high = plan.window(block)
        put(step_size * forward[: high - low, block[0] - low : block[1] - low])
    left, right = plan.sides()
    column = lax.broadcasted_iota(jnp.int32, (wide, lane), 1)
    before = band(plan, taps, wide, lane, left - (plan.halo - lane))
    behind = band(plan, taps, wide, lane, right - (plan.halo + plan.share))
    rows_at = lax.axis_index("rows")
    before = jnp.where((column >= lane - rim) & (rows_at > 0), before, 0.0)
    behind = jnp.where((column < rim) & (rows_at < plan.row_devices - 1), behind, 0.0)
    put(step_size * jnp.concatenate([before, behind], axis=0))


def filter_kernel(plan, sharers, *refs):
    refs = list(refs)

    def take(number):
        taken = refs[:number]
        del refs[:number]
        return taken

    pieces = take(plan.row_devices)
    parts = take(len(sharers))
    square, final = take(2), take(2)
    bands = [take(2) for _ in plan.blocks]
    last, edges = take(2), take(2)
    outs = take(plan.row_devices)
    seen, weight, image, base, total, field, side, high, low, mid_high, mid_low, sem = refs
    for part, owners in zip(parts, sharers):
        for slot, offset in enumerate(owners):
            for index, step in enumerate(plan.steps):
                row = (lax.axis_index("rows") ^ step) * plan.row_local
                row = row + (lax.rem(lax.axis_index("sims"), plan.sharers) ^ offset) * plan.share_rows
                rows = pl.ds(pl.multiple_of(row, plan.share_rows), plan.share_rows)
                pltpu.make_async_copy(part.at[slot, index], weight.at[rows], sem).start()
    for step, piece in zip(plan.steps, pieces):
        rows = pl.ds(pl.multiple_of((lax.axis_index("rows") ^ step) * plan.row_local, plan.row_local), plan.row_local)
        value = piece[...]
        seen[rows, :] = value
        high[rows, :], low[rows, :] = split(value)
    def rows_pass(table, start, stop, full=True):
        count = table[0].shape[0]
        for a in range(start, stop, wide):
            b = min(a + wide, stop)
            value = dot(table[0][...], high[:, a:b]) + dot(table[1][...], high[:, a:b])
            if full:
                value = value + dot(table[0][...], low[:, a:b])
                mid_high[:count, a:b], mid_low[:count, a:b] = split(value)
            else:
                mid_high[:count, a:b] = value.astype(jnp.bfloat16)

    def columns_pass(table, count, window, full=True):
        a, b = window
        value = dot(mid_high[:count, a:b], table[0][...]) + dot(mid_high[:count, a:b], table[1][...])
        return value + dot(mid_low[:count, a:b], table[0][...]) if full else value

    keep = 1.0 - step_size * ridge_term
    for iteration in range(ITERS):
        chosen = plan.stage_blocks(iteration)
        windows = [plan.window(plan.blocks[i]) for i in chosen]
        rows_pass(square, windows[0][0], windows[-1][1], iteration == 0)
        if iteration == 0:
            for i, window in zip(chosen, windows):
                base[:, slice(*plan.blocks[i])] = columns_pass(bands[i], plan.rows, window)
            pltpu.make_async_copy(weight, weight, sem).wait()
        for i, window in zip(chosen, windows):
            a, b = plan.blocks[i]
            value = base[:, a:b]
            if iteration > 0:
                value = keep * image[:, a:b] + value - columns_pass(bands[i], plan.rows, window, False)
            image[:, a:b] = value
            product = weight[:, a:b] * value
            given = seen[:, a:b]
            total[:, a:b] = given - product + keep * (total[:, a:b] if iteration > 0 else given)
            high[:, a:b] = product.astype(jnp.bfloat16)
    first, stop = plan.window(plan.out_blocks[0])[0], plan.window(plan.out_blocks[-1])[1]
    high[:, first:stop], low[:, first:stop] = split(total[:, first:stop])
    rows_pass(final, first, stop)
    count = plan.row_devices * plan.slab
    for block in plan.out_blocks:
        size = block[1] - block[0]
        field[:, block[0] - plan.halo : block[1] - plan.halo] = columns_pass(last, count, plan.window(block))
    value = jnp.zeros((count, lane), jnp.float32)
    for number, start in enumerate(plan.sides()):
        part = slice(number * wide, (number + 1) * wide)
        a, b = mid_high[:count, start : start + wide], mid_low[:count, start : start + wide]
        value = value + dot(a, edges[0][part]) + dot(a, edges[1][part]) + dot(b, edges[0][part])
    side[:count] = value
    turned = side[...].T
    turned = jnp.concatenate([turned[lane - rim :], turned[:rim]], axis=0)
    for device in range(plan.row_devices):
        shift = (side.shape[0] - device * plan.slab - rim) % side.shape[0]
        row = (device + 1) * plan.slab - 2 * rim
        field[row : row + 2 * rim, :lane] = pltpu.roll(turned, shift, 1)[:, :lane]
    for step, out in zip(plan.steps, outs):
        row = pl.multiple_of((lax.axis_index("rows") ^ step) * plan.slab, 8)
        out[...] = field[pl.ds(row, plan.slab), :]


def divergence(own, partner):
    rows, columns = own.shape
    stop, inner = rows - rim, slice(0, columns - lane)
    here = partner[rim:stop]
    down, up = partner[2 * rim :, inner], partner[: stop - rim, inner]
    middle = here[:, inner]
    flow = own[rim + 1 : stop + 1, inner] * (down - middle) - own[rim - 1 : stop - 1, inner] * (middle - up)
    level = own[rim:stop]

    def shifted(value, amount):
        return pltpu.roll(value, amount % columns, 1)[:, inner]

    right = shifted(level, -1) * (shifted(here, -2) - middle)
    left = shifted(level, 1) * (middle - shifted(here, 2))
    return 0.25 * (flow + (right - left))


def collect(plan, near, far, every, corner):
    core = lax.axis_index("sims") % 2
    here = lax.axis_index("sims") // 2
    corner[...] = jnp.zeros(corner.shape, jnp.float32)
    kept = plan.row_local + 2 * rim
    for step in range(plan.chips):
        for source, parity in ((near[step], core), (far[step], 1 - core)):
            at = 2 * (here ^ step) + parity
            every[at, :, : plan.share] = source[:kept]
            corner[lane - rim :] = source[kept : kept + rim, :lane]
            corner[:rim] = source[kept + rim : kept + 2 * rim, :lane]
            every[at, rim : kept - rim, plan.share :] = corner[...].T[: plan.row_local]


def mixed(every, pair_one, pair_two, sim):
    return divergence(every[sim], 2.0 * every[pair_one[sim]] - every[pair_two[sim]])


def estimate_kernel(plan, pair_one, pair_two, *refs):
    near, far, outs = refs[: plan.chips], refs[plan.chips : 2 * plan.chips], refs[2 * plan.chips : -2]
    every, corner = refs[-2:]
    collect(plan, near, far, every, corner)
    chip, core = lax.axis_index("sims") // 2, lax.axis_index("sims") % 2
    for step, out in enumerate(outs):
        out[...] = mixed(every, pair_one, pair_two, 2 * (chip ^ step) + core)


def mean_kernel(plan, field_width, pair_one, pair_two, owner, *refs):
    near, far, done = [refs[first * plan.chips : (first + 1) * plan.chips] for first in range(3)]
    mean_field, every, corner, whole = refs[3 * plan.chips :]
    collect(plan, near, far, every, corner)
    chip, core = lax.axis_index("sims") // 2, lax.axis_index("sims") % 2
    whole[...] = jnp.zeros(whole.shape, jnp.float32)
    for step, estimate in enumerate(done):
        sim = 2 * (chip ^ step)
        whole[owner[sim + core]] += estimate[...]
        whole[owner[sim + 1 - core]] += mixed(every, pair_one, pair_two, sim + 1 - core)
    span = pl.ds(pl.multiple_of(core * field_width, lane), field_width) if field_width < plan.share else slice(None)
    for group in range(OWNERS):
        count = jnp.int32(0)
        for sim in range(plan.sim_devices):
            count = count + (owner[sim] == group).astype(jnp.int32)
        mean_field[group] = whole[group, :, span] / jnp.maximum(count, 1).astype(jnp.float32)


def join_kernel(plan, *refs):
    pieces, estimate, sems = refs[: plan.chips], refs[plan.chips], refs[plan.chips + 1]
    copies = []
    for step, piece in enumerate(pieces):
        column = pl.multiple_of(((lax.axis_index("sims") // 2) ^ step) * plan.share, lane)
        copies.append(pltpu.make_async_copy(piece, estimate.at[:, pl.ds(column, plan.share)], sems.at[step]))
        copies[-1].start()
    for copy in copies:
        copy.wait()


def exchange(value, axis, offset):
    count = lax.axis_size(axis)
    return lax.ppermute(value, axis, [(i, i ^ offset) for i in range(count)])


def exchange_all(plan, values):
    return [exchange(value, "rows", step) if step else value for step, value in zip(plan.steps, values)]


def call(kernel, out_shapes, in_specs, scratch, flops, moved, outs_in=pltpu.VMEM):
    return pl.pallas_call(
        kernel,
        out_shape=out_shapes,
        in_specs=in_specs,
        out_specs=[pl.BlockSpec(memory_space=outs_in)] * len(out_shapes),
        scratch_shapes=scratch,
        compiler_params=pltpu.CompilerParams(vmem_limit_bytes=vmem_bytes),
        cost_estimate=pl.CostEstimate(flops=flops, bytes_accessed=moved, transcendentals=0),
    )


def run_filter(plan, sharers, pieces, parts, tables):
    vmem = pl.BlockSpec(memory_space=pltpu.VMEM)
    far = pl.BlockSpec(memory_space=pltpu.HBM)
    full = (plan.rows, plan.width)
    tall = (max(plan.rows, plan.row_devices * plan.slab), plan.width)
    return call(
        functools.partial(filter_kernel, plan, sharers),
        [jax.ShapeDtypeStruct((plan.slab, plan.share), jnp.float32)] * plan.row_devices,
        [vmem] * plan.row_devices + [far] * len(parts) + [vmem] * len(tables),
        [pltpu.VMEM(full, jnp.float32)] * 5
        + [pltpu.VMEM((plan.row_devices * plan.slab, plan.share), jnp.float32)]
        + [pltpu.VMEM((-(-plan.row_devices * plan.slab // lane) * lane, lane), jnp.float32)]
        + [pltpu.VMEM(full, jnp.bfloat16)] * 2
        + [pltpu.VMEM(tall, jnp.bfloat16)] * 2
        + [pltpu.SemaphoreType.DMA],
        1 << 33,
        1 << 23,
    )(*pieces, *parts, *tables)


def order_of(plan, offset):
    return jnp.where(offset == 0, 0, plan.row_devices - offset)


def run_estimates(plan, pieces, pair_one, pair_two, owner):
    vmem = pl.BlockSpec(memory_space=pltpu.VMEM)
    smem = pl.BlockSpec(memory_space=pltpu.SMEM)
    axes = ("sims", "rows")
    places = [(sim, row) for sim in range(plan.sim_devices) for row in range(plan.row_devices)]

    def f32(*shape):
        return jax.ShapeDtypeStruct(shape, jnp.float32)

    def hop(value, target):
        count = plan.row_devices
        pairs = [(sim * count + row, target(sim, row)[0] * count + target(sim, row)[1]) for sim, row in places]
        return lax.ppermute(value, axes, pairs)

    moved = jnp.stack(exchange_all(plan, pieces))
    here = (lax.axis_index("sims") // 2) ^ lax.axis_index("rows")
    near = []
    for step in range(plan.chips):
        value = lax.dynamic_index_in_dim(moved, order_of(plan, here ^ step), keepdims=False)
        near.append(exchange(value, "sims", 2 * step) if step else value)
    far = [exchange(value, "sims", 1) for value in near]
    scratch = [
        pltpu.VMEM((plan.sim_devices, plan.row_local + 2 * rim, plan.share + lane), jnp.float32),
        pltpu.VMEM((lane, lane), jnp.float32),
    ]
    found = call(
        functools.partial(estimate_kernel, plan),
        [f32(plan.row_local, plan.share)] * plan.chips,
        [smem] * 2 + [vmem] * (2 * plan.chips),
        scratch,
        1 << 24,
        1 << 23,
    )(pair_one, pair_two, *near, *far)
    field_width = plan.columns // plan.sim_devices
    kept = field_width if field_width % lane == 0 else plan.share
    [mean_field] = call(
        functools.partial(mean_kernel, plan, kept),
        [f32(OWNERS, plan.row_local, kept)],
        [smem] * 3 + [vmem] * (3 * plan.chips),
        scratch + [pltpu.VMEM((OWNERS, plan.row_local, plan.share), jnp.float32)],
        1 << 24,
        1 << 23,
    )(pair_one, pair_two, owner, *near, *far, *found)
    if kept != field_width:
        start = (lax.axis_index("sims") % 2) * field_width
        mean_field = lax.dynamic_slice_in_dim(mean_field, start, field_width, axis=2)
    moved = [value if step == 0 else exchange(value, "sims", 2 * step) for step, value in enumerate(found)]
    [estimate] = call(
        functools.partial(join_kernel, plan),
        [f32(plan.row_local, plan.columns)],
        [vmem] * plan.chips,
        [pltpu.SemaphoreType.DMA((plan.chips,))],
        0,
        1 << 20,
        outs_in=pltpu.HBM,
    )(*moved)
    return estimate, mean_field


def body(maps, weight, beam, pair_one, pair_two, owner):
    sim_local, row_local, columns = maps.shape
    taps = beam.shape[0]
    row_devices, sim_devices = lax.axis_size("rows"), lax.axis_size("sims")
    plan = Plan(row_devices, sim_devices, row_local, columns, taps)
    vmem = pl.BlockSpec(memory_space=pltpu.VMEM)
    smem = pl.BlockSpec(memory_space=pltpu.SMEM)
    far = pl.BlockSpec(memory_space=pltpu.HBM)

    def pinned(value):
        return pltpu.with_memory_space_constraint(value, pltpu.HBM)

    def f32(*shape):
        return jax.ShapeDtypeStruct(shape, jnp.float32)

    def b16(*shape):
        return jax.ShapeDtypeStruct(shape, jnp.bfloat16)

    cells = row_local * columns
    made = call(
        functools.partial(piece_kernel, plan),
        [f32(row_local, plan.width)] * row_devices + [f32(plan.share_rows, plan.width)] * row_devices,
        [far, far],
        [pltpu.VMEM((row_local, columns + 2 * plan.halo), jnp.float32)] * 2
        + [pltpu.VMEM((row_local, columns), jnp.float32), pltpu.SemaphoreType.DMA((2, loads))],
        cells,
        16 * cells,
    )(pinned(maps.reshape(row_local, columns)), pinned(weight))
    pieces, parts = made[:row_devices], made[row_devices:]
    parts = exchange_all(plan, parts)
    pieces, parts = lax.optimization_barrier((pieces, parts))
    pieces = exchange_all(plan, pieces)
    shapes = [(plan.rows, plan.rows), (row_devices * plan.slab, plan.rows)]
    for block in plan.blocks + plan.out_blocks[:1]:
        low, high = plan.window(block)
        shapes.append((high - low, block[1] - block[0]))
    shapes.append((2 * wide, lane))


    def spread(parts):
        found = {0: jnp.stack(parts)[None]}
        for bit in [1 << i for i in range(1, plan.sharers.bit_length() - 1)]:
            found |= {offset | bit: exchange(value, "sims", bit) for offset, value in found.items()}
        sharers[:] = [[offset] for offset in found] + [[offset ^ 1 for offset in found]]
        return [*found.values(), exchange(jnp.concatenate(list(found.values())), "sims", 1)]

    sharers = []
    made = jax.eval_shape(spread, parts)
    parts = lax.cond(
        lax.axis_index("rows") < row_devices,
        spread,
        lambda parts: jax.tree.map(lambda x: jnp.zeros(x.shape, x.dtype), made),
        parts,
    )
    beam, parts = lax.optimization_barrier((beam, parts))
    tables = call(
        functools.partial(table_kernel, plan),
        [b16(*shape) for shape in shapes for _ in range(2)],
        [vmem],
        [pltpu.VMEM((8, lane), jnp.float32)],
        0,
        0,
    )(beam[None])
    filtered = run_filter(plan, sharers, pieces, parts, tables)
    estimate, mean_field = run_estimates(plan, filtered, pair_one, pair_two, owner)
    return estimate.reshape(maps.shape), mean_field


def solution(mesh):
    in_specs = (P("sims", "rows", None), P("rows", None), P(), P(), P(), P())
    out_specs = (P("sims", "rows", None), P(None, "rows", "sims"))
    return jax.shard_map(body, mesh=mesh, in_specs=in_specs, out_specs=out_specs, check_vma=False)
```

```python
import functools

import jax
import jax.numpy as jnp
from jax import lax
from jax.experimental import pallas as pl
from jax.experimental.pallas import tpu as pltpu
from jax.sharding import PartitionSpec as P

ITERS = 3
OWNERS = 8

ridge_term = 0.5
step_size = 0.6
exact = lax.Precision.HIGHEST
lane = 128
wide = 256
stretch = 1024
rim = 2
loads = 4
vmem_bytes = 48 * 1024 * 1024


def split(value):
    high = value.astype(jnp.bfloat16)
    low = (value - high.astype(jnp.float32)).astype(jnp.bfloat16)
    return high, low


def dot(a, b):
    return jnp.dot(a, b, preferred_element_type=jnp.float32)


class Plan:
    def __init__(self, row_devices, sim_devices, row_local, columns, taps):
        self.row_devices, self.sim_devices = row_devices, sim_devices
        self.row_local, self.columns = row_local, columns
        self.rows = row_devices * row_local
        self.steps = [0, *range(row_devices - 1, 0, -1)]
        self.margin = (taps - 1) // 2
        self.share = columns // row_devices
        self.halo = -(-self.margin * (2 * ITERS + 1) // lane) * lane
        self.width = self.share + 2 * self.halo
        self.slab = row_local + 4 * rim
        self.chips = sim_devices // 2
        self.sharers = min(sim_devices, row_local // 8)
        self.share_rows = row_local // self.sharers
        self.head = row_local // 8
        self.length = max(2 * wide, -(-self.rows // lane) * lane)
        inner = range(lane, self.width - lane, wide)
        blocks = [(0, lane)] + [(a, min(a + wide, self.width - lane)) for a in inner]
        self.blocks = blocks + [(self.width - lane, self.width)]
        centre = range(self.halo, self.halo + self.share, wide)
        self.out_blocks = [(a, min(a + wide, self.halo + self.share)) for a in centre]

    def sides(self):
        left = (self.halo - rim - self.margin) // lane * lane
        return left, (self.halo + self.share - self.margin) // lane * lane

    def window(self, block):
        return max(0, block[0] - lane), min(self.width, block[1] + lane)

    def stage_blocks(self, iteration):
        low = self.halo - self.margin * (2 * (ITERS - 1 - iteration) + 1)
        return [i for i, (a, b) in enumerate(self.blocks) if b > low and a < self.width - low]


def piece_kernel(plan, maps, weight, *refs):
    count = plan.row_devices
    heads, tails = refs[:count], refs[count : 2 * count]
    padded, weights, given, sems = refs[2 * count :]
    rows_at, sims_at = lax.axis_index("rows"), lax.axis_index("sims")
    chunk = plan.row_local // loads
    inner = slice(plan.halo, plan.halo + plan.columns)
    copies = []
    for number in range(loads):
        rows = pl.ds(number * chunk, chunk)
        copies.append((
            pltpu.make_async_copy(weight.at[rows], weights.at[rows, inner], sems.at[0, number]),
            pltpu.make_async_copy(maps.at[rows], given.at[rows], sems.at[1, number]),
        ))
        for copy in copies[-1]:
            copy.start()
    zeros = jnp.zeros((plan.row_local, plan.halo), jnp.float32)
    for target in (padded, weights):
        target[:, : plan.halo] = zeros
        target[:, plan.halo + plan.columns :] = zeros
    for number in range(loads):
        for copy in copies[number]:
            copy.wait()
        rows = slice(number * chunk, (number + 1) * chunk)
        padded[rows, inner] = weights[rows, inner] * given[rows]
    row = pl.multiple_of(lax.rem(sims_at, plan.sharers) * plan.share_rows, plan.share_rows)
    for index, step in enumerate(plan.steps):
        span = pl.ds(pl.multiple_of((rows_at ^ step) * plan.share, lane), plan.width)
        heads[index][: plan.share_rows] = weights[pl.ds(row, plan.share_rows), span]
        heads[index][plan.share_rows :] = padded[: plan.head, span]
        tails[index][...] = padded[plan.head :, span]


def band(plan, taps, rows, columns, offset):
    if offset % plan.length:
        taps = pltpu.roll(taps, offset % plan.length, 1)
    spread = jnp.broadcast_to(taps[:1], (rows, plan.length))
    rolled = pltpu.roll(spread, 0, 1, stride=1, stride_axis=0)[:, :columns]
    row = lax.broadcasted_iota(jnp.int32, (rows, columns), 0)
    column = lax.broadcasted_iota(jnp.int32, (rows, columns), 1)
    return jnp.where(jnp.abs(column - row - offset) <= plan.margin, rolled, 0.0)


def table_kernel(plan, beam, *refs):
    refs, line = refs[:-1], refs[-1]
    count = beam.shape[1]
    line[...] = jnp.zeros(line.shape, jnp.float32)
    line[:1, :count] = beam[...]
    kernel = line[...]
    kernel = kernel / jnp.sum(kernel[:1], axis=1, keepdims=True)
    size = kernel.shape[1]
    row = lax.broadcasted_iota(jnp.int32, (size, size), 0)
    column = lax.broadcasted_iota(jnp.int32, (size, size), 1)
    mirror = (row + column == count - 1).astype(jnp.float32)
    blank = jnp.zeros((kernel.shape[0], plan.length - size), jnp.float32)

    def centred(values):
        return pltpu.roll(jnp.concatenate([values, blank], axis=1), plan.length - plan.margin, 1)

    taps, reverse = centred(kernel), centred(jnp.dot(kernel, mirror, precision=exact))
    tables = list(refs)

    def put(value):
        high, low = split(value)
        tables.pop(0)[...] = high
        tables.pop(0)[...] = low

    rows = plan.rows
    put(jnp.dot(band(plan, taps, rows, rows, 0), band(plan, reverse, rows, rows, 0), precision=exact))
    slabs = []
    for device in range(plan.row_devices):
        first = device * plan.row_local - rim
        part = band(plan, reverse, plan.slab, rows, first)
        row = lax.broadcasted_iota(jnp.int32, part.shape, 0)
        inside = (row + first >= 0) & (row + first < rows) & (row < plan.row_local + 2 * rim)
        slabs.append(jnp.where(inside, part, 0.0))
    put(jnp.concatenate(slabs, axis=0))
    size = 2 * wide
    forward = band(plan, taps, size, size, 0)
    backward = band(plan, reverse, size, size, 0)[:, lane : lane + wide]
    square = step_size * jnp.dot(forward, backward, precision=exact)
    for block in plan.blocks:
        low, high = plan.window(block)
        first = low - block[0] + lane
        wanted = square[first : first + high - low, : block[1] - block[0]]
        high_term, low_term = tables[0], tables[1]
        put(wanted)
        origin = lax.axis_index("rows") * plan.share - plan.halo + low
        reach = origin + high - low
        cut = ((origin < 0) & (reach > 0)) | ((origin < plan.columns) & (reach > plan.columns))

        @pl.when(cut)
        def _(origin=origin, extent=high - low, first=first, span=block[1] - block[0], terms=(high_term, low_term)):
            column = lax.broadcasted_iota(jnp.int32, (size, size), 1) + (origin - first)
            inside = (column >= 0) & (column < plan.columns)
            value = step_size * jnp.dot(jnp.where(inside, forward, 0.0), backward, precision=exact)
            high_part, low_part = split(value[first : first + extent, :span])
            terms[0][...] = high_part
            terms[1][...] = low_part

    for block in plan.out_blocks[:1]:
        low, high = plan.window(block)
        put(step_size * forward[: high - low, block[0] - low : block[1] - low])
    left, right = plan.sides()
    column = lax.broadcasted_iota(jnp.int32, (wide, lane), 1)
    before = band(plan, taps, wide, lane, left - (plan.halo - lane))
    behind = band(plan, taps, wide, lane, right - (plan.halo + plan.share))
    rows_at = lax.axis_index("rows")
    before = jnp.where((column >= lane - rim) & (rows_at > 0), before, 0.0)
    behind = jnp.where((column < rim) & (rows_at < plan.row_devices - 1), behind, 0.0)
    put(step_size * jnp.concatenate([before, behind], axis=0))


def filter_kernel(plan, sharers, *refs):
    refs = list(refs)

    def take(number):
        taken = refs[:number]
        del refs[:number]
        return taken

    heads, tails = take(plan.row_devices), take(plan.row_devices)
    parts = take(len(sharers))
    square, final = take(2), take(2)
    bands = [take(2) for _ in plan.blocks]
    last, edges = take(2), take(2)
    outs = take(plan.row_devices)
    seen, weight, image, base, total, field, side, high, low, mid_high, mid_low, sem = refs
    for part, owners in zip(parts, sharers):
        for slot, offset in enumerate(owners):
            for index, step in enumerate(plan.steps):
                row = (lax.axis_index("rows") ^ step) * plan.row_local
                row = row + (lax.rem(lax.axis_index("sims"), plan.sharers) ^ offset) * plan.share_rows
                rows = pl.ds(pl.multiple_of(row, plan.share_rows), plan.share_rows)
                pltpu.make_async_copy(part.at[slot, index], weight.at[rows], sem).start()
    for index, step in enumerate(plan.steps):
        row = pl.multiple_of((lax.axis_index("rows") ^ step) * plan.row_local, plan.row_local)
        rows = pl.ds(row, plan.row_local)
        value = jnp.concatenate([heads[index][plan.share_rows :], tails[index][...]], axis=0)
        seen[rows, :] = value
        high[rows, :], low[rows, :] = split(value)

    def rows_pass(table, start, stop, full=True):
        count = table[0].shape[0]
        for a in range(start, stop, wide):
            b = min(a + wide, stop)
            value = dot(table[0][...], high[:, a:b]) + dot(table[1][...], high[:, a:b])
            if full:
                value = value + dot(table[0][...], low[:, a:b])
                mid_high[:count, a:b], mid_low[:count, a:b] = split(value)
            else:
                mid_high[:count, a:b] = value.astype(jnp.bfloat16)

    def columns_pass(table, count, window, full=True):
        a, b = window
        value = dot(mid_high[:count, a:b], table[0][...]) + dot(mid_high[:count, a:b], table[1][...])
        return value + dot(mid_low[:count, a:b], table[0][...]) if full else value

    keep = 1.0 - step_size * ridge_term
    for iteration in range(ITERS):
        chosen = plan.stage_blocks(iteration)
        windows = [plan.window(plan.blocks[i]) for i in chosen]
        rows_pass(square, windows[0][0], windows[-1][1], iteration == 0)
        if iteration == 0:
            for i, window in zip(chosen, windows):
                base[:, slice(*plan.blocks[i])] = columns_pass(bands[i], plan.rows, window)
            pltpu.make_async_copy(weight, weight, sem).wait()
        for i, window in zip(chosen, windows):
            a, b = plan.blocks[i]
            value = base[:, a:b]
            if iteration > 0:
                value = keep * image[:, a:b] + value - columns_pass(bands[i], plan.rows, window, False)
            image[:, a:b] = value
            product = weight[:, a:b] * value
            given = seen[:, a:b]
            total[:, a:b] = given - product + keep * (total[:, a:b] if iteration > 0 else given)
            high[:, a:b] = product.astype(jnp.bfloat16)
    first, stop = plan.window(plan.out_blocks[0])[0], plan.window(plan.out_blocks[-1])[1]
    high[:, first:stop], low[:, first:stop] = split(total[:, first:stop])
    rows_pass(final, first, stop)
    count = plan.row_devices * plan.slab
    for block in plan.out_blocks:
        size = block[1] - block[0]
        field[:, block[0] - plan.halo : block[1] - plan.halo] = columns_pass(last, count, plan.window(block))
    value = jnp.zeros((count, lane), jnp.float32)
    for number, start in enumerate(plan.sides()):
        part = slice(number * wide, (number + 1) * wide)
        a, b = mid_high[:count, start : start + wide], mid_low[:count, start : start + wide]
        value = value + dot(a, edges[0][part]) + dot(a, edges[1][part]) + dot(b, edges[0][part])
    side[:count] = value
    turned = side[...].T
    turned = jnp.concatenate([turned[lane - rim :], turned[:rim]], axis=0)
    for device in range(plan.row_devices):
        shift = (side.shape[0] - device * plan.slab - rim) % side.shape[0]
        row = (device + 1) * plan.slab - 2 * rim
        field[row : row + 2 * rim, :lane] = pltpu.roll(turned, shift, 1)[:, :lane]
    for step, out in zip(plan.steps, outs):
        row = pl.multiple_of((lax.axis_index("rows") ^ step) * plan.slab, 8)
        out[...] = field[pl.ds(row, plan.slab), :]


def divergence(own, partner):
    rows, columns = own.shape
    stop, inner = rows - rim, slice(0, columns - lane)
    here = partner[rim:stop]
    down, up = partner[2 * rim :, inner], partner[: stop - rim, inner]
    middle = here[:, inner]
    flow = own[rim + 1 : stop + 1, inner] * (down - middle) - own[rim - 1 : stop - 1, inner] * (middle - up)
    level = own[rim:stop]

    def shifted(value, amount):
        return pltpu.roll(value, amount % columns, 1)[:, inner]

    right = shifted(level, -1) * (shifted(here, -2) - middle)
    left = shifted(level, 1) * (middle - shifted(here, 2))
    return 0.25 * (flow + (right - left))


def collect(plan, near, far, every, corner):
    core = lax.axis_index("sims") % 2
    here = lax.axis_index("sims") // 2
    corner[...] = jnp.zeros(corner.shape, jnp.float32)
    kept = plan.row_local + 2 * rim
    for step in range(plan.chips):
        for source, parity in ((near[step], core), (far[step], 1 - core)):
            at = 2 * (here ^ step) + parity
            every[at, :, : plan.share] = source[:kept]
            corner[lane - rim :] = source[kept : kept + rim, :lane]
            corner[:rim] = source[kept + rim : kept + 2 * rim, :lane]
            every[at, rim : kept - rim, plan.share :] = corner[...].T[: plan.row_local]


def mixed(every, pair_one, pair_two, sim):
    return divergence(every[sim], 2.0 * every[pair_one[sim]] - every[pair_two[sim]])


def estimate_kernel(plan, pair_one, pair_two, *refs):
    near, far, outs = refs[: plan.chips], refs[plan.chips : 2 * plan.chips], refs[2 * plan.chips : -2]
    every, corner = refs[-2:]
    collect(plan, near, far, every, corner)
    chip, core = lax.axis_index("sims") // 2, lax.axis_index("sims") % 2
    for step, out in enumerate(outs):
        out[...] = mixed(every, pair_one, pair_two, 2 * (chip ^ step) + core)


def mean_kernel(plan, field_width, pair_one, pair_two, owner, *refs):
    near, far, done = [refs[first * plan.chips : (first + 1) * plan.chips] for first in range(3)]
    mean_field, every, corner, whole = refs[3 * plan.chips :]
    collect(plan, near, far, every, corner)
    chip, core = lax.axis_index("sims") // 2, lax.axis_index("sims") % 2
    whole[...] = jnp.zeros(whole.shape, jnp.float32)
    for step, estimate in enumerate(done):
        sim = 2 * (chip ^ step)
        whole[owner[sim + core]] += estimate[...]
        whole[owner[sim + 1 - core]] += mixed(every, pair_one, pair_two, sim + 1 - core)
    span = pl.ds(pl.multiple_of(core * field_width, lane), field_width) if field_width < plan.share else slice(None)
    for group in range(OWNERS):
        count = jnp.int32(0)
        for sim in range(plan.sim_devices):
            count = count + (owner[sim] == group).astype(jnp.int32)
        mean_field[group] = whole[group, :, span] / jnp.maximum(count, 1).astype(jnp.float32)


def join_kernel(plan, *refs):
    pieces, estimate, sems = refs[: plan.chips], refs[plan.chips], refs[plan.chips + 1]
    copies = []
    for step, piece in enumerate(pieces):
        column = pl.multiple_of(((lax.axis_index("sims") // 2) ^ step) * plan.share, lane)
        copies.append(pltpu.make_async_copy(piece, estimate.at[:, pl.ds(column, plan.share)], sems.at[step]))
        copies[-1].start()
    for copy in copies:
        copy.wait()


def exchange(value, axis, offset):
    count = lax.axis_size(axis)
    return lax.ppermute(value, axis, [(i, i ^ offset) for i in range(count)])


def exchange_all(plan, values):
    return [exchange(value, "rows", step) if step else value for step, value in zip(plan.steps, values)]


def call(kernel, out_shapes, in_specs, scratch, flops, moved, outs_in=pltpu.VMEM):
    return pl.pallas_call(
        kernel,
        out_shape=out_shapes,
        in_specs=in_specs,
        out_specs=[pl.BlockSpec(memory_space=outs_in)] * len(out_shapes),
        scratch_shapes=scratch,
        compiler_params=pltpu.CompilerParams(vmem_limit_bytes=vmem_bytes),
        cost_estimate=pl.CostEstimate(flops=flops, bytes_accessed=moved, transcendentals=0),
    )


def run_filter(plan, sharers, heads, tails, parts, tables):
    vmem = pl.BlockSpec(memory_space=pltpu.VMEM)
    far = pl.BlockSpec(memory_space=pltpu.HBM)
    full = (plan.rows, plan.width)
    tall = (max(plan.rows, plan.row_devices * plan.slab), plan.width)
    return call(
        functools.partial(filter_kernel, plan, sharers),
        [jax.ShapeDtypeStruct((plan.slab, plan.share), jnp.float32)] * plan.row_devices,
        [vmem] * (2 * plan.row_devices) + [far] * len(parts) + [vmem] * len(tables),
        [pltpu.VMEM(full, jnp.float32)] * 5
        + [pltpu.VMEM((plan.row_devices * plan.slab, plan.share), jnp.float32)]
        + [pltpu.VMEM((-(-plan.row_devices * plan.slab // lane) * lane, lane), jnp.float32)]
        + [pltpu.VMEM(full, jnp.bfloat16)] * 2
        + [pltpu.VMEM(tall, jnp.bfloat16)] * 2
        + [pltpu.SemaphoreType.DMA],
        1 << 33,
        1 << 23,
    )(*heads, *tails, *parts, *tables)


def order_of(plan, offset):
    return jnp.where(offset == 0, 0, plan.row_devices - offset)


def run_estimates(plan, pieces, pair_one, pair_two, owner):
    vmem = pl.BlockSpec(memory_space=pltpu.VMEM)
    smem = pl.BlockSpec(memory_space=pltpu.SMEM)
    axes = ("sims", "rows")
    places = [(sim, row) for sim in range(plan.sim_devices) for row in range(plan.row_devices)]

    def f32(*shape):
        return jax.ShapeDtypeStruct(shape, jnp.float32)

    def hop(value, target):
        count = plan.row_devices
        pairs = [(sim * count + row, target(sim, row)[0] * count + target(sim, row)[1]) for sim, row in places]
        return lax.ppermute(value, axes, pairs)

    moved = jnp.stack(exchange_all(plan, pieces))
    here = (lax.axis_index("sims") // 2) ^ lax.axis_index("rows")
    near = []
    for step in range(plan.chips):
        value = lax.dynamic_index_in_dim(moved, order_of(plan, here ^ step), keepdims=False)
        near.append(exchange(value, "sims", 2 * step) if step else value)
    far = [exchange(value, "sims", 1) for value in near]
    scratch = [
        pltpu.VMEM((plan.sim_devices, plan.row_local + 2 * rim, plan.share + lane), jnp.float32),
        pltpu.VMEM((lane, lane), jnp.float32),
    ]
    found = call(
        functools.partial(estimate_kernel, plan),
        [f32(plan.row_local, plan.share)] * plan.chips,
        [smem] * 2 + [vmem] * (2 * plan.chips),
        scratch,
        1 << 24,
        1 << 23,
    )(pair_one, pair_two, *near, *far)
    field_width = plan.columns // plan.sim_devices
    kept = field_width if field_width % lane == 0 else plan.share
    [mean_field] = call(
        functools.partial(mean_kernel, plan, kept),
        [f32(OWNERS, plan.row_local, kept)],
        [smem] * 3 + [vmem] * (3 * plan.chips),
        scratch + [pltpu.VMEM((OWNERS, plan.row_local, plan.share), jnp.float32)],
        1 << 24,
        1 << 23,
    )(pair_one, pair_two, owner, *near, *far, *found)
    if kept != field_width:
        start = (lax.axis_index("sims") % 2) * field_width
        mean_field = lax.dynamic_slice_in_dim(mean_field, start, field_width, axis=2)
    moved = [value if step == 0 else exchange(value, "sims", 2 * step) for step, value in enumerate(found)]
    [estimate] = call(
        functools.partial(join_kernel, plan),
        [f32(plan.row_local, plan.columns)],
        [vmem] * plan.chips,
        [pltpu.SemaphoreType.DMA((plan.chips,))],
        0,
        1 << 20,
        outs_in=pltpu.HBM,
    )(*moved)
    return estimate, mean_field


def body(maps, weight, beam, pair_one, pair_two, owner):
    sim_local, row_local, columns = maps.shape
    taps = beam.shape[0]
    row_devices, sim_devices = lax.axis_size("rows"), lax.axis_size("sims")
    plan = Plan(row_devices, sim_devices, row_local, columns, taps)
    vmem = pl.BlockSpec(memory_space=pltpu.VMEM)
    smem = pl.BlockSpec(memory_space=pltpu.SMEM)
    far = pl.BlockSpec(memory_space=pltpu.HBM)

    def pinned(value):
        return pltpu.with_memory_space_constraint(value, pltpu.HBM)

    def f32(*shape):
        return jax.ShapeDtypeStruct(shape, jnp.float32)

    def b16(*shape):
        return jax.ShapeDtypeStruct(shape, jnp.bfloat16)

    cells = row_local * columns
    made = call(
        functools.partial(piece_kernel, plan),
        [f32(plan.share_rows + plan.head, plan.width)] * row_devices
        + [f32(row_local - plan.head, plan.width)] * row_devices,
        [far, far],
        [pltpu.VMEM((row_local, columns + 2 * plan.halo), jnp.float32)] * 2
        + [pltpu.VMEM((row_local, columns), jnp.float32), pltpu.SemaphoreType.DMA((2, loads))],
        cells,
        16 * cells,
    )(pinned(maps.reshape(row_local, columns)), pinned(weight))
    heads, tails = made[:row_devices], made[row_devices:]
    heads = exchange_all(plan, heads)
    tails, heads = lax.optimization_barrier((tails, heads))
    tails = exchange_all(plan, tails)
    parts = lax.optimization_barrier(jnp.stack([head[: plan.share_rows] for head in heads])[None])
    shapes = [(plan.rows, plan.rows), (row_devices * plan.slab, plan.rows)]
    for block in plan.blocks + plan.out_blocks[:1]:
        low, high = plan.window(block)
        shapes.append((high - low, block[1] - block[0]))
    shapes.append((2 * wide, lane))


    def prepare(parts, beam):
        tables = call(
            functools.partial(table_kernel, plan),
            [b16(*shape) for shape in shapes for _ in range(2)],
            [vmem],
            [pltpu.VMEM((8, lane), jnp.float32)],
            1 << 32,
            1 << 23,
        )(beam[None])
        found = {0: parts}
        for bit in [1 << i for i in range(1, plan.sharers.bit_length() - 1)]:
            found |= {offset | bit: exchange(value, "sims", bit) for offset, value in found.items()}
        sharers[:] = [[offset] for offset in found] + [[offset ^ 1 for offset in found]]
        whole, tables = lax.optimization_barrier((jnp.concatenate(list(found.values())), tables))
        return [*found.values(), exchange(whole, "sims", 1)], tables

    sharers = []
    made = jax.eval_shape(prepare, parts, beam)
    parts, tables = lax.cond(
        lax.axis_index("rows") < row_devices,
        prepare,
        lambda parts, beam: jax.tree.map(lambda x: jnp.zeros(x.shape, x.dtype), made),
        parts,
        beam,
    )
    filtered = run_filter(plan, sharers, heads, tails, parts, tables)
    estimate, mean_field = run_estimates(plan, filtered, pair_one, pair_two, owner)
    return estimate.reshape(maps.shape), mean_field


def solution(mesh):
    in_specs = (P("sims", "rows", None), P("rows", None), P(), P(), P(), P())
    out_specs = (P("sims", "rows", None), P(None, "rows", "sims"))
    return jax.shard_map(body, mesh=mesh, in_specs=in_specs, out_specs=out_specs, check_vma=False)
```

```python
import functools

import jax
import jax.numpy as jnp
from jax import lax
from jax.experimental import pallas as pl
from jax.experimental.pallas import tpu as pltpu
from jax.sharding import PartitionSpec as P

ITERS = 3
OWNERS = 8

ridge_term = 0.5
step_size = 0.6
exact = lax.Precision.HIGHEST
lane = 128
wide = 256
stretch = 1024
rim = 2
loads = 4
vmem_bytes = 48 * 1024 * 1024


def split(value):
    high = value.astype(jnp.bfloat16)
    low = (value - high.astype(jnp.float32)).astype(jnp.bfloat16)
    return high, low


def dot(a, b):
    return jnp.dot(a, b, preferred_element_type=jnp.float32)


class Plan:
    def __init__(self, row_devices, sim_devices, row_local, columns, taps):
        self.row_devices, self.sim_devices = row_devices, sim_devices
        self.row_local, self.columns = row_local, columns
        self.rows = row_devices * row_local
        self.steps = [0, *range(row_devices - 1, 0, -1)]
        self.margin = (taps - 1) // 2
        self.share = columns // row_devices
        self.halo = -(-self.margin * (2 * ITERS + 1) // lane) * lane
        self.width = self.share + 2 * self.halo
        self.slab = row_local + 4 * rim
        self.chips = sim_devices // 2
        self.hops = [0, *sorted(range(1, self.chips), key=lambda offset: -offset.bit_count())]
        self.sharers = min(sim_devices, row_local // 8)
        self.share_rows = row_local // self.sharers
        self.head = row_local // 8
        self.length = max(2 * wide, -(-self.rows // lane) * lane)
        inner = range(lane, self.width - lane, wide)
        blocks = [(0, lane)] + [(a, min(a + wide, self.width - lane)) for a in inner]
        self.blocks = blocks + [(self.width - lane, self.width)]
        centre = range(self.halo, self.halo + self.share, wide)
        self.out_blocks = [(a, min(a + wide, self.halo + self.share)) for a in centre]

    def sides(self):
        left = (self.halo - rim - self.margin) // lane * lane
        return left, (self.halo + self.share - self.margin) // lane * lane

    def window(self, block):
        return max(0, block[0] - lane), min(self.width, block[1] + lane)

    def stage_blocks(self, iteration):
        low = self.halo - self.margin * (2 * (ITERS - 1 - iteration) + 1)
        return [i for i, (a, b) in enumerate(self.blocks) if b > low and a < self.width - low]


def piece_kernel(plan, maps, weight, *refs):
    count = plan.row_devices
    heads, tails = refs[:count], refs[count : 2 * count]
    padded, weights, given, sems = refs[2 * count :]
    rows_at, sims_at = lax.axis_index("rows"), lax.axis_index("sims")
    chunk = plan.row_local // loads
    inner = slice(plan.halo, plan.halo + plan.columns)
    copies = []
    for number in range(loads):
        rows = pl.ds(number * chunk, chunk)
        copies.append((
            pltpu.make_async_copy(weight.at[rows], weights.at[rows, inner], sems.at[0, number]),
            pltpu.make_async_copy(maps.at[rows], given.at[rows], sems.at[1, number]),
        ))
        for copy in copies[-1]:
            copy.start()
    zeros = jnp.zeros((plan.row_local, plan.halo), jnp.float32)
    for target in (padded, weights):
        target[:, : plan.halo] = zeros
        target[:, plan.halo + plan.columns :] = zeros
    for number in range(loads):
        for copy in copies[number]:
            copy.wait()
        rows = slice(number * chunk, (number + 1) * chunk)
        padded[rows, inner] = weights[rows, inner] * given[rows]
    row = pl.multiple_of(lax.rem(sims_at, plan.sharers) * plan.share_rows, plan.share_rows)
    for index, step in enumerate(plan.steps):
        span = pl.ds(pl.multiple_of((rows_at ^ step) * plan.share, lane), plan.width)
        heads[index][: plan.share_rows] = weights[pl.ds(row, plan.share_rows), span]
        heads[index][plan.share_rows :] = padded[: plan.head, span]
        tails[index][...] = padded[plan.head :, span]


def band(plan, taps, rows, columns, offset):
    if offset % plan.length:
        taps = pltpu.roll(taps, offset % plan.length, 1)
    spread = jnp.broadcast_to(taps[:1], (rows, plan.length))
    rolled = pltpu.roll(spread, 0, 1, stride=1, stride_axis=0)[:, :columns]
    row = lax.broadcasted_iota(jnp.int32, (rows, columns), 0)
    column = lax.broadcasted_iota(jnp.int32, (rows, columns), 1)
    return jnp.where(jnp.abs(column - row - offset) <= plan.margin, rolled, 0.0)


def table_kernel(plan, beam, *refs):
    refs, given, line, sem = refs[:-3], *refs[-3:]
    count = beam.shape[1]
    copy = pltpu.make_async_copy(beam, given, sem)
    copy.start()
    line[...] = jnp.zeros(line.shape, jnp.float32)
    copy.wait()
    line[:1, :count] = given[...]
    kernel = line[...]
    kernel = kernel / jnp.sum(kernel[:1], axis=1, keepdims=True)
    size = kernel.shape[1]
    row = lax.broadcasted_iota(jnp.int32, (size, size), 0)
    column = lax.broadcasted_iota(jnp.int32, (size, size), 1)
    mirror = (row + column == count - 1).astype(jnp.float32)
    blank = jnp.zeros((kernel.shape[0], plan.length - size), jnp.float32)

    def centred(values):
        return pltpu.roll(jnp.concatenate([values, blank], axis=1), plan.length - plan.margin, 1)

    taps, reverse = centred(kernel), centred(jnp.dot(kernel, mirror, precision=exact))
    tables = list(refs)

    def put(value):
        high, low = split(value)
        tables.pop(0)[...] = high
        tables.pop(0)[...] = low

    rows = plan.rows
    put(jnp.dot(band(plan, taps, rows, rows, 0), band(plan, reverse, rows, rows, 0), precision=exact))
    slabs = []
    for device in range(plan.row_devices):
        first = device * plan.row_local - rim
        part = band(plan, reverse, plan.slab, rows, first)
        row = lax.broadcasted_iota(jnp.int32, part.shape, 0)
        inside = (row + first >= 0) & (row + first < rows) & (row < plan.row_local + 2 * rim)
        slabs.append(jnp.where(inside, part, 0.0))
    put(jnp.concatenate(slabs, axis=0))
    size = 2 * wide
    forward = band(plan, taps, size, size, 0)
    backward = band(plan, reverse, size, size, 0)[:, lane : lane + wide]
    square = step_size * jnp.dot(forward, backward, precision=exact)
    for block in plan.blocks:
        low, high = plan.window(block)
        first = low - block[0] + lane
        wanted = square[first : first + high - low, : block[1] - block[0]]
        high_term, low_term = tables[0], tables[1]
        put(wanted)
        origin = lax.axis_index("rows") * plan.share - plan.halo + low
        reach = origin + high - low
        cut = ((origin < 0) & (reach > 0)) | ((origin < plan.columns) & (reach > plan.columns))

        @pl.when(cut)
        def _(origin=origin, extent=high - low, first=first, span=block[1] - block[0], terms=(high_term, low_term)):
            column = lax.broadcasted_iota(jnp.int32, (size, size), 1) + (origin - first)
            inside = (column >= 0) & (column < plan.columns)
            value = step_size * jnp.dot(jnp.where(inside, forward, 0.0), backward, precision=exact)
            high_part, low_part = split(value[first : first + extent, :span])
            terms[0][...] = high_part
            terms[1][...] = low_part

    for block in plan.out_blocks[:1]:
        low, high = plan.window(block)
        put(step_size * forward[: high - low, block[0] - low : block[1] - low])
    left, right = plan.sides()
    column = lax.broadcasted_iota(jnp.int32, (wide, lane), 1)
    before = band(plan, taps, wide, lane, left - (plan.halo - lane))
    behind = band(plan, taps, wide, lane, right - (plan.halo + plan.share))
    rows_at = lax.axis_index("rows")
    before = jnp.where((column >= lane - rim) & (rows_at > 0), before, 0.0)
    behind = jnp.where((column < rim) & (rows_at < plan.row_devices - 1), behind, 0.0)
    put(step_size * jnp.concatenate([before, behind], axis=0))


def filter_kernel(plan, sharers, *refs):
    refs = list(refs)

    def take(number):
        taken = refs[:number]
        del refs[:number]
        return taken

    heads, tails = take(plan.row_devices), take(plan.row_devices)
    parts = take(len(sharers))
    square, final = take(2), take(2)
    bands = [take(2) for _ in plan.blocks]
    last, edges = take(2), take(2)
    outs = take(plan.row_devices)
    seen, weight, image, base, total, field, side, high, low, mid_high, mid_low, shares, sem = refs
    first = 0
    for part in parts:
        pltpu.make_async_copy(part, shares.at[pl.ds(first, part.shape[0])], sem).start()
        first += part.shape[0]
    for index, step in enumerate(plan.steps):
        row = pl.multiple_of((lax.axis_index("rows") ^ step) * plan.row_local, plan.row_local)
        rows = pl.ds(row, plan.row_local)
        value = jnp.concatenate([heads[index][plan.share_rows :], tails[index][...]], axis=0)
        seen[rows, :] = value
        high[rows, :], low[rows, :] = split(value)

    def rows_pass(table, start, stop, full=True):
        count = table[0].shape[0]
        for a in range(start, stop, wide):
            b = min(a + wide, stop)
            value = dot(table[0][...], high[:, a:b]) + dot(table[1][...], high[:, a:b])
            if full:
                value = value + dot(table[0][...], low[:, a:b])
                mid_high[:count, a:b], mid_low[:count, a:b] = split(value)
            else:
                mid_high[:count, a:b] = value.astype(jnp.bfloat16)

    def columns_pass(table, count, window, full=True):
        a, b = window
        value = dot(mid_high[:count, a:b], table[0][...]) + dot(mid_high[:count, a:b], table[1][...])
        return value + dot(mid_low[:count, a:b], table[0][...]) if full else value

    keep = 1.0 - step_size * ridge_term
    for iteration in range(ITERS):
        chosen = plan.stage_blocks(iteration)
        windows = [plan.window(plan.blocks[i]) for i in chosen]
        rows_pass(square, windows[0][0], windows[-1][1], iteration == 0)
        if iteration == 0:
            for i, window in zip(chosen, windows):
                base[:, slice(*plan.blocks[i])] = columns_pass(bands[i], plan.rows, window)
            pltpu.make_async_copy(shares, shares, sem).wait()
            for slot, offset in enumerate(offset for owners in sharers for offset in owners):
                for index, step in enumerate(plan.steps):
                    row = (lax.axis_index("rows") ^ step) * plan.row_local
                    row = row + (lax.rem(lax.axis_index("sims"), plan.sharers) ^ offset) * plan.share_rows
                    weight[pl.ds(pl.multiple_of(row, plan.share_rows), plan.share_rows), :] = shares[slot, index]
        for i, window in zip(chosen, windows):
            a, b = plan.blocks[i]
            value = base[:, a:b]
            if iteration > 0:
                value = keep * image[:, a:b] + value - columns_pass(bands[i], plan.rows, window, False)
            image[:, a:b] = value
            product = weight[:, a:b] * value
            given = seen[:, a:b]
            total[:, a:b] = given - product + keep * (total[:, a:b] if iteration > 0 else given)
            high[:, a:b] = product.astype(jnp.bfloat16)
    first, stop = plan.window(plan.out_blocks[0])[0], plan.window(plan.out_blocks[-1])[1]
    high[:, first:stop], low[:, first:stop] = split(total[:, first:stop])
    rows_pass(final, first, stop)
    count = plan.row_devices * plan.slab
    for block in plan.out_blocks:
        size = block[1] - block[0]
        field[:, block[0] - plan.halo : block[1] - plan.halo] = columns_pass(last, count, plan.window(block))
    value = jnp.zeros((count, lane), jnp.float32)
    for number, start in enumerate(plan.sides()):
        part = slice(number * wide, (number + 1) * wide)
        a, b = mid_high[:count, start : start + wide], mid_low[:count, start : start + wide]
        value = value + dot(a, edges[0][part]) + dot(a, edges[1][part]) + dot(b, edges[0][part])
    side[:count] = value
    turned = side[...].T
    turned = jnp.concatenate([turned[lane - rim :], turned[:rim]], axis=0)
    for device in range(plan.row_devices):
        shift = (side.shape[0] - device * plan.slab - rim) % side.shape[0]
        row = (device + 1) * plan.slab - 2 * rim
        field[row : row + 2 * rim, :lane] = pltpu.roll(turned, shift, 1)[:, :lane]
    for step, out in zip(plan.steps, outs):
        row = pl.multiple_of((lax.axis_index("rows") ^ step) * plan.slab, 8)
        out[...] = field[pl.ds(row, plan.slab), :]


def divergence(own, partner):
    rows, columns = own.shape
    stop, inner = rows - rim, slice(0, columns - lane)
    here = partner[rim:stop]
    down, up = partner[2 * rim :, inner], partner[: stop - rim, inner]
    middle = here[:, inner]
    flow = own[rim + 1 : stop + 1, inner] * (down - middle) - own[rim - 1 : stop - 1, inner] * (middle - up)
    level = own[rim:stop]

    def shifted(value, amount):
        return pltpu.roll(value, amount % columns, 1)[:, inner]

    right = shifted(level, -1) * (shifted(here, -2) - middle)
    left = shifted(level, 1) * (middle - shifted(here, 2))
    return 0.25 * (flow + (right - left))


def collect(plan, near, far, every, corner):
    core = lax.axis_index("sims") % 2
    here = lax.axis_index("sims") // 2
    corner[...] = jnp.zeros(corner.shape, jnp.float32)
    kept = plan.row_local + 2 * rim
    for index, step in enumerate(plan.hops):
        for source, parity in ((near[index], core), (far[index], 1 - core)):
            at = 2 * (here ^ step) + parity
            every[at, :, : plan.share] = source[:kept]
            corner[lane - rim :] = source[kept : kept + rim, :lane]
            corner[:rim] = source[kept + rim : kept + 2 * rim, :lane]
            every[at, rim : kept - rim, plan.share :] = corner[...].T[: plan.row_local]


def mixed(every, pair_one, pair_two, sim):
    return divergence(every[sim], 2.0 * every[pair_one[sim]] - every[pair_two[sim]])


def estimate_kernel(plan, pair_one, pair_two, *refs):
    near, far, outs = refs[: plan.chips], refs[plan.chips : 2 * plan.chips], refs[2 * plan.chips : -2]
    every, corner = refs[-2:]
    collect(plan, near, far, every, corner)
    chip, core = lax.axis_index("sims") // 2, lax.axis_index("sims") % 2
    for step, out in zip(plan.hops, outs):
        out[...] = mixed(every, pair_one, pair_two, 2 * (chip ^ step) + core)


def mean_kernel(plan, field_width, pair_one, pair_two, owner, *refs):
    near, far, done = [refs[first * plan.chips : (first + 1) * plan.chips] for first in range(3)]
    mean_field, every, corner, whole = refs[3 * plan.chips :]
    collect(plan, near, far, every, corner)
    chip, core = lax.axis_index("sims") // 2, lax.axis_index("sims") % 2
    whole[...] = jnp.zeros(whole.shape, jnp.float32)
    for step, estimate in zip(plan.hops, done):
        sim = 2 * (chip ^ step)
        whole[owner[sim + core]] += estimate[...]
        whole[owner[sim + 1 - core]] += mixed(every, pair_one, pair_two, sim + 1 - core)
    span = pl.ds(pl.multiple_of(core * field_width, lane), field_width) if field_width < plan.share else slice(None)
    for group in range(OWNERS):
        count = jnp.int32(0)
        for sim in range(plan.sim_devices):
            count = count + (owner[sim] == group).astype(jnp.int32)
        mean_field[group] = whole[group, :, span] / jnp.maximum(count, 1).astype(jnp.float32)


def join_kernel(plan, *refs):
    pieces, estimate, sems = refs[: plan.chips], refs[plan.chips], refs[plan.chips + 1]
    copies = []
    for step, piece in zip(plan.hops, pieces):
        column = pl.multiple_of(((lax.axis_index("sims") // 2) ^ step) * plan.share, lane)
        copies.append(pltpu.make_async_copy(piece, estimate.at[:, pl.ds(column, plan.share)], sems.at[step]))
        copies[-1].start()
    for copy in copies:
        copy.wait()


def exchange(value, axis, offset):
    count = lax.axis_size(axis)
    return lax.ppermute(value, axis, [(i, i ^ offset) for i in range(count)])


def exchange_all(plan, values):
    return [exchange(value, "rows", step) if step else value for step, value in zip(plan.steps, values)]


def call(kernel, out_shapes, in_specs, scratch, flops, moved, outs_in=pltpu.VMEM):
    return pl.pallas_call(
        kernel,
        out_shape=out_shapes,
        in_specs=in_specs,
        out_specs=[pl.BlockSpec(memory_space=outs_in)] * len(out_shapes),
        scratch_shapes=scratch,
        compiler_params=pltpu.CompilerParams(vmem_limit_bytes=vmem_bytes),
        cost_estimate=pl.CostEstimate(flops=flops, bytes_accessed=moved, transcendentals=0),
    )


def run_filter(plan, sharers, heads, tails, parts, tables):
    vmem = pl.BlockSpec(memory_space=pltpu.VMEM)
    far = pl.BlockSpec(memory_space=pltpu.HBM)
    full = (plan.rows, plan.width)
    tall = (max(plan.rows, plan.row_devices * plan.slab), plan.width)
    return call(
        functools.partial(filter_kernel, plan, sharers),
        [jax.ShapeDtypeStruct((plan.slab, plan.share), jnp.float32)] * plan.row_devices,
        [vmem] * (2 * plan.row_devices) + [far] * len(parts) + [vmem] * len(tables),
        [pltpu.VMEM(full, jnp.float32)] * 5
        + [pltpu.VMEM((plan.row_devices * plan.slab, plan.share), jnp.float32)]
        + [pltpu.VMEM((-(-plan.row_devices * plan.slab // lane) * lane, lane), jnp.float32)]
        + [pltpu.VMEM(full, jnp.bfloat16)] * 2
        + [pltpu.VMEM(tall, jnp.bfloat16)] * 2
        + [pltpu.VMEM((plan.sharers, plan.row_devices, plan.share_rows, plan.width), jnp.float32)]
        + [pltpu.SemaphoreType.DMA],
        1 << 33,
        1 << 23,
    )(*heads, *tails, *parts, *tables)


def order_of(plan, offset):
    return jnp.where(offset == 0, 0, plan.row_devices - offset)


def run_estimates(plan, pieces, pair_one, pair_two, owner):
    vmem = pl.BlockSpec(memory_space=pltpu.VMEM)
    smem = pl.BlockSpec(memory_space=pltpu.SMEM)
    axes = ("sims", "rows")
    places = [(sim, row) for sim in range(plan.sim_devices) for row in range(plan.row_devices)]

    def f32(*shape):
        return jax.ShapeDtypeStruct(shape, jnp.float32)

    def hop(value, target):
        count = plan.row_devices
        pairs = [(sim * count + row, target(sim, row)[0] * count + target(sim, row)[1]) for sim, row in places]
        return lax.ppermute(value, axes, pairs)

    moved = jnp.stack(exchange_all(plan, pieces))
    here = (lax.axis_index("sims") // 2) ^ lax.axis_index("rows")
    near = []
    for step in plan.hops:
        value = lax.dynamic_index_in_dim(moved, order_of(plan, here ^ step), keepdims=False)
        near.append(exchange(value, "sims", 2 * step) if step else value)
    far = [exchange(value, "sims", 1) for value in near]
    scratch = [
        pltpu.VMEM((plan.sim_devices, plan.row_local + 2 * rim, plan.share + lane), jnp.float32),
        pltpu.VMEM((lane, lane), jnp.float32),
    ]
    found = call(
        functools.partial(estimate_kernel, plan),
        [f32(plan.row_local, plan.share)] * plan.chips,
        [smem] * 2 + [vmem] * (2 * plan.chips),
        scratch,
        1 << 24,
        1 << 23,
    )(pair_one, pair_two, *near, *far)
    field_width = plan.columns // plan.sim_devices
    kept = field_width if field_width % lane == 0 else plan.share
    [mean_field] = call(
        functools.partial(mean_kernel, plan, kept),
        [f32(OWNERS, plan.row_local, kept)],
        [smem] * 3 + [vmem] * (3 * plan.chips),
        scratch + [pltpu.VMEM((OWNERS, plan.row_local, plan.share), jnp.float32)],
        1 << 24,
        1 << 23,
    )(pair_one, pair_two, owner, *near, *far, *found)
    if kept != field_width:
        start = (lax.axis_index("sims") % 2) * field_width
        mean_field = lax.dynamic_slice_in_dim(mean_field, start, field_width, axis=2)
    moved = [exchange(value, "sims", 2 * step) if step else value for step, value in zip(plan.hops, found)]
    [estimate] = call(
        functools.partial(join_kernel, plan),
        [f32(plan.row_local, plan.columns)],
        [vmem] * plan.chips,
        [pltpu.SemaphoreType.DMA((plan.chips,))],
        0,
        1 << 20,
        outs_in=pltpu.HBM,
    )(*moved)
    return estimate, mean_field


def body(maps, weight, beam, pair_one, pair_two, owner):
    sim_local, row_local, columns = maps.shape
    taps = beam.shape[0]
    row_devices, sim_devices = lax.axis_size("rows"), lax.axis_size("sims")
    plan = Plan(row_devices, sim_devices, row_local, columns, taps)
    vmem = pl.BlockSpec(memory_space=pltpu.VMEM)
    smem = pl.BlockSpec(memory_space=pltpu.SMEM)
    far = pl.BlockSpec(memory_space=pltpu.HBM)

    def pinned(value):
        return pltpu.with_memory_space_constraint(value, pltpu.HBM)

    def f32(*shape):
        return jax.ShapeDtypeStruct(shape, jnp.float32)

    def b16(*shape):
        return jax.ShapeDtypeStruct(shape, jnp.bfloat16)

    cells = row_local * columns
    made = call(
        functools.partial(piece_kernel, plan),
        [f32(plan.share_rows + plan.head, plan.width)] * row_devices
        + [f32(row_local - plan.head, plan.width)] * row_devices,
        [far, far],
        [pltpu.VMEM((row_local, columns + 2 * plan.halo), jnp.float32)] * 2
        + [pltpu.VMEM((row_local, columns), jnp.float32), pltpu.SemaphoreType.DMA((2, loads))],
        cells,
        16 * cells,
    )(pinned(maps.reshape(row_local, columns)), pinned(weight))
    heads, tails = made[:row_devices], made[row_devices:]
    heads = exchange_all(plan, heads)
    tails, heads = lax.optimization_barrier((tails, heads))
    tails = exchange_all(plan, tails)
    parts = lax.optimization_barrier(jnp.stack([head[: plan.share_rows] for head in heads])[None])
    shapes = [(plan.rows, plan.rows), (row_devices * plan.slab, plan.rows)]
    for block in plan.blocks + plan.out_blocks[:1]:
        low, high = plan.window(block)
        shapes.append((high - low, block[1] - block[0]))
    shapes.append((2 * wide, lane))


    def prepare(parts, beam):
        tables = call(
            functools.partial(table_kernel, plan),
            [b16(*shape) for shape in shapes for _ in range(2)],
            [far],
            [pltpu.VMEM((1, taps), jnp.float32), pltpu.VMEM((8, lane), jnp.float32), pltpu.SemaphoreType.DMA],
            1 << 32,
            1 << 23,
        )(pinned(beam))
        found = {0: parts}
        for bit in [1 << i for i in range(1, plan.sharers.bit_length() - 1)]:
            found |= {offset | bit: exchange(value, "sims", bit) for offset, value in found.items()}
        sharers[:] = [[offset] for offset in found] + [[offset ^ 1 for offset in found]]
        whole, tables = lax.optimization_barrier((jnp.concatenate(list(found.values())), tables))
        return [*found.values(), exchange(whole, "sims", 1)], tables

    sharers = []
    made = jax.eval_shape(prepare, parts, beam[None])
    parts, tables = lax.cond(
        lax.axis_index("rows") < row_devices,
        prepare,
        lambda parts, beam: jax.tree.map(lambda x: jnp.zeros(x.shape, x.dtype), made),
        parts,
        beam[None],
    )
    filtered = run_filter(plan, sharers, heads, tails, parts, tables)
    estimate, mean_field = run_estimates(plan, filtered, pair_one, pair_two, owner)
    return estimate.reshape(maps.shape), mean_field


def solution(mesh):
    in_specs = (P("sims", "rows", None), P("rows", None), P(), P(), P(), P())
    out_specs = (P("sims", "rows", None), P(None, "rows", "sims"))
    return jax.shard_map(body, mesh=mesh, in_specs=in_specs, out_specs=out_specs, check_vma=False)
```

```python
import functools

import jax
import jax.numpy as jnp
from jax import lax
from jax.experimental import pallas as pl
from jax.experimental.pallas import tpu as pltpu
from jax.sharding import PartitionSpec as P

ITERS = 3
OWNERS = 8

ridge_term = 0.5
step_size = 0.6
exact = lax.Precision.HIGHEST
lane = 128
wide = 256
stretch = 1024
rim = 2
loads = 7
vmem_bytes = 48 * 1024 * 1024


def split(value):
    high = value.astype(jnp.bfloat16)
    low = (value - high.astype(jnp.float32)).astype(jnp.bfloat16)
    return high, low


def dot(a, b):
    return jnp.dot(a, b, preferred_element_type=jnp.float32)


class Plan:
    def __init__(self, row_devices, sim_devices, row_local, columns, taps):
        self.row_devices, self.sim_devices = row_devices, sim_devices
        self.row_local, self.columns = row_local, columns
        self.rows = row_devices * row_local
        self.steps = [0, *range(row_devices - 1, 0, -1)]
        self.margin = (taps - 1) // 2
        self.share = columns // row_devices
        self.halo = -(-self.margin * (2 * ITERS + 1) // lane) * lane
        self.width = self.share + 2 * self.halo
        self.slab = row_local + 4 * rim
        self.chips = sim_devices // 2
        self.hops = [0, *sorted(range(1, self.chips), key=lambda offset: -offset.bit_count())]
        self.sharers = min(sim_devices, row_local // 8)
        self.share_rows = row_local // self.sharers
        self.head = row_local // 8
        self.length = max(2 * wide, -(-self.rows // lane) * lane)
        inner = range(lane, self.width - lane, wide)
        blocks = [(0, lane)] + [(a, min(a + wide, self.width - lane)) for a in inner]
        self.blocks = blocks + [(self.width - lane, self.width)]
        centre = range(self.halo, self.halo + self.share, wide)
        self.out_blocks = [(a, min(a + wide, self.halo + self.share)) for a in centre]

    def sides(self):
        left = (self.halo - rim - self.margin) // lane * lane
        return left, (self.halo + self.share - self.margin) // lane * lane

    def window(self, block):
        return max(0, block[0] - lane), min(self.width, block[1] + lane)

    def stage_blocks(self, iteration):
        low = self.halo - self.margin * (2 * (ITERS - 1 - iteration) + 1)
        return [i for i, (a, b) in enumerate(self.blocks) if b > low and a < self.width - low]


def spread_out(plan, padded, outs, first, rows):
    for step, out in zip(plan.steps, outs):
        column = pl.multiple_of((lax.axis_index("rows") ^ step) * plan.share, lane)
        out[first : first + rows.size] = padded[rows, pl.ds(column, plan.width)]


def clear_sides(plan, padded):
    zeros = jnp.zeros((padded.shape[0], plan.halo), jnp.float32)
    padded[:, : plan.halo] = zeros
    padded[:, plan.halo + plan.columns :] = zeros


def head_kernel(plan, maps, weight, *refs):
    heads = refs[: plan.row_devices]
    share, padded, given, sems = refs[plan.row_devices :]
    row = pl.multiple_of(lax.rem(lax.axis_index("sims"), plan.sharers) * plan.share_rows, plan.share_rows)
    inner = slice(plan.halo, plan.halo + plan.columns)
    copies = [
        pltpu.make_async_copy(weight.at[pl.ds(row, plan.share_rows)], share.at[:, inner], sems.at[0]),
        pltpu.make_async_copy(weight.at[: plan.head], padded.at[:, inner], sems.at[1]),
        pltpu.make_async_copy(maps.at[: plan.head], given, sems.at[2]),
    ]
    for copy in copies:
        copy.start()
    clear_sides(plan, share)
    clear_sides(plan, padded)
    for copy in copies:
        copy.wait()
    padded[:, inner] = padded[:, inner] * given[...]
    spread_out(plan, share, heads, 0, pl.ds(0, plan.share_rows))
    spread_out(plan, padded, heads, plan.share_rows, pl.ds(0, plan.head))


def tail_kernel(plan, maps, weight, *refs):
    tails = refs[: plan.row_devices]
    padded, given, sems = refs[plan.row_devices :]
    inner = slice(plan.halo, plan.halo + plan.columns)
    chunk = (plan.row_local - plan.head) // loads
    copies = []
    for number in range(loads):
        rows, source = pl.ds(number * chunk, chunk), pl.ds(plan.head + number * chunk, chunk)
        copies.append((
            pltpu.make_async_copy(weight.at[source], padded.at[rows, inner], sems.at[0, number]),
            pltpu.make_async_copy(maps.at[source], given.at[rows], sems.at[1, number]),
        ))
        for copy in copies[-1]:
            copy.start()
    clear_sides(plan, padded)
    for number in range(loads):
        for copy in copies[number]:
            copy.wait()
        rows = pl.ds(number * chunk, chunk)
        padded[rows, inner] = padded[rows, inner] * given[rows]
        spread_out(plan, padded, tails, number * chunk, rows)


def band(plan, taps, rows, columns, offset):
    if offset % plan.length:
        taps = pltpu.roll(taps, offset % plan.length, 1)
    spread = jnp.broadcast_to(taps[:1], (rows, plan.length))
    rolled = pltpu.roll(spread, 0, 1, stride=1, stride_axis=0)[:, :columns]
    row = lax.broadcasted_iota(jnp.int32, (rows, columns), 0)
    column = lax.broadcasted_iota(jnp.int32, (rows, columns), 1)
    return jnp.where(jnp.abs(column - row - offset) <= plan.margin, rolled, 0.0)


def table_kernel(plan, beam, *refs):
    refs, given, line, sem = refs[:-3], *refs[-3:]
    count = beam.shape[1]
    copy = pltpu.make_async_copy(beam, given, sem)
    copy.start()
    line[...] = jnp.zeros(line.shape, jnp.float32)
    copy.wait()
    line[:1, :count] = given[...]
    kernel = line[...]
    kernel = kernel / jnp.sum(kernel[:1], axis=1, keepdims=True)
    size = kernel.shape[1]
    row = lax.broadcasted_iota(jnp.int32, (size, size), 0)
    column = lax.broadcasted_iota(jnp.int32, (size, size), 1)
    mirror = (row + column == count - 1).astype(jnp.float32)
    blank = jnp.zeros((kernel.shape[0], plan.length - size), jnp.float32)

    def centred(values):
        return pltpu.roll(jnp.concatenate([values, blank], axis=1), plan.length - plan.margin, 1)

    taps, reverse = centred(kernel), centred(jnp.dot(kernel, mirror, precision=exact))
    tables = list(refs)

    def put(value):
        high, low = split(value)
        tables.pop(0)[...] = high
        tables.pop(0)[...] = low

    rows = plan.rows
    put(jnp.dot(band(plan, taps, rows, rows, 0), band(plan, reverse, rows, rows, 0), precision=exact))
    slabs = []
    for device in range(plan.row_devices):
        first = device * plan.row_local - rim
        part = band(plan, reverse, plan.slab, rows, first)
        row = lax.broadcasted_iota(jnp.int32, part.shape, 0)
        inside = (row + first >= 0) & (row + first < rows) & (row < plan.row_local + 2 * rim)
        slabs.append(jnp.where(inside, part, 0.0))
    put(jnp.concatenate(slabs, axis=0))
    size = 2 * wide
    forward = band(plan, taps, size, size, 0)
    backward = band(plan, reverse, size, size, 0)[:, lane : lane + wide]
    square = step_size * jnp.dot(forward, backward, precision=exact)
    for block in plan.blocks:
        low, high = plan.window(block)
        first = low - block[0] + lane
        wanted = square[first : first + high - low, : block[1] - block[0]]
        high_term, low_term = tables[0], tables[1]
        put(wanted)
        origin = lax.axis_index("rows") * plan.share - plan.halo + low
        reach = origin + high - low
        cut = ((origin < 0) & (reach > 0)) | ((origin < plan.columns) & (reach > plan.columns))

        @pl.when(cut)
        def _(origin=origin, extent=high - low, first=first, span=block[1] - block[0], terms=(high_term, low_term)):
            column = lax.broadcasted_iota(jnp.int32, (size, size), 1) + (origin - first)
            inside = (column >= 0) & (column < plan.columns)
            value = step_size * jnp.dot(jnp.where(inside, forward, 0.0), backward, precision=exact)
            high_part, low_part = split(value[first : first + extent, :span])
            terms[0][...] = high_part
            terms[1][...] = low_part

    for block in plan.out_blocks[:1]:
        low, high = plan.window(block)
        put(step_size * forward[: high - low, block[0] - low : block[1] - low])
    left, right = plan.sides()
    column = lax.broadcasted_iota(jnp.int32, (wide, lane), 1)
    before = band(plan, taps, wide, lane, left - (plan.halo - lane))
    behind = band(plan, taps, wide, lane, right - (plan.halo + plan.share))
    rows_at = lax.axis_index("rows")
    before = jnp.where((column >= lane - rim) & (rows_at > 0), before, 0.0)
    behind = jnp.where((column < rim) & (rows_at < plan.row_devices - 1), behind, 0.0)
    put(step_size * jnp.concatenate([before, behind], axis=0))


def filter_kernel(plan, sharers, *refs):
    refs = list(refs)

    def take(number):
        taken = refs[:number]
        del refs[:number]
        return taken

    heads, tails = take(plan.row_devices), take(plan.row_devices)
    parts = take(len(sharers))
    square, final = take(2), take(2)
    bands = [take(2) for _ in plan.blocks]
    last, edges = take(2), take(2)
    outs = take(plan.row_devices)
    seen, weight, image, base, total, field, side, high, low, mid_high, mid_low, shares, sem = refs
    first = 0
    for part in parts:
        pltpu.make_async_copy(part, shares.at[pl.ds(first, part.shape[0])], sem).start()
        first += part.shape[0]
    for index, step in enumerate(plan.steps):
        row = pl.multiple_of((lax.axis_index("rows") ^ step) * plan.row_local, plan.row_local)
        rows = pl.ds(row, plan.row_local)
        value = jnp.concatenate([heads[index][plan.share_rows :], tails[index][...]], axis=0)
        seen[rows, :] = value
        high[rows, :], low[rows, :] = split(value)

    def rows_pass(table, start, stop, full=True):
        count = table[0].shape[0]
        for a in range(start, stop, wide):
            b = min(a + wide, stop)
            value = dot(table[0][...], high[:, a:b]) + dot(table[1][...], high[:, a:b])
            if full:
                value = value + dot(table[0][...], low[:, a:b])
                mid_high[:count, a:b], mid_low[:count, a:b] = split(value)
            else:
                mid_high[:count, a:b] = value.astype(jnp.bfloat16)

    def columns_pass(table, count, window, full=True):
        a, b = window
        value = dot(mid_high[:count, a:b], table[0][...]) + dot(mid_high[:count, a:b], table[1][...])
        return value + dot(mid_low[:count, a:b], table[0][...]) if full else value

    keep = 1.0 - step_size * ridge_term
    for iteration in range(ITERS):
        chosen = plan.stage_blocks(iteration)
        windows = [plan.window(plan.blocks[i]) for i in chosen]
        rows_pass(square, windows[0][0], windows[-1][1], iteration == 0)
        if iteration == 0:
            for i, window in zip(chosen, windows):
                base[:, slice(*plan.blocks[i])] = columns_pass(bands[i], plan.rows, window)
            pltpu.make_async_copy(shares, shares, sem).wait()
            for slot, offset in enumerate(offset for owners in sharers for offset in owners):
                for index, step in enumerate(plan.steps):
                    row = (lax.axis_index("rows") ^ step) * plan.row_local
                    row = row + (lax.rem(lax.axis_index("sims"), plan.sharers) ^ offset) * plan.share_rows
                    weight[pl.ds(pl.multiple_of(row, plan.share_rows), plan.share_rows), :] = shares[slot, index]
        for i, window in zip(chosen, windows):
            a, b = plan.blocks[i]
            value = base[:, a:b]
            if iteration > 0:
                value = keep * image[:, a:b] + value - columns_pass(bands[i], plan.rows, window, False)
            image[:, a:b] = value
            product = weight[:, a:b] * value
            given = seen[:, a:b]
            total[:, a:b] = given - product + keep * (total[:, a:b] if iteration > 0 else given)
            high[:, a:b] = product.astype(jnp.bfloat16)
    first, stop = plan.window(plan.out_blocks[0])[0], plan.window(plan.out_blocks[-1])[1]
    high[:, first:stop], low[:, first:stop] = split(total[:, first:stop])
    rows_pass(final, first, stop)
    count = plan.row_devices * plan.slab
    for block in plan.out_blocks:
        size = block[1] - block[0]
        field[:, block[0] - plan.halo : block[1] - plan.halo] = columns_pass(last, count, plan.window(block))
    value = jnp.zeros((count, lane), jnp.float32)
    for number, start in enumerate(plan.sides()):
        part = slice(number * wide, (number + 1) * wide)
        a, b = mid_high[:count, start : start + wide], mid_low[:count, start : start + wide]
        value = value + dot(a, edges[0][part]) + dot(a, edges[1][part]) + dot(b, edges[0][part])
    side[:count] = value
    turned = side[...].T
    turned = jnp.concatenate([turned[lane - rim :], turned[:rim]], axis=0)
    for device in range(plan.row_devices):
        shift = (side.shape[0] - device * plan.slab - rim) % side.shape[0]
        row = (device + 1) * plan.slab - 2 * rim
        field[row : row + 2 * rim, :lane] = pltpu.roll(turned, shift, 1)[:, :lane]
    for step, out in zip(plan.steps, outs):
        row = pl.multiple_of((lax.axis_index("rows") ^ step) * plan.slab, 8)
        out[...] = field[pl.ds(row, plan.slab), :]


def divergence(own, partner):
    rows, columns = own.shape
    stop, inner = rows - rim, slice(0, columns - lane)
    here = partner[rim:stop]
    down, up = partner[2 * rim :, inner], partner[: stop - rim, inner]
    middle = here[:, inner]
    flow = own[rim + 1 : stop + 1, inner] * (down - middle) - own[rim - 1 : stop - 1, inner] * (middle - up)
    level = own[rim:stop]

    def shifted(value, amount):
        return pltpu.roll(value, amount % columns, 1)[:, inner]

    right = shifted(level, -1) * (shifted(here, -2) - middle)
    left = shifted(level, 1) * (middle - shifted(here, 2))
    return 0.25 * (flow + (right - left))


def collect(plan, near, far, every, corner):
    core = lax.axis_index("sims") % 2
    here = lax.axis_index("sims") // 2
    corner[...] = jnp.zeros(corner.shape, jnp.float32)
    kept = plan.row_local + 2 * rim
    for index, step in enumerate(plan.hops):
        for source, parity in ((near[index], core), (far[index], 1 - core)):
            at = 2 * (here ^ step) + parity
            every[at, :, : plan.share] = source[:kept]
            corner[lane - rim :] = source[kept : kept + rim, :lane]
            corner[:rim] = source[kept + rim : kept + 2 * rim, :lane]
            every[at, rim : kept - rim, plan.share :] = corner[...].T[: plan.row_local]


def mixed(every, pair_one, pair_two, sim):
    return divergence(every[sim], 2.0 * every[pair_one[sim]] - every[pair_two[sim]])


def estimate_kernel(plan, pair_one, pair_two, *refs):
    near, far, outs = refs[: plan.chips], refs[plan.chips : 2 * plan.chips], refs[2 * plan.chips : -2]
    every, corner = refs[-2:]
    collect(plan, near, far, every, corner)
    chip, core = lax.axis_index("sims") // 2, lax.axis_index("sims") % 2
    for step, out in zip(plan.hops, outs):
        out[...] = mixed(every, pair_one, pair_two, 2 * (chip ^ step) + core)


def mean_kernel(plan, field_width, pair_one, pair_two, owner, *refs):
    near, far, done = [refs[first * plan.chips : (first + 1) * plan.chips] for first in range(3)]
    mean_field, every, corner, whole = refs[3 * plan.chips :]
    collect(plan, near, far, every, corner)
    chip, core = lax.axis_index("sims") // 2, lax.axis_index("sims") % 2
    whole[...] = jnp.zeros(whole.shape, jnp.float32)
    for step, estimate in zip(plan.hops, done):
        sim = 2 * (chip ^ step)
        whole[owner[sim + core]] += estimate[...]
        whole[owner[sim + 1 - core]] += mixed(every, pair_one, pair_two, sim + 1 - core)
    span = pl.ds(pl.multiple_of(core * field_width, lane), field_width) if field_width < plan.share else slice(None)
    for group in range(OWNERS):
        count = jnp.int32(0)
        for sim in range(plan.sim_devices):
            count = count + (owner[sim] == group).astype(jnp.int32)
        mean_field[group] = whole[group, :, span] / jnp.maximum(count, 1).astype(jnp.float32)


def join_kernel(plan, *refs):
    pieces, estimate, sems = refs[: plan.chips], refs[plan.chips], refs[plan.chips + 1]
    copies = []
    for step, piece in zip(plan.hops, pieces):
        column = pl.multiple_of(((lax.axis_index("sims") // 2) ^ step) * plan.share, lane)
        copies.append(pltpu.make_async_copy(piece, estimate.at[:, pl.ds(column, plan.share)], sems.at[step]))
        copies[-1].start()
    for copy in copies:
        copy.wait()


def exchange(value, axis, offset):
    count = lax.axis_size(axis)
    return lax.ppermute(value, axis, [(i, i ^ offset) for i in range(count)])


def exchange_all(plan, values):
    return [exchange(value, "rows", step) if step else value for step, value in zip(plan.steps, values)]


def call(kernel, out_shapes, in_specs, scratch, flops, moved, outs_in=pltpu.VMEM):
    return pl.pallas_call(
        kernel,
        out_shape=out_shapes,
        in_specs=in_specs,
        out_specs=[pl.BlockSpec(memory_space=outs_in)] * len(out_shapes),
        scratch_shapes=scratch,
        compiler_params=pltpu.CompilerParams(vmem_limit_bytes=vmem_bytes),
        cost_estimate=pl.CostEstimate(flops=flops, bytes_accessed=moved, transcendentals=0),
    )


def run_filter(plan, sharers, heads, tails, parts, tables):
    vmem = pl.BlockSpec(memory_space=pltpu.VMEM)
    far = pl.BlockSpec(memory_space=pltpu.HBM)
    full = (plan.rows, plan.width)
    tall = (max(plan.rows, plan.row_devices * plan.slab), plan.width)
    return call(
        functools.partial(filter_kernel, plan, sharers),
        [jax.ShapeDtypeStruct((plan.slab, plan.share), jnp.float32)] * plan.row_devices,
        [vmem] * (2 * plan.row_devices) + [far] * len(parts) + [vmem] * len(tables),
        [pltpu.VMEM(full, jnp.float32)] * 5
        + [pltpu.VMEM((plan.row_devices * plan.slab, plan.share), jnp.float32)]
        + [pltpu.VMEM((-(-plan.row_devices * plan.slab // lane) * lane, lane), jnp.float32)]
        + [pltpu.VMEM(full, jnp.bfloat16)] * 2
        + [pltpu.VMEM(tall, jnp.bfloat16)] * 2
        + [pltpu.VMEM((plan.sharers, plan.row_devices, plan.share_rows, plan.width), jnp.float32)]
        + [pltpu.SemaphoreType.DMA],
        1 << 33,
        1 << 23,
    )(*heads, *tails, *parts, *tables)


def order_of(plan, offset):
    return jnp.where(offset == 0, 0, plan.row_devices - offset)


def run_estimates(plan, pieces, pair_one, pair_two, owner):
    vmem = pl.BlockSpec(memory_space=pltpu.VMEM)
    smem = pl.BlockSpec(memory_space=pltpu.SMEM)
    axes = ("sims", "rows")
    places = [(sim, row) for sim in range(plan.sim_devices) for row in range(plan.row_devices)]

    def f32(*shape):
        return jax.ShapeDtypeStruct(shape, jnp.float32)

    def hop(value, target):
        count = plan.row_devices
        pairs = [(sim * count + row, target(sim, row)[0] * count + target(sim, row)[1]) for sim, row in places]
        return lax.ppermute(value, axes, pairs)

    moved = jnp.stack(exchange_all(plan, pieces))
    here = (lax.axis_index("sims") // 2) ^ lax.axis_index("rows")
    near = []
    for step in plan.hops:
        value = lax.dynamic_index_in_dim(moved, order_of(plan, here ^ step), keepdims=False)
        near.append(exchange(value, "sims", 2 * step) if step else value)
    far = [exchange(value, "sims", 1) for value in near]
    scratch = [
        pltpu.VMEM((plan.sim_devices, plan.row_local + 2 * rim, plan.share + lane), jnp.float32),
        pltpu.VMEM((lane, lane), jnp.float32),
    ]
    found = call(
        functools.partial(estimate_kernel, plan),
        [f32(plan.row_local, plan.share)] * plan.chips,
        [smem] * 2 + [vmem] * (2 * plan.chips),
        scratch,
        1 << 24,
        1 << 23,
    )(pair_one, pair_two, *near, *far)
    field_width = plan.columns // plan.sim_devices
    kept = field_width if field_width % lane == 0 else plan.share
    [mean_field] = call(
        functools.partial(mean_kernel, plan, kept),
        [f32(OWNERS, plan.row_local, kept)],
        [smem] * 3 + [vmem] * (3 * plan.chips),
        scratch + [pltpu.VMEM((OWNERS, plan.row_local, plan.share), jnp.float32)],
        1 << 24,
        1 << 23,
    )(pair_one, pair_two, owner, *near, *far, *found)
    if kept != field_width:
        start = (lax.axis_index("sims") % 2) * field_width
        mean_field = lax.dynamic_slice_in_dim(mean_field, start, field_width, axis=2)
    moved = [exchange(value, "sims", 2 * step) if step else value for step, value in zip(plan.hops, found)]
    [estimate] = call(
        functools.partial(join_kernel, plan),
        [f32(plan.row_local, plan.columns)],
        [vmem] * plan.chips,
        [pltpu.SemaphoreType.DMA((plan.chips,))],
        0,
        1 << 20,
        outs_in=pltpu.HBM,
    )(*moved)
    return estimate, mean_field


def body(maps, weight, beam, pair_one, pair_two, owner):
    sim_local, row_local, columns = maps.shape
    taps = beam.shape[0]
    row_devices, sim_devices = lax.axis_size("rows"), lax.axis_size("sims")
    plan = Plan(row_devices, sim_devices, row_local, columns, taps)
    vmem = pl.BlockSpec(memory_space=pltpu.VMEM)
    smem = pl.BlockSpec(memory_space=pltpu.SMEM)
    far = pl.BlockSpec(memory_space=pltpu.HBM)

    def pinned(value):
        return pltpu.with_memory_space_constraint(value, pltpu.HBM)

    def f32(*shape):
        return jax.ShapeDtypeStruct(shape, jnp.float32)

    def b16(*shape):
        return jax.ShapeDtypeStruct(shape, jnp.bfloat16)

    cells = row_local * columns
    inputs = pinned(maps.reshape(row_local, columns)), pinned(weight)
    padded = columns + 2 * plan.halo
    heads = call(
        functools.partial(head_kernel, plan),
        [f32(plan.share_rows + plan.head, plan.width)] * row_devices,
        [far, far],
        [pltpu.VMEM((rows, padded), jnp.float32) for rows in (plan.share_rows, plan.head)]
        + [pltpu.VMEM((plan.head, columns), jnp.float32), pltpu.SemaphoreType.DMA((3,))],
        cells // 8,
        2 * cells,
    )(*inputs)
    rest = row_local - plan.head
    tails = call(
        functools.partial(tail_kernel, plan),
        [f32(rest, plan.width)] * row_devices,
        [far, far],
        [pltpu.VMEM((rest, padded), jnp.float32), pltpu.VMEM((rest, columns), jnp.float32)]
        + [pltpu.SemaphoreType.DMA((2, loads))],
        cells,
        16 * cells,
    )(*inputs)
    heads = exchange_all(plan, heads)
    tails, heads[1], heads[2] = lax.optimization_barrier((tails, heads[1], heads[2]))
    tails = exchange_all(plan, tails)
    parts = lax.optimization_barrier(jnp.stack([head[: plan.share_rows] for head in heads])[None])
    shapes = [(plan.rows, plan.rows), (row_devices * plan.slab, plan.rows)]
    for block in plan.blocks + plan.out_blocks[:1]:
        low, high = plan.window(block)
        shapes.append((high - low, block[1] - block[0]))
    shapes.append((2 * wide, lane))


    def prepare(parts, beam):
        tables = call(
            functools.partial(table_kernel, plan),
            [b16(*shape) for shape in shapes for _ in range(2)],
            [far],
            [pltpu.VMEM((1, taps), jnp.float32), pltpu.VMEM((8, lane), jnp.float32), pltpu.SemaphoreType.DMA],
            1 << 32,
            1 << 23,
        )(pinned(beam))
        found = {0: parts}
        for bit in [1 << i for i in range(1, plan.sharers.bit_length() - 1)]:
            found |= {offset | bit: exchange(value, "sims", bit) for offset, value in found.items()}
        sharers[:] = [[offset] for offset in found] + [[offset ^ 1 for offset in found]]
        whole, tables = lax.optimization_barrier((jnp.concatenate(list(found.values())), tables))
        return [*found.values(), exchange(whole, "sims", 1)], tables

    sharers = []
    made = jax.eval_shape(prepare, parts, beam[None])
    parts, tables = lax.cond(
        lax.axis_index("rows") < row_devices,
        prepare,
        lambda parts, beam: jax.tree.map(lambda x: jnp.zeros(x.shape, x.dtype), made),
        parts,
        beam[None],
    )
    filtered = run_filter(plan, sharers, heads, tails, parts, tables)
    estimate, mean_field = run_estimates(plan, filtered, pair_one, pair_two, owner)
    return estimate.reshape(maps.shape), mean_field


def solution(mesh):
    in_specs = (P("sims", "rows", None), P("rows", None), P(), P(), P(), P())
    out_specs = (P("sims", "rows", None), P(None, "rows", "sims"))
    return jax.shard_map(body, mesh=mesh, in_specs=in_specs, out_specs=out_specs, check_vma=False)
```

```python
import functools

import jax
import jax.numpy as jnp
from jax import lax
from jax.experimental import pallas as pl
from jax.experimental.pallas import tpu as pltpu
from jax.sharding import PartitionSpec as P

ITERS = 3
OWNERS = 8

ridge_term = 0.5
step_size = 0.6
exact = lax.Precision.HIGHEST
lane = 128
wide = 256
stretch = 1024
rim = 2
loads = 7
vmem_bytes = 48 * 1024 * 1024


def split(value):
    high = value.astype(jnp.bfloat16)
    low = (value - high.astype(jnp.float32)).astype(jnp.bfloat16)
    return high, low


def dot(a, b):
    return jnp.dot(a, b, preferred_element_type=jnp.float32)


class Plan:
    def __init__(self, row_devices, sim_devices, row_local, columns, taps):
        self.row_devices, self.sim_devices = row_devices, sim_devices
        self.row_local, self.columns = row_local, columns
        self.rows = row_devices * row_local
        self.steps = [0, *range(row_devices - 1, 0, -1)]
        self.margin = (taps - 1) // 2
        self.share = columns // row_devices
        self.halo = -(-self.margin * (2 * ITERS + 1) // lane) * lane
        self.width = self.share + 2 * self.halo
        self.slab = row_local + 4 * rim
        self.chips = sim_devices // 2
        self.hops = [0, *sorted(range(1, self.chips), key=lambda offset: -offset.bit_count())]
        self.sharers = min(sim_devices, row_local // 8)
        self.share_rows = row_local // self.sharers
        self.head = row_local // 8
        self.length = max(2 * wide, -(-self.rows // lane) * lane)
        inner = range(lane, self.width - lane, wide)
        blocks = [(0, lane)] + [(a, min(a + wide, self.width - lane)) for a in inner]
        self.blocks = blocks + [(self.width - lane, self.width)]
        centre = range(self.halo, self.halo + self.share, wide)
        self.out_blocks = [(a, min(a + wide, self.halo + self.share)) for a in centre]

    def sides(self):
        left = (self.halo - rim - self.margin) // lane * lane
        return left, (self.halo + self.share - self.margin) // lane * lane

    def window(self, block):
        return max(0, block[0] - lane), min(self.width, block[1] + lane)

    def stage_blocks(self, iteration):
        low = self.halo - self.margin * (2 * (ITERS - 1 - iteration) + 1)
        return [i for i, (a, b) in enumerate(self.blocks) if b > low and a < self.width - low]


def spread_out(plan, padded, outs, first, rows):
    for step, out in zip(plan.steps, outs):
        column = pl.multiple_of((lax.axis_index("rows") ^ step) * plan.share, lane)
        out[first : first + rows.size] = padded[rows, pl.ds(column, plan.width)]


def clear_sides(plan, padded):
    zeros = jnp.zeros((padded.shape[0], plan.halo), jnp.float32)
    padded[:, : plan.halo] = zeros
    padded[:, plan.halo + plan.columns :] = zeros


def head_kernel(plan, maps, weight, *refs):
    heads = refs[: plan.row_devices]
    share, padded, given, sems = refs[plan.row_devices :]
    row = pl.multiple_of(lax.rem(lax.axis_index("sims"), plan.sharers) * plan.share_rows, plan.share_rows)
    inner = slice(plan.halo, plan.halo + plan.columns)
    copies = [
        pltpu.make_async_copy(weight.at[pl.ds(row, plan.share_rows)], share.at[:, inner], sems.at[0]),
        pltpu.make_async_copy(weight.at[: plan.head], padded.at[:, inner], sems.at[1]),
        pltpu.make_async_copy(maps.at[: plan.head], given, sems.at[2]),
    ]
    for copy in copies:
        copy.start()
    clear_sides(plan, share)
    clear_sides(plan, padded)
    for copy in copies:
        copy.wait()
    padded[:, inner] = padded[:, inner] * given[...]
    spread_out(plan, share, heads, 0, pl.ds(0, plan.share_rows))
    spread_out(plan, padded, heads, plan.share_rows, pl.ds(0, plan.head))


def tail_kernel(plan, maps, weight, *refs):
    tails = refs[: plan.row_devices]
    padded, given, sems = refs[plan.row_devices :]
    inner = slice(plan.halo, plan.halo + plan.columns)
    chunk = (plan.row_local - plan.head) // loads
    copies = []
    for number in range(loads):
        rows, source = pl.ds(number * chunk, chunk), pl.ds(plan.head + number * chunk, chunk)
        copies.append((
            pltpu.make_async_copy(weight.at[source], padded.at[rows, inner], sems.at[0, number]),
            pltpu.make_async_copy(maps.at[source], given.at[rows], sems.at[1, number]),
        ))
        for copy in copies[-1]:
            copy.start()
    clear_sides(plan, padded)
    for number in range(loads):
        for copy in copies[number]:
            copy.wait()
        rows = pl.ds(number * chunk, chunk)
        padded[rows, inner] = padded[rows, inner] * given[rows]
        spread_out(plan, padded, tails, number * chunk, rows)


def band(plan, taps, rows, columns, offset):
    if offset % plan.length:
        taps = pltpu.roll(taps, offset % plan.length, 1)
    spread = jnp.broadcast_to(taps[:1], (rows, plan.length))
    rolled = pltpu.roll(spread, 0, 1, stride=1, stride_axis=0)[:, :columns]
    row = lax.broadcasted_iota(jnp.int32, (rows, columns), 0)
    column = lax.broadcasted_iota(jnp.int32, (rows, columns), 1)
    return jnp.where(jnp.abs(column - row - offset) <= plan.margin, rolled, 0.0)


def table_kernel(plan, beam, *refs):
    refs, given, line, sem = refs[:-3], *refs[-3:]
    count = beam.shape[1]
    copy = pltpu.make_async_copy(beam, given, sem)
    copy.start()
    line[...] = jnp.zeros(line.shape, jnp.float32)
    copy.wait()
    line[:1, :count] = given[...]
    kernel = line[...]
    kernel = kernel / jnp.sum(kernel[:1], axis=1, keepdims=True)
    size = kernel.shape[1]
    row = lax.broadcasted_iota(jnp.int32, (size, size), 0)
    column = lax.broadcasted_iota(jnp.int32, (size, size), 1)
    mirror = (row + column == count - 1).astype(jnp.float32)
    blank = jnp.zeros((kernel.shape[0], plan.length - size), jnp.float32)

    def centred(values):
        return pltpu.roll(jnp.concatenate([values, blank], axis=1), plan.length - plan.margin, 1)

    taps, reverse = centred(kernel), centred(jnp.dot(kernel, mirror, precision=exact))
    tables = list(refs)

    def put(value):
        high, low = split(value)
        tables.pop(0)[...] = high
        tables.pop(0)[...] = low

    rows = plan.rows
    put(jnp.dot(band(plan, taps, rows, rows, 0), band(plan, reverse, rows, rows, 0), precision=exact))
    slabs = []
    for device in range(plan.row_devices):
        first = device * plan.row_local - rim
        part = band(plan, reverse, plan.slab, rows, first)
        row = lax.broadcasted_iota(jnp.int32, part.shape, 0)
        inside = (row + first >= 0) & (row + first < rows) & (row < plan.row_local + 2 * rim)
        slabs.append(jnp.where(inside, part, 0.0))
    put(jnp.concatenate(slabs, axis=0))
    size = 2 * wide
    forward = band(plan, taps, size, size, 0)
    backward = band(plan, reverse, size, size, 0)[:, lane : lane + wide]
    square = step_size * jnp.dot(forward, backward, precision=exact)
    for block in plan.blocks:
        low, high = plan.window(block)
        first = low - block[0] + lane
        wanted = square[first : first + high - low, : block[1] - block[0]]
        high_term, low_term = tables[0], tables[1]
        put(wanted)
        origin = lax.axis_index("rows") * plan.share - plan.halo + low
        reach = origin + high - low
        cut = ((origin < 0) & (reach > 0)) | ((origin < plan.columns) & (reach > plan.columns))

        @pl.when(cut)
        def _(origin=origin, extent=high - low, first=first, span=block[1] - block[0], terms=(high_term, low_term)):
            column = lax.broadcasted_iota(jnp.int32, (size, size), 1) + (origin - first)
            inside = (column >= 0) & (column < plan.columns)
            value = step_size * jnp.dot(jnp.where(inside, forward, 0.0), backward, precision=exact)
            high_part, low_part = split(value[first : first + extent, :span])
            terms[0][...] = high_part
            terms[1][...] = low_part

    for block in plan.out_blocks[:1]:
        low, high = plan.window(block)
        put(step_size * forward[: high - low, block[0] - low : block[1] - low])
    left, right = plan.sides()
    column = lax.broadcasted_iota(jnp.int32, (wide, lane), 1)
    before = band(plan, taps, wide, lane, left - (plan.halo - lane))
    behind = band(plan, taps, wide, lane, right - (plan.halo + plan.share))
    rows_at = lax.axis_index("rows")
    before = jnp.where((column >= lane - rim) & (rows_at > 0), before, 0.0)
    behind = jnp.where((column < rim) & (rows_at < plan.row_devices - 1), behind, 0.0)
    put(step_size * jnp.concatenate([before, behind], axis=0))


def filter_kernel(plan, sharers, *refs):
    refs = list(refs)

    def take(number):
        taken = refs[:number]
        del refs[:number]
        return taken

    heads, tails = take(plan.row_devices), take(plan.row_devices)
    parts = take(len(sharers))
    square, final = take(2), take(2)
    bands = [take(2) for _ in plan.blocks]
    last, edges = take(2), take(2)
    outs = take(plan.row_devices)
    seen, weight, image, base, total, field, side, high, low, mid_high, mid_low, shares, sem = refs
    first = 0
    for part in parts:
        pltpu.make_async_copy(part, shares.at[pl.ds(first, part.shape[0])], sem).start()
        first += part.shape[0]
    for index, step in enumerate(plan.steps):
        row = pl.multiple_of((lax.axis_index("rows") ^ step) * plan.row_local, plan.row_local)
        rows = pl.ds(row, plan.row_local)
        value = jnp.concatenate([heads[index][plan.share_rows :], tails[index][...]], axis=0)
        seen[rows, :] = value
        high[rows, :], low[rows, :] = split(value)

    def rows_pass(table, start, stop, full=True):
        count = table[0].shape[0]
        for a in range(start, stop, wide):
            b = min(a + wide, stop)
            value = dot(table[0][...], high[:, a:b]) + dot(table[1][...], high[:, a:b])
            if full:
                value = value + dot(table[0][...], low[:, a:b])
                mid_high[:count, a:b], mid_low[:count, a:b] = split(value)
            else:
                mid_high[:count, a:b] = value.astype(jnp.bfloat16)

    def columns_pass(table, count, window, full=True):
        a, b = window
        value = dot(mid_high[:count, a:b], table[0][...]) + dot(mid_high[:count, a:b], table[1][...])
        return value + dot(mid_low[:count, a:b], table[0][...]) if full else value

    keep = 1.0 - step_size * ridge_term
    for iteration in range(ITERS):
        chosen = plan.stage_blocks(iteration)
        windows = [plan.window(plan.blocks[i]) for i in chosen]
        trim = lane if iteration == ITERS - 1 and plan.halo - rim - 3 * plan.margin >= lane else 0
        rows_pass(square, max(windows[0][0], trim), min(windows[-1][1], plan.width - trim), iteration == 0)
        if iteration == 0:
            for i, window in zip(chosen, windows):
                base[:, slice(*plan.blocks[i])] = columns_pass(bands[i], plan.rows, window)
            pltpu.make_async_copy(shares, shares, sem).wait()
            for slot, offset in enumerate(offset for owners in sharers for offset in owners):
                for index, step in enumerate(plan.steps):
                    row = (lax.axis_index("rows") ^ step) * plan.row_local
                    row = row + (lax.rem(lax.axis_index("sims"), plan.sharers) ^ offset) * plan.share_rows
                    weight[pl.ds(pl.multiple_of(row, plan.share_rows), plan.share_rows), :] = shares[slot, index]
        for i, window in zip(chosen, windows):
            a, b = plan.blocks[i]
            value = base[:, a:b]
            if iteration > 0:
                before = image if iteration > 1 else base
                value = keep * before[:, a:b] + value - columns_pass(bands[i], plan.rows, window, False)
            if 0 < iteration < ITERS - 1:
                image[:, a:b] = value
            product = weight[:, a:b] * value
            given = seen[:, a:b]
            total[:, a:b] = given - product + keep * (total[:, a:b] if iteration > 0 else given)
            high[:, a:b] = product.astype(jnp.bfloat16)
    first, stop = plan.window(plan.out_blocks[0])[0], plan.window(plan.out_blocks[-1])[1]
    high[:, first:stop], low[:, first:stop] = split(total[:, first:stop])
    rows_pass(final, first, stop)
    count = plan.row_devices * plan.slab
    for block in plan.out_blocks:
        size = block[1] - block[0]
        field[:, block[0] - plan.halo : block[1] - plan.halo] = columns_pass(last, count, plan.window(block))
    value = jnp.zeros((count, lane), jnp.float32)
    for number, start in enumerate(plan.sides()):
        part = slice(number * wide, (number + 1) * wide)
        a, b = mid_high[:count, start : start + wide], mid_low[:count, start : start + wide]
        value = value + dot(a, edges[0][part]) + dot(a, edges[1][part]) + dot(b, edges[0][part])
    side[:count] = value
    turned = side[...].T
    turned = jnp.concatenate([turned[lane - rim :], turned[:rim]], axis=0)
    for device in range(plan.row_devices):
        shift = (side.shape[0] - device * plan.slab - rim) % side.shape[0]
        row = (device + 1) * plan.slab - 2 * rim
        field[row : row + 2 * rim, :lane] = pltpu.roll(turned, shift, 1)[:, :lane]
    for step, out in zip(plan.steps, outs):
        row = pl.multiple_of((lax.axis_index("rows") ^ step) * plan.slab, 8)
        out[...] = field[pl.ds(row, plan.slab), :]


def divergence(own, partner):
    rows, columns = own.shape
    stop, inner = rows - rim, slice(0, columns - lane)
    here = partner[rim:stop]
    down, up = partner[2 * rim :, inner], partner[: stop - rim, inner]
    middle = here[:, inner]
    flow = own[rim + 1 : stop + 1, inner] * (down - middle) - own[rim - 1 : stop - 1, inner] * (middle - up)
    level = own[rim:stop]

    def shifted(value, amount):
        return pltpu.roll(value, amount % columns, 1)[:, inner]

    right = shifted(level, -1) * (shifted(here, -2) - middle)
    left = shifted(level, 1) * (middle - shifted(here, 2))
    return 0.25 * (flow + (right - left))


def collect(plan, near, far, every, corner):
    core = lax.axis_index("sims") % 2
    here = lax.axis_index("sims") // 2
    corner[...] = jnp.zeros(corner.shape, jnp.float32)
    kept = plan.row_local + 2 * rim
    for index, step in enumerate(plan.hops):
        for source, parity in ((near[index], core), (far[index], 1 - core)):
            at = 2 * (here ^ step) + parity
            every[at, :, : plan.share] = source[:kept]
            corner[lane - rim :] = source[kept : kept + rim, :lane]
            corner[:rim] = source[kept + rim : kept + 2 * rim, :lane]
            every[at, rim : kept - rim, plan.share :] = corner[...].T[: plan.row_local]


def mixed(every, pair_one, pair_two, sim):
    return divergence(every[sim], 2.0 * every[pair_one[sim]] - every[pair_two[sim]])


def estimate_kernel(plan, pair_one, pair_two, *refs):
    near, far, outs = refs[: plan.chips], refs[plan.chips : 2 * plan.chips], refs[2 * plan.chips : -2]
    every, corner = refs[-2:]
    collect(plan, near, far, every, corner)
    chip, core = lax.axis_index("sims") // 2, lax.axis_index("sims") % 2
    for step, out in zip(plan.hops, outs):
        out[...] = mixed(every, pair_one, pair_two, 2 * (chip ^ step) + core)


def mean_kernel(plan, field_width, pair_one, pair_two, owner, *refs):
    near, far, done = [refs[first * plan.chips : (first + 1) * plan.chips] for first in range(3)]
    mean_field, every, corner, whole = refs[3 * plan.chips :]
    collect(plan, near, far, every, corner)
    chip, core = lax.axis_index("sims") // 2, lax.axis_index("sims") % 2
    whole[...] = jnp.zeros(whole.shape, jnp.float32)
    for step, estimate in zip(plan.hops, done):
        sim = 2 * (chip ^ step)
        whole[owner[sim + core]] += estimate[...]
        whole[owner[sim + 1 - core]] += mixed(every, pair_one, pair_two, sim + 1 - core)
    span = pl.ds(pl.multiple_of(core * field_width, lane), field_width) if field_width < plan.share else slice(None)
    for group in range(OWNERS):
        count = jnp.int32(0)
        for sim in range(plan.sim_devices):
            count = count + (owner[sim] == group).astype(jnp.int32)
        mean_field[group] = whole[group, :, span] / jnp.maximum(count, 1).astype(jnp.float32)


def join_kernel(plan, *refs):
    pieces, estimate, sems = refs[: plan.chips], refs[plan.chips], refs[plan.chips + 1]
    copies = []
    for step, piece in zip(plan.hops, pieces):
        column = pl.multiple_of(((lax.axis_index("sims") // 2) ^ step) * plan.share, lane)
        copies.append(pltpu.make_async_copy(piece, estimate.at[:, pl.ds(column, plan.share)], sems.at[step]))
        copies[-1].start()
    for copy in copies:
        copy.wait()


def exchange(value, axis, offset):
    count = lax.axis_size(axis)
    return lax.ppermute(value, axis, [(i, i ^ offset) for i in range(count)])


def exchange_all(plan, values):
    return [exchange(value, "rows", step) if step else value for step, value in zip(plan.steps, values)]


def call(kernel, out_shapes, in_specs, scratch, flops, moved, outs_in=pltpu.VMEM):
    return pl.pallas_call(
        kernel,
        out_shape=out_shapes,
        in_specs=in_specs,
        out_specs=[pl.BlockSpec(memory_space=outs_in)] * len(out_shapes),
        scratch_shapes=scratch,
        compiler_params=pltpu.CompilerParams(vmem_limit_bytes=vmem_bytes),
        cost_estimate=pl.CostEstimate(flops=flops, bytes_accessed=moved, transcendentals=0),
    )


def run_filter(plan, sharers, heads, tails, parts, tables):
    vmem = pl.BlockSpec(memory_space=pltpu.VMEM)
    far = pl.BlockSpec(memory_space=pltpu.HBM)
    full = (plan.rows, plan.width)
    tall = (max(plan.rows, plan.row_devices * plan.slab), plan.width)
    return call(
        functools.partial(filter_kernel, plan, sharers),
        [jax.ShapeDtypeStruct((plan.slab, plan.share), jnp.float32)] * plan.row_devices,
        [vmem] * (2 * plan.row_devices) + [far] * len(parts) + [vmem] * len(tables),
        [pltpu.VMEM(full, jnp.float32)] * 5
        + [pltpu.VMEM((plan.row_devices * plan.slab, plan.share), jnp.float32)]
        + [pltpu.VMEM((-(-plan.row_devices * plan.slab // lane) * lane, lane), jnp.float32)]
        + [pltpu.VMEM(full, jnp.bfloat16)] * 2
        + [pltpu.VMEM(tall, jnp.bfloat16)] * 2
        + [pltpu.VMEM((plan.sharers, plan.row_devices, plan.share_rows, plan.width), jnp.float32)]
        + [pltpu.SemaphoreType.DMA],
        1 << 33,
        1 << 23,
    )(*heads, *tails, *parts, *tables)


def order_of(plan, offset):
    return jnp.where(offset == 0, 0, plan.row_devices - offset)


def run_estimates(plan, pieces, pair_one, pair_two, owner):
    vmem = pl.BlockSpec(memory_space=pltpu.VMEM)
    smem = pl.BlockSpec(memory_space=pltpu.SMEM)
    axes = ("sims", "rows")
    places = [(sim, row) for sim in range(plan.sim_devices) for row in range(plan.row_devices)]

    def f32(*shape):
        return jax.ShapeDtypeStruct(shape, jnp.float32)

    def hop(value, target):
        count = plan.row_devices
        pairs = [(sim * count + row, target(sim, row)[0] * count + target(sim, row)[1]) for sim, row in places]
        return lax.ppermute(value, axes, pairs)

    moved = jnp.stack(exchange_all(plan, pieces))
    here = (lax.axis_index("sims") // 2) ^ lax.axis_index("rows")
    near = []
    for step in plan.hops:
        value = lax.dynamic_index_in_dim(moved, order_of(plan, here ^ step), keepdims=False)
        near.append(exchange(value, "sims", 2 * step) if step else value)
    far = [exchange(value, "sims", 1) for value in near]
    scratch = [
        pltpu.VMEM((plan.sim_devices, plan.row_local + 2 * rim, plan.share + lane), jnp.float32),
        pltpu.VMEM((lane, lane), jnp.float32),
    ]
    found = call(
        functools.partial(estimate_kernel, plan),
        [f32(plan.row_local, plan.share)] * plan.chips,
        [smem] * 2 + [vmem] * (2 * plan.chips),
        scratch,
        1 << 24,
        1 << 23,
    )(pair_one, pair_two, *near, *far)
    field_width = plan.columns // plan.sim_devices
    kept = field_width if field_width % lane == 0 else plan.share
    [mean_field] = call(
        functools.partial(mean_kernel, plan, kept),
        [f32(OWNERS, plan.row_local, kept)],
        [smem] * 3 + [vmem] * (3 * plan.chips),
        scratch + [pltpu.VMEM((OWNERS, plan.row_local, plan.share), jnp.float32)],
        1 << 24,
        1 << 23,
    )(pair_one, pair_two, owner, *near, *far, *found)
    if kept != field_width:
        start = (lax.axis_index("sims") % 2) * field_width
        mean_field = lax.dynamic_slice_in_dim(mean_field, start, field_width, axis=2)
    moved = [exchange(value, "sims", 2 * step) if step else value for step, value in zip(plan.hops, found)]
    [estimate] = call(
        functools.partial(join_kernel, plan),
        [f32(plan.row_local, plan.columns)],
        [vmem] * plan.chips,
        [pltpu.SemaphoreType.DMA((plan.chips,))],
        0,
        1 << 20,
        outs_in=pltpu.HBM,
    )(*moved)
    return estimate, mean_field


def body(maps, weight, beam, pair_one, pair_two, owner):
    sim_local, row_local, columns = maps.shape
    taps = beam.shape[0]
    row_devices, sim_devices = lax.axis_size("rows"), lax.axis_size("sims")
    plan = Plan(row_devices, sim_devices, row_local, columns, taps)
    vmem = pl.BlockSpec(memory_space=pltpu.VMEM)
    smem = pl.BlockSpec(memory_space=pltpu.SMEM)
    far = pl.BlockSpec(memory_space=pltpu.HBM)

    def pinned(value):
        return pltpu.with_memory_space_constraint(value, pltpu.HBM)

    def f32(*shape):
        return jax.ShapeDtypeStruct(shape, jnp.float32)

    def b16(*shape):
        return jax.ShapeDtypeStruct(shape, jnp.bfloat16)

    cells = row_local * columns
    inputs = pinned(maps.reshape(row_local, columns)), pinned(weight)
    padded = columns + 2 * plan.halo
    heads = call(
        functools.partial(head_kernel, plan),
        [f32(plan.share_rows + plan.head, plan.width)] * row_devices,
        [far, far],
        [pltpu.VMEM((rows, padded), jnp.float32) for rows in (plan.share_rows, plan.head)]
        + [pltpu.VMEM((plan.head, columns), jnp.float32), pltpu.SemaphoreType.DMA((3,))],
        cells // 8,
        2 * cells,
    )(*inputs)
    rest = row_local - plan.head
    tails = call(
        functools.partial(tail_kernel, plan),
        [f32(rest, plan.width)] * row_devices,
        [far, far],
        [pltpu.VMEM((rest, padded), jnp.float32), pltpu.VMEM((rest, columns), jnp.float32)]
        + [pltpu.SemaphoreType.DMA((2, loads))],
        cells,
        16 * cells,
    )(*inputs)
    heads = exchange_all(plan, heads)
    tails, heads[1], heads[2] = lax.optimization_barrier((tails, heads[1], heads[2]))
    tails = exchange_all(plan, tails)
    parts = lax.optimization_barrier(jnp.stack([head[: plan.share_rows] for head in heads])[None])
    shapes = [(plan.rows, plan.rows), (row_devices * plan.slab, plan.rows)]
    for block in plan.blocks + plan.out_blocks[:1]:
        low, high = plan.window(block)
        shapes.append((high - low, block[1] - block[0]))
    shapes.append((2 * wide, lane))


    def prepare(parts, beam):
        tables = call(
            functools.partial(table_kernel, plan),
            [b16(*shape) for shape in shapes for _ in range(2)],
            [far],
            [pltpu.VMEM((1, taps), jnp.float32), pltpu.VMEM((8, lane), jnp.float32), pltpu.SemaphoreType.DMA],
            1 << 32,
            1 << 23,
        )(pinned(beam))
        found = {0: parts}
        for bit in [1 << i for i in range(1, plan.sharers.bit_length() - 1)]:
            found |= {offset | bit: exchange(value, "sims", bit) for offset, value in found.items()}
        sharers[:] = [[offset] for offset in found] + [[offset ^ 1 for offset in found]]
        whole, tables = lax.optimization_barrier((jnp.concatenate(list(found.values())), tables))
        return [*found.values(), exchange(whole, "sims", 1)], tables

    sharers = []
    made = jax.eval_shape(prepare, parts, beam[None])
    parts, tables = lax.cond(
        lax.axis_index("rows") < row_devices,
        prepare,
        lambda parts, beam: jax.tree.map(lambda x: jnp.zeros(x.shape, x.dtype), made),
        parts,
        beam[None],
    )
    filtered = run_filter(plan, sharers, heads, tails, parts, tables)
    estimate, mean_field = run_estimates(plan, filtered, pair_one, pair_two, owner)
    return estimate.reshape(maps.shape), mean_field


def solution(mesh):
    in_specs = (P("sims", "rows", None), P("rows", None), P(), P(), P(), P())
    out_specs = (P("sims", "rows", None), P(None, "rows", "sims"))
    return jax.shard_map(body, mesh=mesh, in_specs=in_specs, out_specs=out_specs, check_vma=False)
```
